32 devices in a mesh: dp: 16 (over z, x, core), mp: 2 (over y).
Axes of the slice: x: 2, y: 2, z: 4, core: 2. Of those that a mesh axis runs over, the one named last changes fastest.
Arguments:
- master: float32 [2, 256, 512], P('mp', 'dp'), may hold values from -4 to 4
- moment: float32 [2, 256, 512], P('mp', 'dp'), may hold values from -0.06 to 0.06
- variance: float32 [2, 256, 512], P('mp', 'dp'), may hold values from 3e-06 to 3e-05
- flat_slot: int32 [256], replicated, may hold values from 0 to 255, each once
- feedback: bfloat16 [16, 2, 16, 8192], P('dp', None, 'mp'), may hold values from -0.029907227 to 0.029907227
- activations: bfloat16 [2, 2048, 8192], P(None, ('dp', 'mp')), may hold values from -6 to 6
- output_grads: bfloat16 [2, 2048, 8192], P(None, ('dp', 'mp')), may hold values from -6 to 6
Outputs:
- master_out: float32 [2, 256, 512], P('mp', 'dp')
- moment_out: float32 [2, 256, 512], P('mp', 'dp')
- feedback_out: bfloat16 [16, 2, 16, 8192], P('dp', None, 'mp')
The draws below stay inside these ranges and needn't reach their ends.
Inputs may be any that keep to these rules, and one draw needn't show every extreme that they name: `flat_slot`: every position of the flat buffer holds exactly one of the 256 segments.
All inputs are finite; a program needn't handle non-finite values. Where the reference program divides by a largest or mean magnitude, that divisor is 1e-20 or more.
Results may differ from the reference program's by a relative error of at most 0.0036.
The reference program's roundings to bfloat16 on the way (of `working` and `local_weights`) count: a program that leaves them out, or rounds other values in their place, can miss the bound.
Values may be sent and summed in bfloat16 or wider, within the bound.
No kernel may reach another device: no remote copies, remote signals or barrier semaphores. Data moves between devices by JAX's collectives and lax.ppermute only.
A program may use at most 64 MiB of HBM per device.

```python
import math
import jax
import jax.numpy as jnp
from jax import lax

D = 8192
HID_DEV = 8
TOK = 128
SEG = 512
HID = 16
TOKENS = 2048
NSEG = 256
N_DP = 16
N_MP = 2


def spiked(array, stream_key, source, target, blocks, factor):
    owner, partner = [(jnp.arange(array.shape[position]) // (array.shape[position] // blocks)).reshape([-1 if axis == position else 1 for axis in range(array.ndim)]) for position in (source, target)]
    chosen = jax.random.permutation(stream_key, blocks)[partner]
    strong = (owner == chosen) | (owner == (partner + blocks // 2) % blocks)
    return jnp.where(strong, factor * array, array)


def block_levels(own_key, shape, cuts, smallest, largest):
    gain = 1.0
    for dim, shards_of in cuts:
        heights = jax.random.uniform(jax.random.fold_in(jax.random.fold_in(own_key, 6), dim), (shards_of,), jnp.float32, smallest / len(cuts), largest / len(cuts))
        gain = gain * jnp.repeat(jnp.exp(heights), shape[dim] // shards_of).reshape((-1,) + (1,) * (len(shape) - 1 - dim))
    return gain


def bell_draw(rng, dims, deviation, most, cuts=(), dtype=jnp.bfloat16):
    drawn = jax.random.normal(rng, dims, jnp.float32) * deviation
    if len(cuts) > 0:
        drawn = block_levels(rng, dims, cuts, -0.22, 0.18) * drawn
    return jnp.clip(drawn, min=-most, max=most).astype(dtype)


def bell_draw_with(own_key, shape, width, limit, cuts, heavy, dtype=jnp.bfloat16):
    entries = width * jax.random.normal(own_key, shape, jnp.float32)
    if cuts:
        entries = entries * block_levels(own_key, shape, cuts, -0.22, 0.18)
    return jnp.clip(spiked(entries, jax.random.fold_in(own_key, 3), *heavy), -limit, limit).astype(dtype)


def setup_inputs(seed: int = 0) -> dict:
    arg_keys = jax.random.split(jax.random.key(seed), 8)
    return {
        "master": bell_draw(arg_keys[0], (N_MP, NSEG, SEG), 1.0, 4.0, ((0, 2), (1, 16)), jnp.float32),
        "moment": bell_draw(arg_keys[1], (N_MP, NSEG, SEG), 0.01, 0.06, ((0, 2), (1, 16)), jnp.float32),
        "variance": jnp.clip(jnp.exp(math.log(2.9999999242136255e-05) - 2.30258503 * jax.random.uniform(arg_keys[2], (N_MP, NSEG, SEG), jnp.float32) ** block_levels(arg_keys[2], (N_MP, NSEG, SEG), ((0, 2), (1, 16)), -0.2, 0.2)), 3.000000106112566e-06, 2.9999999242136255e-05),
        "flat_slot": jax.random.permutation(arg_keys[3], NSEG).astype(jnp.int32),
        "feedback": bell_draw(arg_keys[4], (N_DP, 2, HID, D), 0.005, 0.029907227, ((0, 16), (2, 2))),
        "activations": bell_draw_with(arg_keys[5], (2, TOKENS, D), 1.0, 6.0, ((1, 32),), (1, 2, 32, 2.75)),
        "output_grads": bell_draw_with(arg_keys[6], (2, TOKENS, D), 1.0, 6.0, ((1, 32),), (1, 2, 32, 2.75)),
    }


beta_one = 0.9
step_rate = 0.05
epsilon = 1e-08
down_scale = 28672.0 ** (-0.5)

def tensor_order(flat, flat_slot):
    pieces = flat[:, flat_slot, :].reshape(N_MP, 2, HID_DEV, D)
    return jnp.transpose(pieces, (1, 0, 2, 3)).reshape(2, HID, D)

def flat_order(tensor, flat_slot):
    pieces = jnp.transpose(tensor.reshape(2, N_MP, HID_DEV, D), (1, 0, 2, 3)).reshape(N_MP, NSEG, SEG)
    return jnp.zeros_like(pieces).at[:, flat_slot, :].set(pieces)

def silu_slope(preact):
    sigmoid_value = jax.nn.sigmoid(preact)
    return sigmoid_value * (1.0 + preact * (1.0 - sigmoid_value))

def gradients(weights, inputs, cotangent):
    up_scale = D ** (-0.5)
    before = up_scale * jnp.dot(inputs, weights[0].T, preferred_element_type=jnp.float32)
    hidden = jax.nn.silu(before).astype(jnp.bfloat16)
    back_grad = down_scale * jnp.dot(cotangent, weights[1].T, preferred_element_type=jnp.float32)
    slope_grad = (back_grad * silu_slope(before)).astype(jnp.bfloat16)
    grad_up = up_scale * jnp.dot(slope_grad.T, inputs, preferred_element_type=jnp.float32)
    grad_down = down_scale * jnp.dot(hidden.T, cotangent, preferred_element_type=jnp.float32)
    return jnp.stack([grad_up, grad_down])

def reference(master, moment, variance, flat_slot, feedback, activations, output_grads):
    master_t = tensor_order(master, flat_slot)
    working = master_t.astype(jnp.bfloat16)
    moment_t = tensor_order(moment, flat_slot)
    denominator = jnp.sqrt(tensor_order(variance, flat_slot)) + epsilon
    inputs_all = activations.reshape(2, N_DP, TOK, D)
    grads_all = output_grads.reshape(2, N_DP, TOK, D)

    def worker(sums, things):
        first_inputs, second_inputs, first_grads, second_grads, residue = things
        step_one = gradients(working, first_inputs, first_grads)
        local_moment = beta_one * moment_t + (1.0 - beta_one) * step_one
        local_weights = (working.astype(jnp.float32) - step_rate * local_moment / denominator).astype(jnp.bfloat16)
        step_two = gradients(local_weights, second_inputs, second_grads)
        shifted = local_moment + residue.astype(jnp.float32)
        magnitude = lax.optimization_barrier(jnp.mean(jnp.abs(shifted), axis=-1, keepdims=True)) + 1e-06
        packed = magnitude * jnp.tanh(shifted / magnitude)
        new_error = (shifted - packed).astype(jnp.bfloat16)
        return ((sums[0] + packed, sums[1] + step_two), new_error)
    empty_sums = jnp.zeros((2, HID, D), jnp.float32)
    (moment_sum, grad_sum), feedback_out = lax.scan(worker, (empty_sums, empty_sums), (inputs_all[0], inputs_all[1], grads_all[0], grads_all[1], feedback))
    mean_moment = moment_sum / N_DP
    mean_grad = grad_sum / N_DP
    moment_new = beta_one * mean_moment + (1.0 - beta_one) * mean_grad
    master_new = master_t - step_rate * (mean_moment + moment_new) / denominator
    return (flat_order(master_new, flat_slot), flat_order(moment_new, flat_slot), feedback_out)
```

```python
import functools

import jax
import jax.numpy as jnp
from jax import lax
from jax.experimental import pallas as pl
from jax.experimental.pallas import tpu as pltpu
from jax.sharding import PartitionSpec as P

beta_one = 0.9
step_rate = 0.05
epsilon = 1e-08
down_scale = 28672.0 ** (-0.5)
BF = jnp.bfloat16
F32 = jnp.float32
NT = (((1,), (1,)), ((), ()))
NN = (((1,), (0,)), ((), ()))


def dot(a, b, dims=NN):
    return lax.dot_general(a, b, dims, preferred_element_type=F32)


def swap(x, axis, mask):
    n = lax.axis_size(axis)
    return lax.ppermute(x, axis, [(i, i ^ mask) for i in range(n)])


def bits_of(n, lowest=1):
    masks = []
    mask = n // 2
    while mask >= lowest:
        masks.append(mask)
        mask //= 2
    return masks


def gradient_rows(weights, x_ref, g_ref, hidden_rows, up_scale):
    before = up_scale * dot(weights, x_ref[...], NT)[:hidden_rows]
    back = down_scale * dot(weights, g_ref[...], NT)[hidden_rows:]
    sigmoid = jax.nn.sigmoid(before)
    hidden = before * sigmoid
    slope = back * (sigmoid * (1.0 + before * (1.0 - sigmoid)))
    zeros = jnp.zeros_like(slope)
    left_up = jnp.concatenate([slope, zeros], axis=0).astype(BF)
    left_down = jnp.concatenate([zeros, hidden], axis=0).astype(BF)

    def columns(at):
        return up_scale * dot(left_up, x_ref[:, at]) + down_scale * dot(left_down, g_ref[:, at])

    return columns


def first_kernel(hidden_rows, up_scale, chunk, place_ref, w0_ref, w1_ref, x_ref, g_ref, weights_ref, part_ref):
    rows = 2 * hidden_rows
    segment = w0_ref.shape[1]
    half = w0_ref.shape[0]
    width = x_ref.shape[1]
    ordered = dot(place_ref[:, :half], w0_ref[...]) + dot(place_ref[:, half:], w1_ref[...])
    for c in range(width // segment):
        weights_ref[:, c * segment : (c + 1) * segment] = ordered[c * rows : (c + 1) * rows].astype(BF)
    columns = gradient_rows(weights_ref[...], x_ref, g_ref, hidden_rows, up_scale)
    for c in range(width // chunk):
        at = slice(c * chunk, (c + 1) * chunk)
        part_ref[:, at] = columns(at).astype(BF)


def moments_kernel(rows, place_ref, a0_ref, a1_ref, moment_ref, rate_ref):
    half = a0_ref.shape[0]
    segment = a0_ref.shape[1] // 2
    width = moment_ref.shape[1]
    ordered = dot(place_ref[:, :half], a0_ref[...]) + dot(place_ref[:, half:], a1_ref[...])
    rate = step_rate / (jnp.sqrt(ordered[:, segment:]) + epsilon)
    for c in range(width // segment):
        at = slice(c * segment, (c + 1) * segment)
        moment_ref[:, at] = ordered[c * rows : (c + 1) * rows, :segment]
        rate_ref[:, at] = rate[c * rows : (c + 1) * rows]


def second_kernel(
    hidden_rows, up_scale, own, back_ref, part_ref, got_ref, weights_ref, moment_ref, rate_ref, x_ref, g_ref, *rest
):
    if own:
        feedback_ref, grad_ref, packed_ref, error_ref, local_ref, seg_ref = rest
    else:
        grad_ref, local_ref, seg_ref = rest
    rows = 2 * hidden_rows
    segment = grad_ref.shape[1]
    width = x_ref.shape[1]
    step_one = part_ref[...].astype(F32) + got_ref[...].astype(F32)
    local_moment = beta_one * moment_ref[...] + (1.0 - beta_one) * step_one
    local_ref[...] = (weights_ref[...].astype(F32) - local_moment * rate_ref[...]).astype(BF)
    columns = gradient_rows(local_ref[...], x_ref, g_ref, hidden_rows, up_scale)
    for c in range(width // segment):
        seg_ref[c * rows : (c + 1) * rows] = columns(slice(c * segment, (c + 1) * segment)).astype(BF)
    grad_ref[...] = dot(back_ref[...], seg_ref[...]).astype(BF)
    if own:
        shifted = local_moment + feedback_ref[...].astype(F32)
        magnitude = jnp.sum(jnp.abs(shifted), axis=1, keepdims=True) * (1.0 / width) + 1e-06
        packed = magnitude * jnp.tanh(shifted / magnitude)
        error_ref[...] = (shifted - packed).astype(BF)
        for c in range(width // segment):
            seg_ref[c * rows : (c + 1) * rows] = packed[:, c * segment : (c + 1) * segment].astype(BF)
        packed_ref[...] = dot(back_ref[...], seg_ref[...]).astype(BF)


def call(kernel, out_shape, operands, scratch=()):
    return pl.pallas_call(
        kernel,
        out_shape=out_shape,
        in_specs=[pl.BlockSpec(memory_space=pltpu.VMEM)] * len(operands),
        out_specs=jax.tree.map(lambda _: pl.BlockSpec(memory_space=pltpu.VMEM), out_shape),
        scratch_shapes=list(scratch),
        compiler_params=pltpu.CompilerParams(vmem_limit_bytes=32 * 1024 * 1024),
    )(*operands)


def per_device(master, moment, variance, flat_slot, feedback, activations, output_grads):
    n_dp, n_mp = lax.axis_size("dp"), lax.axis_size("mp")
    me = lax.axis_index("dp")
    span, segment = master.shape[1:]
    segments = flat_slot.shape[0]
    hidden_rows, width = feedback.shape[2:]
    rows = 2 * hidden_rows
    up_scale = width ** (-0.5)
    far = bits_of(n_dp, 2)
    mp_bits = bits_of(n_mp)
    shape = jax.ShapeDtypeStruct

    near_w = master[0].astype(BF)
    near_a = jnp.concatenate([moment[0].astype(BF), variance[0].astype(BF)], axis=1)
    for mask in far:
        got_w = swap(near_w, "dp", mask)
        got_a = swap(near_a, "dp", mask)
        near_w = jnp.concatenate([near_w, got_w], axis=0)
        near_a = jnp.concatenate([near_a, got_a], axis=0)

    owner = (flat_slot // span) ^ me
    position = jnp.zeros_like(owner)
    for place, mask in enumerate(far + [1]):
        position = position + jnp.where((owner & mask) != 0, 1 << place, 0)
    position = position * span + flat_slot % span
    position = position.reshape(rows, width // segment).T.reshape(segments)
    line = jnp.arange(segments, dtype=jnp.int32)
    place_map = (position[:, None] == line[None, :]).astype(BF)
    back_map = (line[:, None] == position[None, :]).astype(BF)

    blocks_w, blocks_a = [near_w], [near_a]
    for mask in reversed(mp_bits):
        blocks_w = blocks_w + [swap(b, "mp", mask) for b in blocks_w]
        blocks_a = blocks_a + [swap(b, "mp", mask) for b in blocks_a]
    pairs_w = [(b, swap(b, "dp", 1)) for b in blocks_w]
    pairs_a = [(b, swap(b, "dp", 1)) for b in blocks_a]

    x_one, x_two = activations[0], activations[1]
    g_one, g_two = output_grads[0], output_grads[1]
    tensor = (rows, width)
    flat = (segments, segment)
    weights, parts = [], []
    for w0, w1 in pairs_w:
        kernel = functools.partial(first_kernel, hidden_rows, up_scale, min(width, 1024))
        w_t, part = call(kernel, (shape(tensor, BF), shape(tensor, BF)), (place_map, w0, w1, x_one, g_one))
        weights.append(w_t)
        parts.append(part)
    moments, rates = [], []
    for a0, a1 in pairs_a:
        kernel = functools.partial(moments_kernel, rows)
        m_t, rate = call(kernel, (shape(tensor, F32), shape(tensor, F32)), (place_map, a0, a1))
        moments.append(m_t)
        rates.append(rate)

    for step, mask in enumerate(mp_bits):
        sent = [swap(part, "mp", mask) for part in parts]
        got = [sent[k ^ mask] for k in range(n_mp)]
        if step < len(mp_bits) - 1:
            parts = [(p.astype(F32) + q.astype(F32)).astype(BF) for p, q in zip(parts, got)]

    grads = [None] * n_mp
    for k in reversed(range(n_mp)):
        own = k == 0
        operands = [back_map, parts[k], got[k], weights[k], moments[k], rates[k], x_two, g_two]
        out = [shape(flat, BF)]
        if own:
            operands.append(feedback[0].reshape(tensor))
            out += [shape(flat, BF), shape(tensor, BF)]
        result = call(
            functools.partial(second_kernel, hidden_rows, up_scale, own),
            tuple(out),
            operands,
            [pltpu.VMEM(tensor, BF), pltpu.VMEM(flat, BF)],
        )
        grads[k] = result[0]
        if own:
            packed, error = result[1], result[2]

    for mask in mp_bits:
        kept = [k for k in range(len(grads)) if not k & mask]
        got = {k: swap(grads[k ^ mask], "mp", mask) for k in kept}
        grads = [(grads[k].astype(F32) + got[k].astype(F32)).astype(BF) for k in kept]
    both = jnp.concatenate([grads[0], packed], axis=1)
    last = None
    for mask in [1] + far[::-1]:
        count = both.shape[0] // 2
        got = swap(both[count:], "dp", mask)
        last = both[:count].astype(F32) + got.astype(F32)
        both = last.astype(BF)
    mean_grad = last[:, :segment] / n_dp
    mean_moment = last[:, segment:] / n_dp
    moment_new = beta_one * mean_moment + (1.0 - beta_one) * mean_grad
    denominator = jnp.sqrt(variance[0]) + epsilon
    master_new = master[0] - step_rate * (mean_moment + moment_new) / denominator
    return (master_new[None], moment_new[None], error.reshape(feedback.shape))


def solution(mesh):
    in_specs = (
        P("mp", "dp", None),
        P("mp", "dp", None),
        P("mp", "dp", None),
        P(),
        P("dp", None, "mp", None),
        P(None, ("dp", "mp"), None),
        P(None, ("dp", "mp"), None),
    )
    out_specs = (P("mp", "dp", None), P("mp", "dp", None), P("dp", None, "mp", None))
    return jax.shard_map(
        per_device, mesh=mesh, in_specs=in_specs, out_specs=out_specs, check_vma=False
    )
```

```python
import functools

import jax
import jax.numpy as jnp
from jax import lax
from jax.experimental import pallas as pl
from jax.experimental.pallas import tpu as pltpu
from jax.sharding import PartitionSpec as P

beta_one = 0.9
step_rate = 0.05
epsilon = 1e-08
down_scale = 28672.0 ** (-0.5)
BF = jnp.bfloat16
F32 = jnp.float32
NT = (((1,), (1,)), ((), ()))
NN = (((1,), (0,)), ((), ()))


def dot(a, b, dims=NN):
    return lax.dot_general(a, b, dims, preferred_element_type=F32)


def swap(x, axis, mask):
    n = lax.axis_size(axis)
    return lax.ppermute(x, axis, [(i, i ^ mask) for i in range(n)])


def bits_of(n, lowest=1):
    masks = []
    mask = n // 2
    while mask >= lowest:
        masks.append(mask)
        mask //= 2
    return masks


def gradient_rows(weights, step, x_ref, g_ref, hidden_rows, up_scale):
    before = up_scale * dot(weights, x_ref[step], NT)[:hidden_rows]
    back = down_scale * dot(weights, g_ref[step], NT)[hidden_rows:]
    sigmoid = jax.nn.sigmoid(before)
    hidden = before * sigmoid
    slope = back * (sigmoid * (1.0 + before * (1.0 - sigmoid)))
    zeros = jnp.zeros_like(slope)
    left_up = jnp.concatenate([slope, zeros], axis=0).astype(BF)
    left_down = jnp.concatenate([zeros, hidden], axis=0).astype(BF)

    def columns(at):
        return up_scale * dot(left_up, x_ref[step, :, at]) + down_scale * dot(left_down, g_ref[step, :, at])

    return columns


def first_kernel(hidden_rows, up_scale, chunk, place_ref, w0_ref, w1_ref, x_ref, g_ref, weights_ref, part_ref, sent_ref):
    rows = 2 * hidden_rows
    half, segment = w0_ref.shape
    width = x_ref.shape[2]
    ordered = dot(place_ref[:, :half], w0_ref[...]) + dot(place_ref[:, half:], w1_ref[...])
    for c in range(width // segment):
        weights_ref[:, c * segment : (c + 1) * segment] = ordered[c * rows : (c + 1) * rows].astype(BF)
    columns = gradient_rows(weights_ref[...], 0, x_ref, g_ref, hidden_rows, up_scale)
    for c in range(width // chunk):
        at = slice(c * chunk, (c + 1) * chunk)
        part = columns(at)
        part_ref[:, at] = part
        sent_ref[:, at] = part.astype(BF)


def moments_kernel(rows, split, place_ref, a0_ref, a1_ref, moment_ref, rate_ref):
    half = a0_ref.shape[0]
    segment = a0_ref.shape[1] // (3 if split else 2)
    width = moment_ref.shape[1]
    ordered = dot(place_ref[:, :half], a0_ref[...]) + dot(place_ref[:, half:], a1_ref[...])
    moment = ordered[:, :segment]
    if split:
        moment = moment + ordered[:, segment : 2 * segment]
    rate = step_rate / (jnp.sqrt(ordered[:, -segment:]) + epsilon)
    for c in range(width // segment):
        at = slice(c * segment, (c + 1) * segment)
        moment_ref[:, at] = moment[c * rows : (c + 1) * rows]
        rate_ref[:, at] = rate[c * rows : (c + 1) * rows]


def second_kernel(
    hidden_rows, up_scale, own, back_ref, part_ref, got_ref, weights_ref, moment_ref, rate_ref, x_ref, g_ref, *rest
):
    if own:
        feedback_ref, kept_ref, sent_ref, error_ref, local_ref, seg_ref = rest
    else:
        kept_ref, sent_ref, local_ref, seg_ref = rest
    rows = 2 * hidden_rows
    half = kept_ref.shape[0]
    segment = seg_ref.shape[1]
    width = x_ref.shape[2]
    step_one = part_ref[...] + got_ref[...].astype(F32)
    local_moment = beta_one * moment_ref[...] + (1.0 - beta_one) * step_one
    local_ref[...] = (weights_ref[...].astype(F32) - local_moment * rate_ref[...]).astype(BF)
    columns = gradient_rows(local_ref[...], 1, x_ref, g_ref, hidden_rows, up_scale)
    for c in range(width // segment):
        seg_ref[c * rows : (c + 1) * rows] = columns(slice(c * segment, (c + 1) * segment)).astype(BF)
    flat = dot(back_ref[...], seg_ref[...]).astype(BF)
    kept_ref[:, :segment] = flat[:half]
    sent_ref[:, :segment] = flat[half:]
    if own:
        shifted = local_moment + feedback_ref[...].astype(F32)
        magnitude = jnp.sum(jnp.abs(shifted), axis=1, keepdims=True) * (1.0 / width) + 1e-06
        packed = magnitude * jnp.tanh(shifted / magnitude)
        error_ref[...] = (shifted - packed).astype(BF)
        for c in range(width // segment):
            seg_ref[c * rows : (c + 1) * rows] = packed[:, c * segment : (c + 1) * segment].astype(BF)
        flat = dot(back_ref[...], seg_ref[...]).astype(BF)
        kept_ref[:, segment:] = flat[:half]
        sent_ref[:, segment:] = flat[half:]


def call(kernel, out_shape, operands, scratch=()):
    return pl.pallas_call(
        kernel,
        out_shape=out_shape,
        in_specs=[pl.BlockSpec(memory_space=pltpu.VMEM)] * len(operands),
        out_specs=jax.tree.map(lambda _: pl.BlockSpec(memory_space=pltpu.VMEM), out_shape),
        scratch_shapes=list(scratch),
        compiler_params=pltpu.CompilerParams(vmem_limit_bytes=32 * 1024 * 1024),
    )(*operands)


def per_device(master, moment, variance, flat_slot, feedback, activations, output_grads):
    n_dp, n_mp = lax.axis_size("dp"), lax.axis_size("mp")
    me = lax.axis_index("dp")
    span, segment = master.shape[1:]
    segments = flat_slot.shape[0]
    hidden_rows, width = feedback.shape[2:]
    rows = 2 * hidden_rows
    up_scale = width ** (-0.5)
    far = bits_of(n_dp, 2)
    mp_bits = bits_of(n_mp)
    shape = jax.ShapeDtypeStruct

    near_w = master[0].astype(BF)
    for mask in far:
        near_w = jnp.concatenate([near_w, swap(near_w, "dp", mask)], axis=0)

    high = moment[0].astype(BF)
    low = (moment[0] - high.astype(F32)).astype(BF)
    spread = variance[0].astype(BF)
    blocks_a = [jnp.concatenate([high, spread], axis=1)]
    for mask in reversed(mp_bits):
        blocks_a = blocks_a + [swap(b, "mp", mask) for b in blocks_a]
    blocks_a[0] = jnp.concatenate([high, low, spread], axis=1)
    for mask in far:
        blocks_a = [jnp.concatenate([b, swap(b, "dp", mask)], axis=0) for b in blocks_a]

    owner = (flat_slot // span) ^ me
    position = jnp.zeros_like(owner)
    for place, mask in enumerate(far + [1]):
        position = position + jnp.where((owner & mask) != 0, 1 << place, 0)
    position = position * span + flat_slot % span
    position = position.reshape(rows, width // segment).T.reshape(segments)
    line = jnp.arange(segments, dtype=jnp.int32)
    place_map = (position[:, None] == line[None, :]).astype(BF)
    back_map = (line[:, None] == position[None, :]).astype(BF)

    blocks_w = [near_w]
    for mask in reversed(mp_bits):
        blocks_w = blocks_w + [swap(b, "mp", mask) for b in blocks_w]
    pairs_w = [(b, swap(b, "dp", 1)) for b in blocks_w]
    pairs_a = [(b, swap(b, "dp", 1)) for b in blocks_a]

    tensor = (rows, width)
    half = segments // 2
    weights, parts, sent = [], [], []
    for w0, w1 in pairs_w:
        kernel = functools.partial(first_kernel, hidden_rows, up_scale, min(width, 1024))
        out = (shape(tensor, BF), shape(tensor, F32), shape(tensor, BF))
        w_t, part, part_sent = call(kernel, out, (place_map, w0, w1, activations, output_grads))
        weights.append(w_t)
        parts.append(part)
        sent.append(part_sent)
    moments, rates = [], []
    for k, (a0, a1) in enumerate(pairs_a):
        kernel = functools.partial(moments_kernel, rows, k == 0)
        m_t, rate = call(kernel, (shape(tensor, F32), shape(tensor, F32)), (place_map, a0, a1))
        moments.append(m_t)
        rates.append(rate)

    for step, mask in enumerate(mp_bits):
        if step > 0:
            parts = [p + q.astype(F32) for p, q in zip(parts, got)]
            sent = [p.astype(BF) for p in parts]
        crossed = [swap(p, "mp", mask) for p in sent]
        got = [crossed[k ^ mask] for k in range(n_mp)]

    kept, sent = [None] * n_mp, [None] * n_mp
    for k in reversed(range(n_mp)):
        own = k == 0
        operands = [back_map, parts[k], got[k], weights[k], moments[k], rates[k], activations, output_grads]
        lanes = 2 * segment if own else segment
        out = [shape((half, lanes), BF), shape((half, lanes), BF)]
        if own:
            operands.append(feedback[0].reshape(tensor))
            out.append(shape(tensor, BF))
        result = call(
            functools.partial(second_kernel, hidden_rows, up_scale, own),
            tuple(out),
            operands,
            [pltpu.VMEM(tensor, BF), pltpu.VMEM((segments, segment), BF)],
        )
        kept[k], sent[k] = result[:2]
        if own:
            error = result[2]

    sums = [p.astype(F32) + swap(q, "dp", 1).astype(F32) for p, q in zip(kept, sent)]
    total, packed = sums[0][:, :segment], sums[0][:, segment:]
    grads = [total] + sums[1:]
    for mask in mp_bits:
        stay = [k for k in range(len(grads)) if not k & mask]
        got = {k: swap(grads[k ^ mask].astype(BF), "mp", mask) for k in stay}
        grads = [grads[k] + got[k].astype(F32) for k in stay]
    last = jnp.concatenate([grads[0], packed], axis=1)
    for mask in far[::-1]:
        count = last.shape[0] // 2
        last = last[:count] + swap(last[count:].astype(BF), "dp", mask).astype(F32)
    mean_grad = last[:, :segment] / n_dp
    mean_moment = last[:, segment:] / n_dp
    moment_new = beta_one * mean_moment + (1.0 - beta_one) * mean_grad
    denominator = jnp.sqrt(variance[0]) + epsilon
    master_new = master[0] - step_rate * (mean_moment + moment_new) / denominator
    return (master_new[None], moment_new[None], error.reshape(feedback.shape))


def solution(mesh):
    in_specs = (
        P("mp", "dp", None),
        P("mp", "dp", None),
        P("mp", "dp", None),
        P(),
        P("dp", None, "mp", None),
        P(None, ("dp", "mp"), None),
        P(None, ("dp", "mp"), None),
    )
    out_specs = (P("mp", "dp", None), P("mp", "dp", None), P("dp", None, "mp", None))
    return jax.shard_map(
        per_device, mesh=mesh, in_specs=in_specs, out_specs=out_specs, check_vma=False
    )
```

```python
import functools

import jax
import jax.numpy as jnp
from jax import lax
from jax.experimental import pallas as pl
from jax.experimental.pallas import tpu as pltpu
from jax.sharding import PartitionSpec as P

beta_one = 0.9
step_rate = 0.05
epsilon = 1e-08
down_scale = 28672.0 ** (-0.5)
BF = jnp.bfloat16
F32 = jnp.float32
NT = (((1,), (1,)), ((), ()))
NN = (((1,), (0,)), ((), ()))


def dot(a, b, dims=NN):
    return lax.dot_general(a, b, dims, preferred_element_type=F32)


def swap(x, axis, mask):
    n = lax.axis_size(axis)
    return lax.ppermute(x, axis, [(i, i ^ mask) for i in range(n)])


def after(x, *others):
    return lax.optimization_barrier((x, *others))[0]


def bits_of(n, lowest=1):
    masks = []
    mask = n // 2
    while mask >= lowest:
        masks.append(mask)
        mask //= 2
    return masks


def gradient_rows(weights, x_ref, g_ref, hidden_rows, up_scale):
    before = up_scale * dot(weights, x_ref[...], NT)[:hidden_rows]
    back = down_scale * dot(weights, g_ref[...], NT)[hidden_rows:]
    sigmoid = jax.nn.sigmoid(before)
    hidden = before * sigmoid
    slope = back * (sigmoid * (1.0 + before * (1.0 - sigmoid)))
    zeros = jnp.zeros_like(slope)
    left_up = jnp.concatenate([slope, zeros], axis=0).astype(BF)
    left_down = jnp.concatenate([zeros, hidden], axis=0).astype(BF)

    def columns(at):
        return up_scale * dot(left_up, x_ref[:, at]) + down_scale * dot(left_down, g_ref[:, at])

    return columns


def first_kernel(hidden_rows, up_scale, chunk, place_ref, w0_ref, w1_ref, x_ref, g_ref, weights_ref, part_ref, sent_ref):
    rows = 2 * hidden_rows
    half, segment = w0_ref.shape
    width = x_ref.shape[1]
    ordered = dot(place_ref[:, :half], w0_ref[...]) + dot(place_ref[:, half:], w1_ref[...])
    for c in range(width // segment):
        weights_ref[:, c * segment : (c + 1) * segment] = ordered[c * rows : (c + 1) * rows].astype(BF)
    columns = gradient_rows(weights_ref[...], x_ref, g_ref, hidden_rows, up_scale)
    for c in range(width // chunk):
        at = slice(c * chunk, (c + 1) * chunk)
        part = columns(at)
        part_ref[:, at] = part
        sent_ref[:, at] = part.astype(BF)


def moments_kernel(rows, split, place_ref, a0_ref, a1_ref, moment_ref, rate_ref):
    half = a0_ref.shape[0]
    segment = a0_ref.shape[1] // (3 if split else 2)
    width = moment_ref.shape[1]
    ordered = dot(place_ref[:, :half], a0_ref[...]) + dot(place_ref[:, half:], a1_ref[...])
    moment = ordered[:, :segment]
    if split:
        moment = moment + ordered[:, segment : 2 * segment]
    rate = step_rate / (jnp.sqrt(ordered[:, -segment:]) + epsilon)
    for c in range(width // segment):
        at = slice(c * segment, (c + 1) * segment)
        moment_ref[:, at] = moment[c * rows : (c + 1) * rows]
        rate_ref[:, at] = rate[c * rows : (c + 1) * rows]


def second_kernel(
    hidden_rows, up_scale, own, back_ref, part_ref, got_ref, weights_ref, moment_ref, rate_ref, x_ref, g_ref, *rest
):
    if own:
        feedback_ref, grad_ref, packed_ref, error_ref, local_ref, seg_ref = rest
    else:
        grad_ref, local_ref, seg_ref = rest
    rows = 2 * hidden_rows
    segment = seg_ref.shape[1]
    width = x_ref.shape[1]
    step_one = part_ref[...] + got_ref[...].astype(F32)
    local_moment = beta_one * moment_ref[...] + (1.0 - beta_one) * step_one
    local_ref[...] = (weights_ref[...].astype(F32) - local_moment * rate_ref[...]).astype(BF)
    columns = gradient_rows(local_ref[...], x_ref, g_ref, hidden_rows, up_scale)
    for c in range(width // segment):
        seg_ref[c * rows : (c + 1) * rows] = columns(slice(c * segment, (c + 1) * segment)).astype(BF)
    grad_ref[...] = dot(back_ref[...], seg_ref[...]).astype(BF)
    if own:
        shifted = local_moment + feedback_ref[...].astype(F32)
        magnitude = jnp.sum(jnp.abs(shifted), axis=1, keepdims=True) * (1.0 / width) + 1e-06
        packed = magnitude * jnp.tanh(shifted / magnitude)
        error_ref[...] = (shifted - packed).astype(BF)
        for c in range(width // segment):
            seg_ref[c * rows : (c + 1) * rows] = packed[:, c * segment : (c + 1) * segment].astype(BF)
        packed_ref[...] = dot(back_ref[...], seg_ref[...]).astype(BF)


def tokens_of(step, arrays, *others):
    return [x[step] for x in lax.optimization_barrier((*arrays, *others))[: len(arrays)]]


def call(kernel, out_shape, operands, scratch=()):
    return pl.pallas_call(
        kernel,
        out_shape=out_shape,
        in_specs=[pl.BlockSpec(memory_space=pltpu.VMEM)] * len(operands),
        out_specs=jax.tree.map(lambda _: pl.BlockSpec(memory_space=pltpu.VMEM), out_shape),
        scratch_shapes=list(scratch),
        cost_estimate=pl.CostEstimate(flops=1, bytes_accessed=1, transcendentals=0),
        compiler_params=pltpu.CompilerParams(vmem_limit_bytes=16 * 1024 * 1024),
    )(*operands)


def per_device(master, moment, variance, flat_slot, feedback, activations, output_grads):
    n_dp, n_mp = lax.axis_size("dp"), lax.axis_size("mp")
    me = lax.axis_index("dp")
    span, segment = master.shape[1:]
    segments = flat_slot.shape[0]
    hidden_rows, width = feedback.shape[2:]
    rows = 2 * hidden_rows
    up_scale = width ** (-0.5)
    far = bits_of(n_dp, 2)
    mp_bits = bits_of(n_mp)
    shape = jax.ShapeDtypeStruct

    near_w = master[0].astype(BF)
    exact = after(moment[0], near_w)
    high = lax.reduce_precision(exact, 8, 7)
    low = (exact - high).astype(BF)
    high, spread = high.astype(BF), variance[0].astype(BF)
    blocks_a = [jnp.concatenate([high, low, spread], axis=1)]
    near_a = jnp.concatenate([high, spread], axis=1)
    steps = []
    for mask in far:
        near_w = jnp.concatenate([near_w, swap(near_w, "dp", mask)], axis=0)
        steps.append(near_w)
    others = [near_a]
    for mask in reversed(mp_bits):
        others = others + [swap(after(b, steps[0]), "mp", mask) for b in others]
    blocks_a = blocks_a + others[1:]
    for mask, step in zip(far, steps):
        blocks_a = [jnp.concatenate([b, swap(after(b, step), "dp", mask)], axis=0) for b in blocks_a]

    owner = (flat_slot // span) ^ me
    position = jnp.zeros_like(owner)
    for place, mask in enumerate(far + [1]):
        position = position + jnp.where((owner & mask) != 0, 1 << place, 0)
    position = position * span + flat_slot % span
    position = position.reshape(rows, width // segment).T.reshape(segments)
    line = jnp.arange(segments, dtype=jnp.int32)
    place_map = (position[:, None] == line[None, :]).astype(BF)
    back_map = (line[:, None] == position[None, :]).astype(BF)

    blocks_w = [near_w]
    for mask in reversed(mp_bits):
        blocks_w = blocks_w + [swap(b, "mp", mask) for b in blocks_w]
    pairs_w = [(b, swap(b, "dp", 1)) for b in blocks_w]

    tensor = (rows, width)
    one = tokens_of(0, (activations, output_grads), steps[0])
    half = segments // 2
    weights, parts, sent = [], [], []
    for w0, w1 in pairs_w:
        kernel = functools.partial(first_kernel, hidden_rows, up_scale, min(width, 1024))
        out = (shape(tensor, BF), shape(tensor, F32), shape(tensor, BF))
        w_t, part, part_sent = call(kernel, out, (place_map, w0, w1, *one))
        weights.append(w_t)
        parts.append(part)
        sent.append(part_sent)
    two = tokens_of(1, (activations, output_grads), sent[0])

    for step, mask in enumerate(mp_bits):
        if step > 0:
            parts = [p + q.astype(F32) for p, q in zip(parts, got)]
            sent = [p.astype(BF) for p in parts]
        crossed = [swap(p, "mp", mask) for p in sent]
        got = [crossed[k ^ mask] for k in range(n_mp)]

    pairs_a = [(b, swap(b, "dp", 1)) for b in blocks_a]
    moments, rates = [], []
    for k, (a0, a1) in enumerate(pairs_a):
        kernel = functools.partial(moments_kernel, rows, k == 0)
        m_t, rate = call(kernel, (shape(tensor, F32), shape(tensor, F32)), (place_map, a0, a1))
        moments.append(m_t)
        rates.append(rate)

    grads = [None] * n_mp
    for k in reversed(range(n_mp)):
        own = k == 0
        operands = [back_map, parts[k], got[k], weights[k], moments[k], rates[k], *two]
        out = [shape((segments, segment), BF)]
        if own:
            operands.append(feedback[0].reshape(tensor))
            out += [shape((segments, segment), BF), shape(tensor, BF)]
        result = call(
            functools.partial(second_kernel, hidden_rows, up_scale, own),
            tuple(out),
            operands,
            [pltpu.VMEM(tensor, BF), pltpu.VMEM((segments, segment), BF)],
        )
        grads[k] = result[0]
    packed, error = result[1:]
    for mask in mp_bits:
        crossing = [p.astype(BF) for p in grads[mask:]]
        grads = [p.astype(F32) + swap(q, "mp", mask).astype(F32) for p, q in zip(grads, crossing)]
    last = jnp.concatenate([grads[0], packed.astype(F32)], axis=1)
    for mask in [1] + far[::-1]:
        count = last.shape[0] // 2
        last = last[:count] + swap(last[count:].astype(BF), "dp", mask).astype(F32)
    mean_grad = last[:, :segment] / n_dp
    mean_moment = last[:, segment:] / n_dp
    moment_new = beta_one * mean_moment + (1.0 - beta_one) * mean_grad
    denominator = jnp.sqrt(variance[0]) + epsilon
    master_new = master[0] - step_rate * (mean_moment + moment_new) / denominator
    return (master_new[None], moment_new[None], error.reshape(feedback.shape))


def solution(mesh):
    in_specs = (
        P("mp", "dp", None),
        P("mp", "dp", None),
        P("mp", "dp", None),
        P(),
        P("dp", None, "mp", None),
        P(None, ("dp", "mp"), None),
        P(None, ("dp", "mp"), None),
    )
    out_specs = (P("mp", "dp", None), P("mp", "dp", None), P("dp", None, "mp", None))
    return jax.shard_map(
        per_device, mesh=mesh, in_specs=in_specs, out_specs=out_specs, check_vma=False
    )
```

```python
import functools

import jax
import jax.numpy as jnp
from jax import lax
from jax.experimental import pallas as pl
from jax.experimental.pallas import tpu as pltpu
from jax.sharding import PartitionSpec as P

beta_one = 0.9
step_rate = 0.05
epsilon = 1e-08
down_scale = 28672.0 ** (-0.5)
BF = jnp.bfloat16
F32 = jnp.float32
NT = (((1,), (1,)), ((), ()))
NN = (((1,), (0,)), ((), ()))


def dot(a, b, dims=NN):
    return lax.dot_general(a, b, dims, preferred_element_type=F32)


def swap(x, axis, mask):
    n = lax.axis_size(axis)
    return lax.ppermute(x, axis, [(i, i ^ mask) for i in range(n)])


def after(x, *others):
    return lax.optimization_barrier((x, *others))[0]


def bits_of(n, lowest=1):
    masks = []
    mask = n // 2
    while mask >= lowest:
        masks.append(mask)
        mask //= 2
    return masks


def gradient_rows(weights, x_ref, g_ref, hidden_rows, up_scale):
    before = up_scale * dot(weights, x_ref[...], NT)[:hidden_rows]
    back = down_scale * dot(weights, g_ref[...], NT)[hidden_rows:]
    sigmoid = jax.nn.sigmoid(before)
    hidden = before * sigmoid
    slope = back * (sigmoid * (1.0 + before * (1.0 - sigmoid)))
    zeros = jnp.zeros_like(slope)
    left_up = jnp.concatenate([slope, zeros], axis=0).astype(BF)
    left_down = jnp.concatenate([zeros, hidden], axis=0).astype(BF)

    def columns(at):
        return up_scale * dot(left_up, x_ref[:, at]) + down_scale * dot(left_down, g_ref[:, at])

    return columns


def first_kernel(hidden_rows, up_scale, chunk, place_ref, w0_ref, w1_ref, x_ref, g_ref, weights_ref, part_ref, sent_ref):
    rows = 2 * hidden_rows
    half, segment = w0_ref.shape
    width = x_ref.shape[1]
    ordered = dot(place_ref[:, :half], w0_ref[...]) + dot(place_ref[:, half:], w1_ref[...])
    for c in range(width // segment):
        weights_ref[:, c * segment : (c + 1) * segment] = ordered[c * rows : (c + 1) * rows].astype(BF)
    columns = gradient_rows(weights_ref[...], x_ref, g_ref, hidden_rows, up_scale)
    for c in range(width // chunk):
        at = slice(c * chunk, (c + 1) * chunk)
        part = columns(at)
        part_ref[:, at] = part
        sent_ref[:, at] = part.astype(BF)


def moments_kernel(rows, place_ref, *refs):
    terms, (moment_ref, rate_ref) = refs[:-2], refs[-2:]
    count = len(terms) // 2
    half, segment = terms[0].shape
    width = moment_ref.shape[1]
    near, far = place_ref[:, :half], place_ref[:, half:]
    ordered = [dot(near, a[...]) + dot(far, b[...]) for a, b in zip(terms[:count], terms[count:])]
    moment = sum(ordered[1:-1], ordered[0])
    rate = step_rate / (jnp.sqrt(ordered[-1]) + epsilon)
    for c in range(width // segment):
        at = slice(c * segment, (c + 1) * segment)
        moment_ref[:, at] = moment[c * rows : (c + 1) * rows]
        rate_ref[:, at] = rate[c * rows : (c + 1) * rows]


def second_kernel(
    hidden_rows, up_scale, own, back_ref, part_ref, got_ref, weights_ref, moment_ref, rate_ref, x_ref, g_ref, *rest
):
    if own:
        feedback_ref, grad_ref, packed_ref, error_ref, local_ref, seg_ref = rest
    else:
        grad_ref, local_ref, seg_ref = rest
    rows = 2 * hidden_rows
    segment = seg_ref.shape[1]
    width = x_ref.shape[1]
    step_one = part_ref[...] + got_ref[...].astype(F32)
    local_moment = beta_one * moment_ref[...] + (1.0 - beta_one) * step_one
    local_ref[...] = (weights_ref[...].astype(F32) - local_moment * rate_ref[...]).astype(BF)
    columns = gradient_rows(local_ref[...], x_ref, g_ref, hidden_rows, up_scale)
    for c in range(width // segment):
        seg_ref[c * rows : (c + 1) * rows] = columns(slice(c * segment, (c + 1) * segment)).astype(BF)
    grad_ref[...] = dot(back_ref[...], seg_ref[...]).astype(BF)
    if own:
        shifted = local_moment + feedback_ref[...].astype(F32)
        magnitude = jnp.sum(jnp.abs(shifted), axis=1, keepdims=True) * (1.0 / width) + 1e-06
        packed = magnitude * jnp.tanh(shifted / magnitude)
        error_ref[...] = (shifted - packed).astype(BF)
        for c in range(width // segment):
            seg_ref[c * rows : (c + 1) * rows] = packed[:, c * segment : (c + 1) * segment].astype(BF)
        packed_ref[...] = dot(back_ref[...], seg_ref[...]).astype(BF)


def split_kernel(moment_ref, variance_ref, own_ref, near_ref):
    segment = moment_ref.shape[1]
    high = moment_ref[...].astype(BF)
    spread = variance_ref[...].astype(BF)
    own_ref[:, :segment] = high
    own_ref[:, segment : 2 * segment] = (moment_ref[...] - high.astype(F32)).astype(BF)
    own_ref[:, 2 * segment :] = spread
    near_ref[:, :segment] = high
    near_ref[:, segment:] = spread


def tokens_of(step, arrays, *others):
    return [x[step] for x in lax.optimization_barrier((*arrays, *others))[: len(arrays)]]


def call(kernel, out_shape, operands, scratch=()):
    return pl.pallas_call(
        kernel,
        out_shape=out_shape,
        in_specs=[pl.BlockSpec(memory_space=pltpu.VMEM)] * len(operands),
        out_specs=jax.tree.map(lambda _: pl.BlockSpec(memory_space=pltpu.VMEM), out_shape),
        scratch_shapes=list(scratch),
        cost_estimate=pl.CostEstimate(flops=1, bytes_accessed=1, transcendentals=0),
        compiler_params=pltpu.CompilerParams(vmem_limit_bytes=16 * 1024 * 1024),
    )(*operands)


def per_device(master, moment, variance, flat_slot, feedback, activations, output_grads):
    n_dp, n_mp = lax.axis_size("dp"), lax.axis_size("mp")
    me = lax.axis_index("dp")
    span, segment = master.shape[1:]
    segments = flat_slot.shape[0]
    hidden_rows, width = feedback.shape[2:]
    rows = 2 * hidden_rows
    up_scale = width ** (-0.5)
    far = bits_of(n_dp, 2)
    mp_bits = bits_of(n_mp)
    shape = jax.ShapeDtypeStruct

    near_w = master[0].astype(BF)
    own_a, near_a = call(
        split_kernel,
        (shape((span, 3 * segment), BF), shape((span, 2 * segment), BF)),
        (after(moment[0], near_w), variance[0]),
    )
    steps = []
    for mask in far:
        near_w = jnp.concatenate([near_w, swap(near_w, "dp", mask)], axis=0)
        steps.append(near_w)
    others = [near_a]
    for mask in reversed(mp_bits):
        others = others + [swap(b, "mp", mask) for b in others]
    blocks_a = [after(own_a, steps[0])] + others[1:]

    slot = after(flat_slot, steps[-1])
    owner = (slot // span) ^ me
    position = jnp.zeros_like(owner)
    for place, mask in enumerate(far + [1]):
        position = position + jnp.where((owner & mask) != 0, 1 << place, 0)
    position = position * span + slot % span
    position = position.reshape(rows, width // segment).T.reshape(segments)
    line = jnp.arange(segments, dtype=jnp.int32)
    place_map = (position[:, None] == line[None, :]).astype(BF)
    back_map = (line[:, None] == position[None, :]).astype(BF)

    blocks_w = [near_w]
    for mask in reversed(mp_bits):
        blocks_w = blocks_w + [swap(b, "mp", mask) for b in blocks_w]
    pairs_w = [(b, swap(b, "dp", 1)) for b in blocks_w]

    tensor = (rows, width)
    one = tokens_of(0, (activations, output_grads), steps[-2])
    half = segments // 2
    weights, parts, sent = [], [], []
    for w0, w1 in pairs_w:
        kernel = functools.partial(first_kernel, hidden_rows, up_scale, min(width, 1024))
        out = (shape(tensor, BF), shape(tensor, F32), shape(tensor, BF))
        w_t, part, part_sent = call(kernel, out, (place_map, w0, w1, *one))
        weights.append(w_t)
        parts.append(part)
        sent.append(part_sent)
    two = tokens_of(1, (activations, output_grads), sent[-1])

    for step, mask in enumerate(mp_bits):
        if step > 0:
            parts = [p + q.astype(F32) for p, q in zip(parts, got)]
            sent = [p.astype(BF) for p in parts]
        crossed = [swap(p, "mp", mask) for p in sent]
        got = [crossed[k ^ mask] for k in range(n_mp)]

    for mask, event in zip(far[:-1], [steps[-1]] * (len(far) - 2) + [sent[0]]):
        arrived = [after(swap(b, "dp", mask), event) for b in blocks_a]
        blocks_a = [jnp.concatenate(pair, axis=0) for pair in zip(blocks_a, arrived)]
    arrived = [swap(b, "dp", far[-1]) for b in blocks_a]

    grads, event = [None] * n_mp, sent[-1]
    for k in reversed(range(n_mp)):
        own = k == 0
        block = jnp.concatenate([blocks_a[k], after(arrived[k], event)], axis=0)
        terms = [block[:, at : at + segment] for at in range(0, block.shape[1], segment)]
        terms += [swap(term, "dp", 1) for term in terms]
        moment_t, rate = call(
            functools.partial(moments_kernel, rows), (shape(tensor, F32), shape(tensor, F32)), (place_map, *terms)
        )
        operands = [back_map, parts[k], got[k], weights[k], moment_t, rate, *two]
        out = [shape((segments, segment), BF)]
        if own:
            operands.append(feedback[0].reshape(tensor))
            out += [shape((segments, segment), BF), shape(tensor, BF)]
        result = call(
            functools.partial(second_kernel, hidden_rows, up_scale, own),
            tuple(out),
            operands,
            [pltpu.VMEM(tensor, BF), pltpu.VMEM((segments, segment), BF)],
        )
        grads[k] = result[0]
        event = grads[k]
    packed, error = result[1:]
    for mask in mp_bits:
        crossing = [p.astype(BF) for p in grads[mask:]]
        grads = [p.astype(F32) + swap(q, "mp", mask).astype(F32) for p, q in zip(grads, crossing)]
    last = jnp.concatenate([grads[0], packed.astype(F32)], axis=1)
    for mask in [1] + far[::-1]:
        count = last.shape[0] // 2
        last = last[:count] + swap(last[count:].astype(BF), "dp", mask).astype(F32)
    mean_grad = last[:, :segment] / n_dp
    mean_moment = last[:, segment:] / n_dp
    moment_new = beta_one * mean_moment + (1.0 - beta_one) * mean_grad
    denominator = jnp.sqrt(variance[0]) + epsilon
    master_new = master[0] - step_rate * (mean_moment + moment_new) / denominator
    return (master_new[None], moment_new[None], error.reshape(feedback.shape))


def solution(mesh):
    in_specs = (
        P("mp", "dp", None),
        P("mp", "dp", None),
        P("mp", "dp", None),
        P(),
        P("dp", None, "mp", None),
        P(None, ("dp", "mp"), None),
        P(None, ("dp", "mp"), None),
    )
    out_specs = (P("mp", "dp", None), P("mp", "dp", None), P("dp", None, "mp", None))
    return jax.shard_map(
        per_device, mesh=mesh, in_specs=in_specs, out_specs=out_specs, check_vma=False
    )
```

```python
import functools

import jax
import jax.numpy as jnp
from jax import lax
from jax.experimental import pallas as pl
from jax.experimental.pallas import tpu as pltpu
from jax.sharding import PartitionSpec as P

beta_one = 0.9
step_rate = 0.05
epsilon = 1e-08
down_scale = 28672.0 ** (-0.5)
BF = jnp.bfloat16
F32 = jnp.float32
NT = (((1,), (1,)), ((), ()))
NN = (((1,), (0,)), ((), ()))


def dot(a, b, dims=NN):
    return lax.dot_general(a, b, dims, preferred_element_type=F32)


def swap(x, axis, mask):
    n = lax.axis_size(axis)
    return lax.ppermute(x, axis, [(i, i ^ mask) for i in range(n)])


def after(x, *others):
    return lax.optimization_barrier((x, *others))[0]


def bits_of(n, lowest=1):
    masks = []
    mask = n // 2
    while mask >= lowest:
        masks.append(mask)
        mask //= 2
    return masks


def gradient_rows(weights, x_ref, g_ref, hidden_rows, up_scale):
    before = up_scale * dot(weights, x_ref[...], NT)[:hidden_rows]
    back = down_scale * dot(weights, g_ref[...], NT)[hidden_rows:]
    sigmoid = jax.nn.sigmoid(before)
    hidden = before * sigmoid
    slope = back * (sigmoid * (1.0 + before * (1.0 - sigmoid)))
    zeros = jnp.zeros_like(slope)
    left_up = jnp.concatenate([slope, zeros], axis=0).astype(BF)
    left_down = jnp.concatenate([zeros, hidden], axis=0).astype(BF)

    def columns(at):
        return up_scale * dot(left_up, x_ref[:, at]) + down_scale * dot(left_down, g_ref[:, at])

    return columns


def first_kernel(hidden_rows, up_scale, chunk, place_ref, w0_ref, w1_ref, x_ref, g_ref, weights_ref, part_ref, sent_ref):
    rows = 2 * hidden_rows
    half, segment = w0_ref.shape
    width = x_ref.shape[1]
    ordered = dot(place_ref[:, :half], w0_ref[...]) + dot(place_ref[:, half:], w1_ref[...])
    for c in range(width // segment):
        weights_ref[:, c * segment : (c + 1) * segment] = ordered[c * rows : (c + 1) * rows].astype(BF)
    columns = gradient_rows(weights_ref[...], x_ref, g_ref, hidden_rows, up_scale)
    for c in range(width // chunk):
        at = slice(c * chunk, (c + 1) * chunk)
        part = columns(at)
        part_ref[:, at] = part
        sent_ref[:, at] = part.astype(BF)


def moments_kernel(rows, place_ref, *refs):
    terms, (moment_ref, rate_ref) = refs[:-2], refs[-2:]
    count = len(terms) // 2
    half, segment = terms[0].shape
    width = moment_ref.shape[1]
    near, far = place_ref[:, :half], place_ref[:, half:]
    ordered = [dot(near, a[...]) + dot(far, b[...]) for a, b in zip(terms[:count], terms[count:])]
    moment = sum(ordered[1:-1], ordered[0])
    rate = step_rate / (jnp.sqrt(ordered[-1]) + epsilon)
    for c in range(width // segment):
        at = slice(c * segment, (c + 1) * segment)
        moment_ref[:, at] = moment[c * rows : (c + 1) * rows]
        rate_ref[:, at] = rate[c * rows : (c + 1) * rows]


def store_flat(back_ref, seg_ref, refs):
    flat = dot(back_ref[...], seg_ref[...]).astype(BF)
    count = flat.shape[0] // len(refs)
    for i, ref in enumerate(refs):
        ref[...] = flat[i * count : (i + 1) * count]


def second_kernel(
    hidden_rows, up_scale, own, back_ref, part_ref, got_ref, weights_ref, moment_ref, rate_ref, x_ref, g_ref, *rest
):
    if own:
        feedback_ref, *flat_refs, error_ref, local_ref, seg_ref = rest
    else:
        *flat_refs, local_ref, seg_ref = rest
    rows = 2 * hidden_rows
    segment = seg_ref.shape[1]
    width = x_ref.shape[1]
    step_one = part_ref[...] + got_ref[...].astype(F32)
    local_moment = beta_one * moment_ref[...] + (1.0 - beta_one) * step_one
    local_ref[...] = (weights_ref[...].astype(F32) - local_moment * rate_ref[...]).astype(BF)
    columns = gradient_rows(local_ref[...], x_ref, g_ref, hidden_rows, up_scale)
    for c in range(width // segment):
        seg_ref[c * rows : (c + 1) * rows] = columns(slice(c * segment, (c + 1) * segment)).astype(BF)
    store_flat(back_ref, seg_ref, flat_refs[:2] if own else flat_refs)
    if own:
        shifted = local_moment + feedback_ref[...].astype(F32)
        magnitude = jnp.sum(jnp.abs(shifted), axis=1, keepdims=True) * (1.0 / width) + 1e-06
        packed = magnitude * jnp.tanh(shifted / magnitude)
        error_ref[...] = (shifted - packed).astype(BF)
        for c in range(width // segment):
            seg_ref[c * rows : (c + 1) * rows] = packed[:, c * segment : (c + 1) * segment].astype(BF)
        store_flat(back_ref, seg_ref, flat_refs[2:])


def cast_kernel(master_ref, moment_ref, variance_ref, weights_ref, own_ref, near_ref):
    segment = master_ref.shape[1]
    weights_ref[...] = master_ref[...].astype(BF)
    high = moment_ref[...].astype(BF)
    spread = variance_ref[...].astype(BF)
    own_ref[:, :segment] = high
    own_ref[:, segment : 2 * segment] = (moment_ref[...] - high.astype(F32)).astype(BF)
    own_ref[:, 2 * segment :] = spread
    near_ref[:, :segment] = high
    near_ref[:, segment:] = spread


def tokens_of(step, arrays, *others):
    return [x[step] for x in lax.optimization_barrier((*arrays, *others))[: len(arrays)]]


def call(kernel, out_shape, operands, scratch=()):
    return pl.pallas_call(
        kernel,
        out_shape=out_shape,
        in_specs=[pl.BlockSpec(memory_space=pltpu.VMEM)] * len(operands),
        out_specs=jax.tree.map(lambda _: pl.BlockSpec(memory_space=pltpu.VMEM), out_shape),
        scratch_shapes=list(scratch),
        cost_estimate=pl.CostEstimate(flops=1, bytes_accessed=1, transcendentals=0),
        compiler_params=pltpu.CompilerParams(vmem_limit_bytes=16 * 1024 * 1024),
    )(*operands)


def per_device(master, moment, variance, flat_slot, feedback, activations, output_grads):
    n_dp, n_mp = lax.axis_size("dp"), lax.axis_size("mp")
    me = lax.axis_index("dp")
    span, segment = master.shape[1:]
    segments = flat_slot.shape[0]
    hidden_rows, width = feedback.shape[2:]
    rows = 2 * hidden_rows
    up_scale = width ** (-0.5)
    far = bits_of(n_dp, 2)
    mp_bits = bits_of(n_mp)
    shape = jax.ShapeDtypeStruct

    near_w, own_a, near_a = call(
        cast_kernel,
        tuple(shape((span, terms * segment), BF) for terms in (1, 3, 2)),
        (master[0], moment[0], variance[0]),
    )

    owner = (flat_slot // span) ^ me
    position = jnp.zeros_like(owner)
    for place, mask in enumerate(far + [1]):
        position = position + jnp.where((owner & mask) != 0, 1 << place, 0)
    position = position * span + flat_slot % span
    position = position.reshape(rows, width // segment).T.reshape(segments)

    steps = []
    for mask in far:
        near_w = jnp.concatenate([near_w, swap(near_w, "dp", mask)], axis=0)
        steps.append(near_w)
    others = [after(near_a, position)]
    for mask in reversed(mp_bits):
        others = others + [swap(b, "mp", mask) for b in others]
    all_a = jnp.concatenate([own_a] + others[1:], axis=1)

    line = jnp.arange(segments, dtype=jnp.int32)
    spot = after(position, steps[-1])
    place_map = (spot[:, None] == line[None, :]).astype(BF)
    back_map = (line[:, None] == spot[None, :]).astype(BF)

    blocks_w = [near_w]
    for mask in reversed(mp_bits):
        blocks_w = blocks_w + [swap(b, "mp", mask) for b in blocks_w]
    pairs_w = [(b, swap(b, "dp", 1)) for b in blocks_w]

    tensor = (rows, width)
    one = tokens_of(0, (activations, output_grads), steps[-2])
    half = segments // 2
    weights, parts, sent = [], [], []
    for w0, w1 in pairs_w:
        kernel = functools.partial(first_kernel, hidden_rows, up_scale, min(width, 1024))
        out = (shape(tensor, BF), shape(tensor, F32), shape(tensor, BF))
        w_t, part, part_sent = call(kernel, out, (place_map, w0, w1, *one))
        weights.append(w_t)
        parts.append(part)
        sent.append(part_sent)
    two = tokens_of(1, (activations, output_grads), sent[-1])

    for step, mask in enumerate(mp_bits):
        if step > 0:
            parts = [p + q.astype(F32) for p, q in zip(parts, got)]
            sent = [p.astype(BF) for p in parts]
        crossed = [swap(p, "mp", mask) for p in sent]
        got = [crossed[k ^ mask] for k in range(n_mp)]

    for mask, event in zip(far[:-1], [steps[-1]] * (len(far) - 2) + [sent[0]]):
        all_a = jnp.concatenate([all_a, after(swap(all_a, "dp", mask), event)], axis=0)
    ends = [0] + [(3 + 2 * k) * segment for k in range(n_mp)]
    blocks_a = [all_a[:, ends[k] : ends[k + 1]] for k in range(n_mp)]
    arrived = [None] * n_mp
    for k in reversed(range(n_mp)):
        arrived[k] = swap(blocks_a[k], "dp", far[-1])

    half = segments // 2
    kept, away, event = [None] * n_mp, [None] * n_mp, sent[-1]
    for k in reversed(range(n_mp)):
        own = k == 0
        block = jnp.concatenate([blocks_a[k], after(arrived[k], event)], axis=0)
        terms = [block[:, at : at + segment] for at in range(0, block.shape[1], segment)]
        terms += [swap(term, "dp", 1) for term in terms]
        moment_t, rate = call(
            functools.partial(moments_kernel, rows), (shape(tensor, F32), shape(tensor, F32)), (place_map, *terms)
        )
        operands = [back_map, parts[k], got[k], weights[k], moment_t, rate, *two]
        out = [shape((half, segment), BF)] * (4 if own else 2)
        if own:
            operands.append(feedback[0].reshape(tensor))
            out.append(shape(tensor, BF))
        result = call(
            functools.partial(second_kernel, hidden_rows, up_scale, own),
            tuple(out),
            operands,
            [pltpu.VMEM(tensor, BF), pltpu.VMEM((segments, segment), BF)],
        )
        kept[k], away[k] = result[:2]
        event = kept[k]
    packed = result[2].astype(F32) + swap(result[3], "dp", 1).astype(F32)
    error = result[4]

    for mask in mp_bits:
        away_got = [swap(p.astype(BF), "mp", mask) for p in away[mask:]]
        kept_got = [swap(p.astype(BF), "mp", mask) for p in kept[mask:]]
        away = [p.astype(F32) + q.astype(F32) for p, q in zip(away, away_got)]
        kept = [p.astype(F32) + q.astype(F32) for p, q in zip(kept, kept_got)]
    grad = kept[0] + swap(away[0].astype(BF), "dp", 1).astype(F32)

    def over_chips(total):
        for mask in far[::-1]:
            count = total.shape[0] // 2
            total = total[:count] + swap(total[count:].astype(BF), "dp", mask).astype(F32)
        return total

    own_packed = over_chips(packed)
    own_grad = over_chips(grad)
    mean_grad = own_grad / n_dp
    mean_moment = own_packed / n_dp
    moment_new = beta_one * mean_moment + (1.0 - beta_one) * mean_grad
    denominator = jnp.sqrt(variance[0]) + epsilon
    master_new = master[0] - step_rate * (mean_moment + moment_new) / denominator
    return (master_new[None], moment_new[None], error.reshape(feedback.shape))


def solution(mesh):
    in_specs = (
        P("mp", "dp", None),
        P("mp", "dp", None),
        P("mp", "dp", None),
        P(),
        P("dp", None, "mp", None),
        P(None, ("dp", "mp"), None),
        P(None, ("dp", "mp"), None),
    )
    out_specs = (P("mp", "dp", None), P("mp", "dp", None), P("dp", None, "mp", None))
    return jax.shard_map(
        per_device, mesh=mesh, in_specs=in_specs, out_specs=out_specs, check_vma=False
    )
```

```python
import functools

import jax
import jax.numpy as jnp
from jax import lax
from jax.experimental import pallas as pl
from jax.experimental.pallas import tpu as pltpu
from jax.sharding import PartitionSpec as P

beta_one = 0.9
step_rate = 0.05
epsilon = 1e-08
down_scale = 28672.0 ** (-0.5)
BF = jnp.bfloat16
F32 = jnp.float32
NT = (((1,), (1,)), ((), ()))
NN = (((1,), (0,)), ((), ()))


def dot(a, b, dims=NN):
    return lax.dot_general(a, b, dims, preferred_element_type=F32)


def swap(x, axis, mask):
    n = lax.axis_size(axis)
    return lax.ppermute(x, axis, [(i, i ^ mask) for i in range(n)])


def after(x, *others):
    return lax.optimization_barrier((x, *others))[0]


def bits_of(n, lowest=1):
    masks = []
    mask = n // 2
    while mask >= lowest:
        masks.append(mask)
        mask //= 2
    return masks


def gradient_rows(weights, x_ref, g_ref, hidden_rows, up_scale):
    before = up_scale * dot(weights, x_ref[...], NT)[:hidden_rows]
    back = down_scale * dot(weights, g_ref[...], NT)[hidden_rows:]
    sigmoid = jax.nn.sigmoid(before)
    hidden = before * sigmoid
    slope = back * (sigmoid * (1.0 + before * (1.0 - sigmoid)))
    zeros = jnp.zeros_like(slope)
    left_up = jnp.concatenate([slope, zeros], axis=0).astype(BF)
    left_down = jnp.concatenate([zeros, hidden], axis=0).astype(BF)

    def columns(at):
        return up_scale * dot(left_up, x_ref[:, at]) + down_scale * dot(left_down, g_ref[:, at])

    return columns


def first_kernel(hidden_rows, up_scale, chunk, place_ref, w0_ref, w1_ref, x_ref, g_ref, weights_ref, part_ref, sent_ref):
    rows = 2 * hidden_rows
    half, segment = w0_ref.shape
    width = x_ref.shape[1]
    ordered = dot(place_ref[:, :half], w0_ref[...]) + dot(place_ref[:, half:], w1_ref[...])
    for c in range(width // segment):
        weights_ref[:, c * segment : (c + 1) * segment] = ordered[c * rows : (c + 1) * rows].astype(BF)
    columns = gradient_rows(weights_ref[...], x_ref, g_ref, hidden_rows, up_scale)
    for c in range(width // chunk):
        at = slice(c * chunk, (c + 1) * chunk)
        part = columns(at)
        part_ref[:, at] = part
        sent_ref[:, at] = part.astype(BF)


def moments_kernel(rows, place_ref, *refs):
    terms, (moment_ref, rate_ref) = refs[:-2], refs[-2:]
    count = len(terms) // 2
    half, segment = terms[0].shape
    width = moment_ref.shape[1]
    near, far = place_ref[:, :half], place_ref[:, half:]
    ordered = [dot(near, a[...]) + dot(far, b[...]) for a, b in zip(terms[:count], terms[count:])]
    moment = sum(ordered[2:], ordered[0])
    rate = step_rate / (jnp.sqrt(ordered[1]) + epsilon)
    for c in range(width // segment):
        at = slice(c * segment, (c + 1) * segment)
        moment_ref[:, at] = moment[c * rows : (c + 1) * rows]
        rate_ref[:, at] = rate[c * rows : (c + 1) * rows]


def store_flat(back_ref, seg_ref, refs):
    flat = dot(back_ref[...], seg_ref[...]).astype(BF)
    count = flat.shape[0] // len(refs)
    for i, ref in enumerate(refs):
        ref[...] = flat[i * count : (i + 1) * count]


def second_kernel(
    hidden_rows, up_scale, own, back_ref, part_ref, got_ref, weights_ref, moment_ref, rate_ref, x_ref, g_ref, *rest
):
    if own:
        feedback_ref, *flat_refs, error_ref, local_ref, seg_ref = rest
    else:
        *flat_refs, local_ref, seg_ref = rest
    rows = 2 * hidden_rows
    segment = seg_ref.shape[1]
    width = x_ref.shape[1]
    step_one = part_ref[...] + got_ref[...].astype(F32)
    local_moment = beta_one * moment_ref[...] + (1.0 - beta_one) * step_one
    local_ref[...] = (weights_ref[...].astype(F32) - local_moment * rate_ref[...]).astype(BF)
    columns = gradient_rows(local_ref[...], x_ref, g_ref, hidden_rows, up_scale)
    for c in range(width // segment):
        seg_ref[c * rows : (c + 1) * rows] = columns(slice(c * segment, (c + 1) * segment)).astype(BF)
    store_flat(back_ref, seg_ref, flat_refs[:2] if own else flat_refs)
    if own:
        shifted = local_moment + feedback_ref[...].astype(F32)
        magnitude = jnp.sum(jnp.abs(shifted), axis=1, keepdims=True) * (1.0 / width) + 1e-06
        packed = magnitude * jnp.tanh(shifted / magnitude)
        error_ref[...] = (shifted - packed).astype(BF)
        for c in range(width // segment):
            seg_ref[c * rows : (c + 1) * rows] = packed[:, c * segment : (c + 1) * segment].astype(BF)
        store_flat(back_ref, seg_ref, flat_refs[2:])


def tokens_of(step, arrays, *others):
    return [x[step] for x in lax.optimization_barrier((*arrays, *others))[: len(arrays)]]


def call(kernel, out_shape, operands, scratch=()):
    return pl.pallas_call(
        kernel,
        out_shape=out_shape,
        in_specs=[pl.BlockSpec(memory_space=pltpu.VMEM)] * len(operands),
        out_specs=jax.tree.map(lambda _: pl.BlockSpec(memory_space=pltpu.VMEM), out_shape),
        scratch_shapes=list(scratch),
        cost_estimate=pl.CostEstimate(flops=1, bytes_accessed=1, transcendentals=0),
        compiler_params=pltpu.CompilerParams(vmem_limit_bytes=16 * 1024 * 1024),
    )(*operands)


def per_device(master, moment, variance, flat_slot, feedback, activations, output_grads):
    n_dp, n_mp = lax.axis_size("dp"), lax.axis_size("mp")
    me = lax.axis_index("dp")
    span, segment = master.shape[1:]
    segments = flat_slot.shape[0]
    hidden_rows, width = feedback.shape[2:]
    rows = 2 * hidden_rows
    up_scale = width ** (-0.5)
    far = bits_of(n_dp, 2)
    mp_bits = bits_of(n_mp)
    shape = jax.ShapeDtypeStruct

    near_w = master[0].astype(BF)
    spans = jnp.concatenate([after(moment[0], near_w), variance[0]], axis=1)
    near_a = spans.astype(BF)
    low = spans[:, :segment] - lax.reduce_precision(spans[:, :segment], 8, 7)
    steps = []
    for mask in far:
        near_w = jnp.concatenate([near_w, swap(near_w, "dp", mask)], axis=0)
        steps.append(near_w)
    blocks_a = [near_a]
    for mask in reversed(mp_bits):
        blocks_a = blocks_a + [swap(b, "mp", mask) for b in blocks_a]
    blocks_a[0] = jnp.concatenate([near_a, low.astype(BF)], axis=1)

    slot = after(flat_slot, steps[-1])
    owner = (slot // span) ^ me
    position = jnp.zeros_like(owner)
    for place, mask in enumerate(far + [1]):
        position = position + jnp.where((owner & mask) != 0, 1 << place, 0)
    position = position * span + slot % span
    position = position.reshape(rows, width // segment).T.reshape(segments)
    line = jnp.arange(segments, dtype=jnp.int32)
    place_map = (position[:, None] == line[None, :]).astype(BF)
    back_map = (line[:, None] == position[None, :]).astype(BF)

    blocks_w = [near_w]
    for mask in reversed(mp_bits):
        blocks_w = blocks_w + [swap(b, "mp", mask) for b in blocks_w]
    pairs_w = [(b, swap(b, "dp", 1)) for b in blocks_w]

    tensor = (rows, width)
    one = tokens_of(0, (activations, output_grads), steps[-2])
    half = segments // 2
    weights, parts, sent = [], [], []
    for w0, w1 in pairs_w:
        kernel = functools.partial(first_kernel, hidden_rows, up_scale, min(width, 1024))
        out = (shape(tensor, BF), shape(tensor, F32), shape(tensor, BF))
        w_t, part, part_sent = call(kernel, out, (place_map, w0, w1, *one))
        weights.append(w_t)
        parts.append(part)
        sent.append(part_sent)
    two = tokens_of(1, (activations, output_grads), sent[-1])

    for step, mask in enumerate(mp_bits):
        if step > 0:
            parts = [p + q.astype(F32) for p, q in zip(parts, got)]
            sent = [p.astype(BF) for p in parts]
        crossed = [swap(p, "mp", mask) for p in sent]
        got = [crossed[k ^ mask] for k in range(n_mp)]

    early = [one[0]] + [sent[0]] * (len(far) - 3)

    def stage(block, mask, event):
        return jnp.concatenate([block, after(swap(block, "dp", mask), event)], axis=0)

    for mask, event, late in zip(far[:-1], early + [sent[0]], early[1:] + [sent[0], sent[-1]]):
        blocks_a = [stage(b, mask, event if k else late) for k, b in enumerate(blocks_a)]

    half = segments // 2
    kept, away, event = [None] * n_mp, [None] * n_mp, sent[-1]
    for k in reversed(range(n_mp)):
        own = k == 0
        block = stage(blocks_a[k], far[-1], event)
        terms = [block[:, at : at + segment] for at in range(0, block.shape[1], segment)]
        terms += [swap(term, "dp", 1) for term in terms]
        moment_t, rate = call(
            functools.partial(moments_kernel, rows), (shape(tensor, F32), shape(tensor, F32)), (place_map, *terms)
        )
        operands = [back_map, parts[k], got[k], weights[k], moment_t, rate, *two]
        out = [shape((half, segment), BF)] * (4 if own else 2)
        if own:
            operands.append(feedback[0].reshape(tensor))
            out.append(shape(tensor, BF))
        result = call(
            functools.partial(second_kernel, hidden_rows, up_scale, own),
            tuple(out),
            operands,
            [pltpu.VMEM(tensor, BF), pltpu.VMEM((segments, segment), BF)],
        )
        kept[k], away[k] = result[:2]
        event = kept[k]
    packed = result[2].astype(F32) + swap(result[3], "dp", 1).astype(F32)
    error = result[4]

    for mask in mp_bits:
        away_got = [swap(p.astype(BF), "mp", mask) for p in away[mask:]]
        kept_got = [after(swap(p.astype(BF), "mp", mask), packed) for p in kept[mask:]]
        away = [p.astype(F32) + q.astype(F32) for p, q in zip(away, away_got)]
        kept = [p.astype(F32) + q.astype(F32) for p, q in zip(kept, kept_got)]
    grad = kept[0] + swap(away[0].astype(BF), "dp", 1).astype(F32)

    def halves(total, masks):
        for mask in masks:
            count = total.shape[0] // 2
            total = total[:count] + swap(total[count:].astype(BF), "dp", mask).astype(F32)
        return total

    packed, grad = halves(packed, far[:1:-1]), halves(grad, far[:1:-1])
    both = jnp.concatenate([grad, packed], axis=1)
    total = both[:span]
    for k, mask in ((3, far[0] | far[1]), (1, far[0]), (2, far[1])):
        total = total + swap(both[k * span : (k + 1) * span].astype(BF), "dp", mask).astype(F32)
    own_grad, own_packed = total[:, :segment], total[:, segment:]
    mean_grad = own_grad / n_dp
    mean_moment = own_packed / n_dp
    moment_new = beta_one * mean_moment + (1.0 - beta_one) * mean_grad
    denominator = jnp.sqrt(variance[0]) + epsilon
    master_new = master[0] - step_rate * (mean_moment + moment_new) / denominator
    return (master_new[None], moment_new[None], error.reshape(feedback.shape))


def solution(mesh):
    in_specs = (
        P("mp", "dp", None),
        P("mp", "dp", None),
        P("mp", "dp", None),
        P(),
        P("dp", None, "mp", None),
        P(None, ("dp", "mp"), None),
        P(None, ("dp", "mp"), None),
    )
    out_specs = (P("mp", "dp", None), P("mp", "dp", None), P("dp", None, "mp", None))
    return jax.shard_map(
        per_device, mesh=mesh, in_specs=in_specs, out_specs=out_specs, check_vma=False
    )
```

```python
import functools

import jax
import jax.numpy as jnp
from jax import lax
from jax.experimental import pallas as pl
from jax.experimental.pallas import tpu as pltpu
from jax.sharding import PartitionSpec as P

beta_one = 0.9
step_rate = 0.05
epsilon = 1e-08
down_scale = 28672.0 ** (-0.5)
BF = jnp.bfloat16
F32 = jnp.float32
NT = (((1,), (1,)), ((), ()))
NN = (((1,), (0,)), ((), ()))


def dot(a, b, dims=NN):
    return lax.dot_general(a, b, dims, preferred_element_type=F32)


def swap(x, axis, mask):
    n = lax.axis_size(axis)
    return lax.ppermute(x, axis, [(i, i ^ mask) for i in range(n)])


def after(x, *others):
    return lax.optimization_barrier((x, *others))[0]


def bits_of(n, lowest=1):
    masks = []
    mask = n // 2
    while mask >= lowest:
        masks.append(mask)
        mask //= 2
    return masks


def gradient_rows(weights, x_ref, g_ref, hidden_rows, up_scale):
    before = up_scale * dot(weights, x_ref[...], NT)[:hidden_rows]
    back = down_scale * dot(weights, g_ref[...], NT)[hidden_rows:]
    sigmoid = jax.nn.sigmoid(before)
    hidden = before * sigmoid
    slope = back * (sigmoid * (1.0 + before * (1.0 - sigmoid)))
    zeros = jnp.zeros_like(slope)
    left_up = jnp.concatenate([slope, zeros], axis=0).astype(BF)
    left_down = jnp.concatenate([zeros, hidden], axis=0).astype(BF)

    def columns(at):
        return up_scale * dot(left_up, x_ref[:, at]) + down_scale * dot(left_down, g_ref[:, at])

    return columns


def first_kernel(hidden_rows, up_scale, chunk, place_ref, w0_ref, w1_ref, x_ref, g_ref, weights_ref, part_ref, sent_ref):
    rows = 2 * hidden_rows
    half, segment = w0_ref.shape
    width = x_ref.shape[1]
    ordered = dot(place_ref[:, :half], w0_ref[...]) + dot(place_ref[:, half:], w1_ref[...])
    for c in range(width // segment):
        weights_ref[:, c * segment : (c + 1) * segment] = ordered[c * rows : (c + 1) * rows].astype(BF)
    columns = gradient_rows(weights_ref[...], x_ref, g_ref, hidden_rows, up_scale)
    for c in range(width // chunk):
        at = slice(c * chunk, (c + 1) * chunk)
        part = columns(at)
        part_ref[:, at] = part
        sent_ref[:, at] = part.astype(BF)


def moments_kernel(rows, place_ref, *refs):
    terms, (moment_ref, rate_ref) = refs[:-2], refs[-2:]
    count = len(terms) // 2
    half, segment = terms[0].shape
    width = moment_ref.shape[1]
    near, far = place_ref[:, :half], place_ref[:, half:]
    ordered = [dot(near, a[...]) + dot(far, b[...]) for a, b in zip(terms[:count], terms[count:])]
    moment = sum(ordered[2:], ordered[0])
    rate = step_rate / (jnp.sqrt(ordered[1]) + epsilon)
    for c in range(width // segment):
        at = slice(c * segment, (c + 1) * segment)
        moment_ref[:, at] = moment[c * rows : (c + 1) * rows]
        rate_ref[:, at] = rate[c * rows : (c + 1) * rows]


def store_flat(back_ref, seg_ref, refs):
    flat = dot(back_ref[...], seg_ref[...]).astype(BF)
    count = flat.shape[0] // len(refs)
    for i, ref in enumerate(refs):
        ref[...] = flat[i * count : (i + 1) * count]


def second_kernel(
    hidden_rows, up_scale, own, back_ref, part_ref, got_ref, weights_ref, moment_ref, rate_ref, x_ref, g_ref, *rest
):
    if own:
        feedback_ref, *flat_refs, error_ref, local_ref, seg_ref = rest
    else:
        *flat_refs, local_ref, seg_ref = rest
    rows = 2 * hidden_rows
    segment = seg_ref.shape[1]
    width = x_ref.shape[1]
    step_one = part_ref[...] + got_ref[...].astype(F32)
    local_moment = beta_one * moment_ref[...] + (1.0 - beta_one) * step_one
    local_ref[...] = (weights_ref[...].astype(F32) - local_moment * rate_ref[...]).astype(BF)
    columns = gradient_rows(local_ref[...], x_ref, g_ref, hidden_rows, up_scale)
    for c in range(width // segment):
        seg_ref[c * rows : (c + 1) * rows] = columns(slice(c * segment, (c + 1) * segment)).astype(BF)
    store_flat(back_ref, seg_ref, flat_refs[:2] if own else flat_refs)
    if own:
        shifted = local_moment + feedback_ref[...].astype(F32)
        magnitude = jnp.sum(jnp.abs(shifted), axis=1, keepdims=True) * (1.0 / width) + 1e-06
        packed = magnitude * jnp.tanh(shifted / magnitude)
        error_ref[...] = (shifted - packed).astype(BF)
        for c in range(width // segment):
            seg_ref[c * rows : (c + 1) * rows] = packed[:, c * segment : (c + 1) * segment].astype(BF)
        store_flat(back_ref, seg_ref, flat_refs[2:])


def tokens_of(step, arrays, *others):
    return [x[step] for x in lax.optimization_barrier((*arrays, *others))[: len(arrays)]]


def call(kernel, out_shape, operands, scratch=()):
    return pl.pallas_call(
        kernel,
        out_shape=out_shape,
        in_specs=[pl.BlockSpec(memory_space=pltpu.VMEM)] * len(operands),
        out_specs=jax.tree.map(lambda _: pl.BlockSpec(memory_space=pltpu.VMEM), out_shape),
        scratch_shapes=list(scratch),
        cost_estimate=pl.CostEstimate(flops=1, bytes_accessed=1, transcendentals=0),
        compiler_params=pltpu.CompilerParams(vmem_limit_bytes=16 * 1024 * 1024),
    )(*operands)


def per_device(master, moment, variance, flat_slot, feedback, activations, output_grads):
    n_dp, n_mp = lax.axis_size("dp"), lax.axis_size("mp")
    me = lax.axis_index("dp")
    span, segment = master.shape[1:]
    segments = flat_slot.shape[0]
    hidden_rows, width = feedback.shape[2:]
    rows = 2 * hidden_rows
    up_scale = width ** (-0.5)
    far = bits_of(n_dp, 2)
    mp_bits = bits_of(n_mp)
    shape = jax.ShapeDtypeStruct

    near_w = master[0].astype(BF)
    spans = jnp.concatenate([after(moment[0], near_w), variance[0]], axis=1)
    near_a = spans.astype(BF)
    low = (spans[:, :segment] - lax.reduce_precision(spans[:, :segment], 8, 7)).astype(BF)
    steps = []
    for mask in far:
        near_w = jnp.concatenate([near_w, swap(near_w, "dp", mask)], axis=0)
        steps.append(near_w)
    blocks_a = [near_a]
    for mask in reversed(mp_bits):
        blocks_a = blocks_a + [swap(b, "mp", mask) for b in blocks_a]
    blocks_a[0] = jnp.concatenate([near_a, low], axis=1)
    blocks_a = [after(b, steps[0]) for b in blocks_a]

    slot = after(flat_slot, steps[-1])
    owner = (slot // span) ^ me
    position = jnp.zeros_like(owner)
    for place, mask in enumerate(far + [1]):
        position = position + jnp.where((owner & mask) != 0, 1 << place, 0)
    position = position * span + slot % span
    position = position.reshape(rows, width // segment).T.reshape(segments)
    line = jnp.arange(segments, dtype=jnp.int32)
    place_map = (position[:, None] == line[None, :]).astype(BF)
    back_map = (line[:, None] == position[None, :]).astype(BF)

    blocks_w = [near_w]
    for mask in reversed(mp_bits):
        blocks_w = blocks_w + [swap(b, "mp", mask) for b in blocks_w]
    pairs_w = [(b, swap(b, "dp", 1)) for b in blocks_w]

    tensor = (rows, width)
    one = tokens_of(0, (activations, output_grads), steps[-2])
    half = segments // 2
    weights, parts, sent = [], [], []
    for w0, w1 in pairs_w:
        kernel = functools.partial(first_kernel, hidden_rows, up_scale, min(width, 1024))
        out = (shape(tensor, BF), shape(tensor, F32), shape(tensor, BF))
        w_t, part, part_sent = call(kernel, out, (place_map, w0, w1, *one))
        weights.append(w_t)
        parts.append(part)
        sent.append(part_sent)
    two = tokens_of(1, (activations, output_grads), sent[-1])

    for step, mask in enumerate(mp_bits):
        if step > 0:
            parts = [p + q.astype(F32) for p, q in zip(parts, got)]
            sent = [p.astype(BF) for p in parts]
        crossed = [swap(p, "mp", mask) for p in sent]
        got = [crossed[k ^ mask] for k in range(n_mp)]

    for mask, event in zip(far[:-1], [one[0]] + [sent[0]] * (len(far) - 2)):
        arrived = [after(swap(b, "dp", mask), event) for b in blocks_a]
        blocks_a = [jnp.concatenate(pair, axis=0) for pair in zip(blocks_a, arrived)]
    arrived = [swap(b, "dp", far[-1]) for b in blocks_a]

    half = segments // 2
    kept, away, event = [None] * n_mp, [None] * n_mp, sent[-1]
    for k in reversed(range(n_mp)):
        own = k == 0
        block = jnp.concatenate([blocks_a[k], after(arrived[k], event)], axis=0)
        terms = [block[:, at : at + segment] for at in range(0, block.shape[1], segment)]
        terms += [swap(term, "dp", 1) for term in terms]
        moment_t, rate = call(
            functools.partial(moments_kernel, rows), (shape(tensor, F32), shape(tensor, F32)), (place_map, *terms)
        )
        operands = [back_map, parts[k], got[k], weights[k], moment_t, rate, *two]
        out = [shape((half, segment), BF)] * (4 if own else 2)
        if own:
            operands.append(feedback[0].reshape(tensor))
            out.append(shape(tensor, BF))
        result = call(
            functools.partial(second_kernel, hidden_rows, up_scale, own),
            tuple(out),
            operands,
            [pltpu.VMEM(tensor, BF), pltpu.VMEM((segments, segment), BF)],
        )
        kept[k], away[k] = result[:2]
        event = kept[k]
    packed = result[2].astype(F32) + swap(result[3], "dp", 1).astype(F32)
    error = result[4]

    def halves(total, masks):
        for mask in masks:
            count = total.shape[0] // 2
            total = total[:count] + swap(total[count:].astype(BF), "dp", mask).astype(F32)
        return total

    for mask in mp_bits:
        away_got = [swap(p.astype(BF), "mp", mask) for p in away[mask:]]
        kept_got = [after(swap(p.astype(BF), "mp", mask), packed) for p in kept[mask:]]
        away = [p.astype(F32) + q.astype(F32) for p, q in zip(away, away_got)]
        kept = [p.astype(F32) + q.astype(F32) for p, q in zip(kept, kept_got)]
    grad = kept[0] + swap(away[0].astype(BF), "dp", 1).astype(F32)
    packed, grad = halves(packed, far[:-2:-1]), halves(grad, far[:-2:-1])
    both = halves(jnp.concatenate([grad, packed], axis=1), far[-2::-1])
    own_grad, own_packed = both[:, :segment], both[:, segment:]
    mean_grad = own_grad / n_dp
    mean_moment = own_packed / n_dp
    moment_new = beta_one * mean_moment + (1.0 - beta_one) * mean_grad
    denominator = jnp.sqrt(variance[0]) + epsilon
    master_new = master[0] - step_rate * (mean_moment + moment_new) / denominator
    return (master_new[None], moment_new[None], error.reshape(feedback.shape))


def solution(mesh):
    in_specs = (
        P("mp", "dp", None),
        P("mp", "dp", None),
        P("mp", "dp", None),
        P(),
        P("dp", None, "mp", None),
        P(None, ("dp", "mp"), None),
        P(None, ("dp", "mp"), None),
    )
    out_specs = (P("mp", "dp", None), P("mp", "dp", None), P("dp", None, "mp", None))
    return jax.shard_map(
        per_device, mesh=mesh, in_specs=in_specs, out_specs=out_specs, check_vma=False
    )
```

```python
import functools

import jax
import jax.numpy as jnp
from jax import lax
from jax.experimental import pallas as pl
from jax.experimental.pallas import tpu as pltpu
from jax.sharding import PartitionSpec as P

beta_one = 0.9
step_rate = 0.05
epsilon = 1e-08
down_scale = 28672.0 ** (-0.5)
BF = jnp.bfloat16
F32 = jnp.float32
NT = (((1,), (1,)), ((), ()))
NN = (((1,), (0,)), ((), ()))


def dot(a, b, dims=NN):
    return lax.dot_general(a, b, dims, preferred_element_type=F32)


def swap(x, axis, mask):
    n = lax.axis_size(axis)
    return lax.ppermute(x, axis, [(i, i ^ mask) for i in range(n)])


def after(x, *others):
    return lax.optimization_barrier((x, *others))[0]


def bits_of(n, lowest=1):
    masks = []
    mask = n // 2
    while mask >= lowest:
        masks.append(mask)
        mask //= 2
    return masks


def gradient_rows(weights, x_ref, g_ref, hidden_rows, up_scale):
    before = up_scale * dot(weights, x_ref[...], NT)[:hidden_rows]
    back = down_scale * dot(weights, g_ref[...], NT)[hidden_rows:]
    sigmoid = jax.nn.sigmoid(before)
    hidden = before * sigmoid
    slope = back * (sigmoid * (1.0 + before * (1.0 - sigmoid)))
    zeros = jnp.zeros_like(slope)
    left_up = jnp.concatenate([slope, zeros], axis=0).astype(BF)
    left_down = jnp.concatenate([zeros, hidden], axis=0).astype(BF)

    def columns(at):
        return up_scale * dot(left_up, x_ref[:, at]) + down_scale * dot(left_down, g_ref[:, at])

    return columns


def first_kernel(hidden_rows, up_scale, chunk, place_ref, w0_ref, w1_ref, x_ref, g_ref, weights_ref, part_ref, sent_ref):
    rows = 2 * hidden_rows
    half, segment = w0_ref.shape
    width = x_ref.shape[1]
    ordered = dot(place_ref[:, :half], w0_ref[...]) + dot(place_ref[:, half:], w1_ref[...])
    for c in range(width // segment):
        weights_ref[:, c * segment : (c + 1) * segment] = ordered[c * rows : (c + 1) * rows].astype(BF)
    columns = gradient_rows(weights_ref[...], x_ref, g_ref, hidden_rows, up_scale)
    for c in range(width // chunk):
        at = slice(c * chunk, (c + 1) * chunk)
        part = columns(at)
        part_ref[:, at] = part
        sent_ref[:, at] = part.astype(BF)


def moments_kernel(rows, place_ref, *refs):
    terms, (moment_ref, rate_ref) = refs[:-2], refs[-2:]
    count = len(terms) // 2
    half, segment = terms[0].shape
    width = moment_ref.shape[1]
    near, far = place_ref[:, :half], place_ref[:, half:]
    ordered = [dot(near, a[...]) + dot(far, b[...]) for a, b in zip(terms[:count], terms[count:])]
    moment = sum(ordered[2:], ordered[0])
    rate = step_rate / (jnp.sqrt(ordered[1]) + epsilon)
    for c in range(width // segment):
        at = slice(c * segment, (c + 1) * segment)
        moment_ref[:, at] = moment[c * rows : (c + 1) * rows]
        rate_ref[:, at] = rate[c * rows : (c + 1) * rows]


def store_flat(back_ref, seg_ref, refs):
    flat = dot(back_ref[...], seg_ref[...]).astype(BF)
    count = flat.shape[0] // len(refs)
    for i, ref in enumerate(refs):
        ref[...] = flat[i * count : (i + 1) * count]


def second_kernel(
    hidden_rows, up_scale, own, back_ref, part_ref, got_ref, weights_ref, moment_ref, rate_ref, x_ref, g_ref, *rest
):
    if own:
        feedback_ref, *flat_refs, error_ref, local_ref, seg_ref = rest
    else:
        *flat_refs, local_ref, seg_ref = rest
    rows = 2 * hidden_rows
    segment = seg_ref.shape[1]
    width = x_ref.shape[1]
    step_one = part_ref[...] + got_ref[...].astype(F32)
    local_moment = beta_one * moment_ref[...] + (1.0 - beta_one) * step_one
    local_ref[...] = (weights_ref[...].astype(F32) - local_moment * rate_ref[...]).astype(BF)
    columns = gradient_rows(local_ref[...], x_ref, g_ref, hidden_rows, up_scale)
    for c in range(width // segment):
        seg_ref[c * rows : (c + 1) * rows] = columns(slice(c * segment, (c + 1) * segment)).astype(BF)
    store_flat(back_ref, seg_ref, flat_refs[:2] if own else flat_refs)
    if own:
        shifted = local_moment + feedback_ref[...].astype(F32)
        magnitude = jnp.sum(jnp.abs(shifted), axis=1, keepdims=True) * (1.0 / width) + 1e-06
        packed = magnitude * jnp.tanh(shifted / magnitude)
        error_ref[...] = (shifted - packed).astype(BF)
        for c in range(width // segment):
            seg_ref[c * rows : (c + 1) * rows] = packed[:, c * segment : (c + 1) * segment].astype(BF)
        store_flat(back_ref, seg_ref, flat_refs[2:])


def tokens_of(step, arrays, *others):
    return [x[step] for x in lax.optimization_barrier((*arrays, *others))[: len(arrays)]]


def call(kernel, out_shape, operands, scratch=()):
    return pl.pallas_call(
        kernel,
        out_shape=out_shape,
        in_specs=[pl.BlockSpec(memory_space=pltpu.VMEM)] * len(operands),
        out_specs=jax.tree.map(lambda _: pl.BlockSpec(memory_space=pltpu.VMEM), out_shape),
        scratch_shapes=list(scratch),
        cost_estimate=pl.CostEstimate(flops=1, bytes_accessed=1, transcendentals=0),
        compiler_params=pltpu.CompilerParams(vmem_limit_bytes=16 * 1024 * 1024),
    )(*operands)


def per_device(master, moment, variance, flat_slot, feedback, activations, output_grads):
    n_dp, n_mp = lax.axis_size("dp"), lax.axis_size("mp")
    me = lax.axis_index("dp")
    span, segment = master.shape[1:]
    segments = flat_slot.shape[0]
    hidden_rows, width = feedback.shape[2:]
    rows = 2 * hidden_rows
    up_scale = width ** (-0.5)
    far = bits_of(n_dp, 2)
    mp_bits = bits_of(n_mp)
    shape = jax.ShapeDtypeStruct

    near_w = master[0].astype(BF)
    spans = jnp.concatenate([after(moment[0], near_w), variance[0]], axis=1)
    near_a = spans.astype(BF)
    low = (spans[:, :segment] - lax.reduce_precision(spans[:, :segment], 8, 7)).astype(BF)
    steps = []
    for mask in far:
        near_w = jnp.concatenate([near_w, swap(near_w, "dp", mask)], axis=0)
        steps.append(near_w)
    blocks_a = [near_a]
    for mask in reversed(mp_bits):
        blocks_a = blocks_a + [swap(b, "mp", mask) for b in blocks_a]
    all_a = after(jnp.concatenate([near_a, low] + blocks_a[1:], axis=1), steps[0])

    slot = after(flat_slot, steps[-1])
    owner = (slot // span) ^ me
    position = jnp.zeros_like(owner)
    for place, mask in enumerate(far + [1]):
        position = position + jnp.where((owner & mask) != 0, 1 << place, 0)
    position = position * span + slot % span
    position = position.reshape(rows, width // segment).T.reshape(segments)
    line = jnp.arange(segments, dtype=jnp.int32)
    place_map = (position[:, None] == line[None, :]).astype(BF)
    back_map = (line[:, None] == position[None, :]).astype(BF)

    blocks_w = [near_w]
    for mask in reversed(mp_bits):
        blocks_w = blocks_w + [swap(b, "mp", mask) for b in blocks_w]
    pairs_w = [(b, swap(b, "dp", 1)) for b in blocks_w]

    tensor = (rows, width)
    one = tokens_of(0, (activations, output_grads), steps[-2])
    half = segments // 2
    weights, parts, sent = [], [], []
    for w0, w1 in pairs_w:
        kernel = functools.partial(first_kernel, hidden_rows, up_scale, min(width, 1024))
        out = (shape(tensor, BF), shape(tensor, F32), shape(tensor, BF))
        w_t, part, part_sent = call(kernel, out, (place_map, w0, w1, *one))
        weights.append(w_t)
        parts.append(part)
        sent.append(part_sent)
    two = tokens_of(1, (activations, output_grads), sent[-1])

    for step, mask in enumerate(mp_bits):
        if step > 0:
            parts = [p + q.astype(F32) for p, q in zip(parts, got)]
            sent = [p.astype(BF) for p in parts]
        crossed = [swap(p, "mp", mask) for p in sent]
        got = [crossed[k ^ mask] for k in range(n_mp)]

    for mask in far[:-2]:
        all_a = jnp.concatenate([all_a, after(swap(all_a, "dp", mask), steps[-1])], axis=0)
    ends = [0] + [(3 + 2 * k) * segment for k in range(n_mp)]
    blocks_a = [all_a[:, ends[k] : ends[k + 1]] for k in range(n_mp)]
    arrived = [after(swap(b, "dp", far[-2]), sent[0]) for b in blocks_a]
    blocks_a = [jnp.concatenate(pair, axis=0) for pair in zip(blocks_a, arrived)]
    arrived = [swap(b, "dp", far[-1]) for b in blocks_a]

    half = segments // 2
    kept, away, event = [None] * n_mp, [None] * n_mp, sent[-1]
    for k in reversed(range(n_mp)):
        own = k == 0
        block = jnp.concatenate([blocks_a[k], after(arrived[k], event)], axis=0)
        terms = [block[:, at : at + segment] for at in range(0, block.shape[1], segment)]
        terms += [swap(term, "dp", 1) for term in terms]
        moment_t, rate = call(
            functools.partial(moments_kernel, rows), (shape(tensor, F32), shape(tensor, F32)), (place_map, *terms)
        )
        operands = [back_map, parts[k], got[k], weights[k], moment_t, rate, *two]
        out = [shape((half, segment), BF)] * (4 if own else 2)
        if own:
            operands.append(feedback[0].reshape(tensor))
            out.append(shape(tensor, BF))
        result = call(
            functools.partial(second_kernel, hidden_rows, up_scale, own),
            tuple(out),
            operands,
            [pltpu.VMEM(tensor, BF), pltpu.VMEM((segments, segment), BF)],
        )
        kept[k], away[k] = result[:2]
        event = kept[k]
    packed = result[2].astype(F32) + swap(result[3], "dp", 1).astype(F32)
    error = result[4]

    def halves(total, masks):
        for mask in masks:
            count = total.shape[0] // 2
            total = total[:count] + swap(total[count:].astype(BF), "dp", mask).astype(F32)
        return total

    for mask in mp_bits:
        away_got = [swap(p.astype(BF), "mp", mask) for p in away[mask:]]
        kept_got = [after(swap(p.astype(BF), "mp", mask), packed) for p in kept[mask:]]
        away = [p.astype(F32) + q.astype(F32) for p, q in zip(away, away_got)]
        kept = [p.astype(F32) + q.astype(F32) for p, q in zip(kept, kept_got)]
    grad = kept[0] + swap(away[0].astype(BF), "dp", 1).astype(F32)
    packed, grad = halves(packed, far[:-2:-1]), halves(grad, far[:-2:-1])
    both = halves(jnp.concatenate([grad, packed], axis=1), far[-2::-1])
    own_grad, own_packed = both[:, :segment], both[:, segment:]
    mean_grad = own_grad / n_dp
    mean_moment = own_packed / n_dp
    moment_new = beta_one * mean_moment + (1.0 - beta_one) * mean_grad
    denominator = jnp.sqrt(variance[0]) + epsilon
    master_new = master[0] - step_rate * (mean_moment + moment_new) / denominator
    return (master_new[None], moment_new[None], error.reshape(feedback.shape))


def solution(mesh):
    in_specs = (
        P("mp", "dp", None),
        P("mp", "dp", None),
        P("mp", "dp", None),
        P(),
        P("dp", None, "mp", None),
        P(None, ("dp", "mp"), None),
        P(None, ("dp", "mp"), None),
    )
    out_specs = (P("mp", "dp", None), P("mp", "dp", None), P("dp", None, "mp", None))
    return jax.shard_map(
        per_device, mesh=mesh, in_specs=in_specs, out_specs=out_specs, check_vma=False
    )
```

```python
import functools

import jax
import jax.numpy as jnp
from jax import lax
from jax.experimental import pallas as pl
from jax.experimental.pallas import tpu as pltpu
from jax.sharding import PartitionSpec as P

beta_one = 0.9
step_rate = 0.05
epsilon = 1e-08
down_scale = 28672.0 ** (-0.5)
BF = jnp.bfloat16
F32 = jnp.float32
NT = (((1,), (1,)), ((), ()))
NN = (((1,), (0,)), ((), ()))


def dot(a, b, dims=NN):
    return lax.dot_general(a, b, dims, preferred_element_type=F32)


def swap(x, axis, mask):
    n = lax.axis_size(axis)
    return lax.ppermute(x, axis, [(i, i ^ mask) for i in range(n)])


def after(x, *others):
    return lax.optimization_barrier((x, *others))[0]


def bits_of(n, lowest=1):
    masks = []
    mask = n // 2
    while mask >= lowest:
        masks.append(mask)
        mask //= 2
    return masks


def gradient_rows(weights, x_ref, g_ref, hidden_rows, up_scale):
    before = up_scale * dot(weights, x_ref[...], NT)[:hidden_rows]
    back = down_scale * dot(weights, g_ref[...], NT)[hidden_rows:]
    sigmoid = jax.nn.sigmoid(before)
    hidden = before * sigmoid
    slope = back * (sigmoid * (1.0 + before * (1.0 - sigmoid)))
    zeros = jnp.zeros_like(slope)
    left_up = jnp.concatenate([slope, zeros], axis=0).astype(BF)
    left_down = jnp.concatenate([zeros, hidden], axis=0).astype(BF)

    def columns(at):
        return up_scale * dot(left_up, x_ref[:, at]) + down_scale * dot(left_down, g_ref[:, at])

    return columns


def first_kernel(hidden_rows, up_scale, chunk, place_ref, w0_ref, w1_ref, x_ref, g_ref, weights_ref, part_ref, sent_ref):
    rows = 2 * hidden_rows
    half, segment = w0_ref.shape
    width = x_ref.shape[1]
    ordered = dot(place_ref[:, :half], w0_ref[...]) + dot(place_ref[:, half:], w1_ref[...])
    for c in range(width // segment):
        weights_ref[:, c * segment : (c + 1) * segment] = ordered[c * rows : (c + 1) * rows].astype(BF)
    columns = gradient_rows(weights_ref[...], x_ref, g_ref, hidden_rows, up_scale)
    for c in range(width // chunk):
        at = slice(c * chunk, (c + 1) * chunk)
        part = columns(at)
        part_ref[:, at] = part
        sent_ref[:, at] = part.astype(BF)


def moments_kernel(rows, place_ref, *refs):
    terms, (moment_ref, rate_ref) = refs[:-2], refs[-2:]
    count = len(terms) // 2
    half, segment = terms[0].shape
    width = moment_ref.shape[1]
    near, far = place_ref[:, :half], place_ref[:, half:]
    ordered = [dot(near, a[...]) + dot(far, b[...]) for a, b in zip(terms[:count], terms[count:])]
    moment = sum(ordered[2:], ordered[0])
    rate = step_rate / (jnp.sqrt(ordered[1]) + epsilon)
    for c in range(width // segment):
        at = slice(c * segment, (c + 1) * segment)
        moment_ref[:, at] = moment[c * rows : (c + 1) * rows]
        rate_ref[:, at] = rate[c * rows : (c + 1) * rows]


def store_flat(back_ref, seg_ref, kept_ref, away_ref, lanes):
    flat = dot(back_ref[...], seg_ref[...]).astype(BF)
    half = kept_ref.shape[0]
    kept_ref[:, lanes] = flat[:half]
    away_ref[:, lanes] = flat[half:]


def second_kernel(
    hidden_rows, up_scale, own, back_ref, part_ref, got_ref, weights_ref, moment_ref, rate_ref, x_ref, g_ref, *rest
):
    if own:
        feedback_ref, kept_ref, away_ref, error_ref, local_ref, seg_ref = rest
    else:
        kept_ref, away_ref, local_ref, seg_ref = rest
    rows = 2 * hidden_rows
    segment = seg_ref.shape[1]
    width = x_ref.shape[1]
    step_one = part_ref[...] + got_ref[...].astype(F32)
    local_moment = beta_one * moment_ref[...] + (1.0 - beta_one) * step_one
    local_ref[...] = (weights_ref[...].astype(F32) - local_moment * rate_ref[...]).astype(BF)
    columns = gradient_rows(local_ref[...], x_ref, g_ref, hidden_rows, up_scale)
    for c in range(width // segment):
        seg_ref[c * rows : (c + 1) * rows] = columns(slice(c * segment, (c + 1) * segment)).astype(BF)
    store_flat(back_ref, seg_ref, kept_ref, away_ref, slice(0, segment))
    if own:
        shifted = local_moment + feedback_ref[...].astype(F32)
        magnitude = jnp.sum(jnp.abs(shifted), axis=1, keepdims=True) * (1.0 / width) + 1e-06
        packed = magnitude * jnp.tanh(shifted / magnitude)
        error_ref[...] = (shifted - packed).astype(BF)
        for c in range(width // segment):
            seg_ref[c * rows : (c + 1) * rows] = packed[:, c * segment : (c + 1) * segment].astype(BF)
        store_flat(back_ref, seg_ref, kept_ref, away_ref, slice(segment, 2 * segment))


def tokens_of(step, arrays, *others):
    return [x[step] for x in lax.optimization_barrier((*arrays, *others))[: len(arrays)]]


def call(kernel, out_shape, operands, scratch=()):
    return pl.pallas_call(
        kernel,
        out_shape=out_shape,
        in_specs=[pl.BlockSpec(memory_space=pltpu.VMEM)] * len(operands),
        out_specs=jax.tree.map(lambda _: pl.BlockSpec(memory_space=pltpu.VMEM), out_shape),
        scratch_shapes=list(scratch),
        cost_estimate=pl.CostEstimate(flops=1, bytes_accessed=1, transcendentals=0),
        compiler_params=pltpu.CompilerParams(vmem_limit_bytes=16 * 1024 * 1024),
    )(*operands)


def per_device(master, moment, variance, flat_slot, feedback, activations, output_grads):
    n_dp, n_mp = lax.axis_size("dp"), lax.axis_size("mp")
    me = lax.axis_index("dp")
    span, segment = master.shape[1:]
    segments = flat_slot.shape[0]
    hidden_rows, width = feedback.shape[2:]
    rows = 2 * hidden_rows
    up_scale = width ** (-0.5)
    far = bits_of(n_dp, 2)
    mp_bits = bits_of(n_mp)
    shape = jax.ShapeDtypeStruct

    near_w = master[0].astype(BF)
    spans = jnp.concatenate([after(moment[0], near_w), variance[0]], axis=1)
    near_a = spans.astype(BF)
    low = (spans[:, :segment] - lax.reduce_precision(spans[:, :segment], 8, 7)).astype(BF)
    steps = []
    for mask in far:
        near_w = jnp.concatenate([near_w, swap(near_w, "dp", mask)], axis=0)
        steps.append(near_w)
    blocks_a = [near_a]
    for mask in reversed(mp_bits):
        blocks_a = blocks_a + [swap(b, "mp", mask) for b in blocks_a]
    all_a = after(jnp.concatenate([near_a, low] + blocks_a[1:], axis=1), steps[0])

    slot = after(flat_slot, steps[-1])
    owner = (slot // span) ^ me
    position = jnp.zeros_like(owner)
    for place, mask in enumerate(far + [1]):
        position = position + jnp.where((owner & mask) != 0, 1 << place, 0)
    position = position * span + slot % span
    position = position.reshape(rows, width // segment).T.reshape(segments)
    line = jnp.arange(segments, dtype=jnp.int32)
    place_map = (position[:, None] == line[None, :]).astype(BF)
    back_map = (line[:, None] == position[None, :]).astype(BF)

    blocks_w = [near_w]
    for mask in reversed(mp_bits):
        blocks_w = blocks_w + [swap(b, "mp", mask) for b in blocks_w]
    pairs_w = [(b, swap(b, "dp", 1)) for b in blocks_w]

    tensor = (rows, width)
    one = tokens_of(0, (activations, output_grads), steps[-2])
    half = segments // 2
    weights, parts, sent = [], [], []
    for w0, w1 in pairs_w:
        kernel = functools.partial(first_kernel, hidden_rows, up_scale, min(width, 1024))
        out = (shape(tensor, BF), shape(tensor, F32), shape(tensor, BF))
        w_t, part, part_sent = call(kernel, out, (place_map, w0, w1, *one))
        weights.append(w_t)
        parts.append(part)
        sent.append(part_sent)
    two = tokens_of(1, (activations, output_grads), sent[-1])

    for step, mask in enumerate(mp_bits):
        if step > 0:
            parts = [p + q.astype(F32) for p, q in zip(parts, got)]
            sent = [p.astype(BF) for p in parts]
        crossed = [swap(p, "mp", mask) for p in sent]
        got = [crossed[k ^ mask] for k in range(n_mp)]

    for mask in far[:-2]:
        all_a = jnp.concatenate([all_a, after(swap(all_a, "dp", mask), steps[-1])], axis=0)
    ends = [0] + [(3 + 2 * k) * segment for k in range(n_mp)]
    blocks_a = [all_a[:, ends[k] : ends[k + 1]] for k in range(n_mp)]
    arrived = [after(swap(b, "dp", far[-2]), sent[0]) for b in blocks_a]
    blocks_a = [jnp.concatenate(pair, axis=0) for pair in zip(blocks_a, arrived)]
    arrived = [swap(b, "dp", far[-1]) for b in blocks_a]

    half = segments // 2
    sums, event = [None] * n_mp, sent[-1]
    for k in reversed(range(n_mp)):
        own = k == 0
        block = jnp.concatenate([blocks_a[k], after(arrived[k], event)], axis=0)
        terms = [block[:, at : at + segment] for at in range(0, block.shape[1], segment)]
        terms += [swap(term, "dp", 1) for term in terms]
        moment_t, rate = call(
            functools.partial(moments_kernel, rows), (shape(tensor, F32), shape(tensor, F32)), (place_map, *terms)
        )
        operands = [back_map, parts[k], got[k], weights[k], moment_t, rate, *two]
        out = [shape((half, (2 if own else 1) * segment), BF)] * 2
        if own:
            operands.append(feedback[0].reshape(tensor))
            out.append(shape(tensor, BF))
        result = call(
            functools.partial(second_kernel, hidden_rows, up_scale, own),
            tuple(out),
            operands,
            [pltpu.VMEM(tensor, BF), pltpu.VMEM((segments, segment), BF)],
        )
        event = result[0]
        sums[k] = result[0].astype(F32) + swap(result[1], "dp", 1).astype(F32)
    error = result[2]

    for mask in far[::-1]:
        count = sums[0].shape[0] // 2
        sums = [p[:count] + swap(p[count:].astype(BF), "dp", mask).astype(F32) for p in sums]
    own_grad, own_packed = sums[0][:, :segment], sums[0][:, segment:]
    grads = [own_grad] + sums[1:]
    for mask in mp_bits:
        crossed = [swap(p.astype(BF), "mp", mask).astype(F32) for p in grads[mask:]]
        grads = [p + q for p, q in zip(grads, crossed)]
    own_grad = grads[0]
    mean_grad = own_grad / n_dp
    mean_moment = own_packed / n_dp
    moment_new = beta_one * mean_moment + (1.0 - beta_one) * mean_grad
    denominator = jnp.sqrt(variance[0]) + epsilon
    master_new = master[0] - step_rate * (mean_moment + moment_new) / denominator
    return (master_new[None], moment_new[None], error.reshape(feedback.shape))


def solution(mesh):
    in_specs = (
        P("mp", "dp", None),
        P("mp", "dp", None),
        P("mp", "dp", None),
        P(),
        P("dp", None, "mp", None),
        P(None, ("dp", "mp"), None),
        P(None, ("dp", "mp"), None),
    )
    out_specs = (P("mp", "dp", None), P("mp", "dp", None), P("dp", None, "mp", None))
    return jax.shard_map(
        per_device, mesh=mesh, in_specs=in_specs, out_specs=out_specs, check_vma=False
    )
```

```python
import functools

import jax
import jax.numpy as jnp
from jax import lax
from jax.experimental import pallas as pl
from jax.experimental.pallas import tpu as pltpu
from jax.sharding import PartitionSpec as P

beta_one = 0.9
step_rate = 0.05
epsilon = 1e-08
down_scale = 28672.0 ** (-0.5)
BF = jnp.bfloat16
F32 = jnp.float32
NT = (((1,), (1,)), ((), ()))
NN = (((1,), (0,)), ((), ()))


def dot(a, b, dims=NN):
    return lax.dot_general(a, b, dims, preferred_element_type=F32)


def swap(x, axis, mask):
    n = lax.axis_size(axis)
    return lax.ppermute(x, axis, [(i, i ^ mask) for i in range(n)])


def after(x, *others):
    return lax.optimization_barrier((x, *others))[0]


def bits_of(n, lowest=1):
    masks = []
    mask = n // 2
    while mask >= lowest:
        masks.append(mask)
        mask //= 2
    return masks


def gradient_rows(weights, x_ref, g_ref, hidden_rows, up_scale):
    before = up_scale * dot(weights, x_ref[...], NT)[:hidden_rows]
    back = down_scale * dot(weights, g_ref[...], NT)[hidden_rows:]
    sigmoid = jax.nn.sigmoid(before)
    hidden = before * sigmoid
    slope = back * (sigmoid * (1.0 + before * (1.0 - sigmoid)))
    zeros = jnp.zeros_like(slope)
    left_up = jnp.concatenate([slope, zeros], axis=0).astype(BF)
    left_down = jnp.concatenate([zeros, hidden], axis=0).astype(BF)

    def columns(at):
        return up_scale * dot(left_up, x_ref[:, at]) + down_scale * dot(left_down, g_ref[:, at])

    return columns


def first_kernel(hidden_rows, up_scale, chunk, place_ref, w0_ref, w1_ref, x_ref, g_ref, weights_ref, part_ref, sent_ref):
    rows = 2 * hidden_rows
    half, segment = w0_ref.shape
    width = x_ref.shape[1]
    ordered = dot(place_ref[:, :half], w0_ref[...]) + dot(place_ref[:, half:], w1_ref[...])
    for c in range(width // segment):
        weights_ref[:, c * segment : (c + 1) * segment] = ordered[c * rows : (c + 1) * rows].astype(BF)
    columns = gradient_rows(weights_ref[...], x_ref, g_ref, hidden_rows, up_scale)
    for c in range(width // chunk):
        at = slice(c * chunk, (c + 1) * chunk)
        part = columns(at)
        part_ref[:, at] = part
        sent_ref[:, at] = part.astype(BF)


def moments_kernel(rows, place_ref, *refs):
    terms, (moment_ref, rate_ref) = refs[:-2], refs[-2:]
    count = len(terms) // 2
    half, segment = terms[0].shape
    width = moment_ref.shape[1]
    near, far = place_ref[:, :half], place_ref[:, half:]
    ordered = [dot(near, a[...]) + dot(far, b[...]) for a, b in zip(terms[:count], terms[count:])]
    moment = sum(ordered[2:], ordered[0])
    rate = step_rate / (jnp.sqrt(ordered[1]) + epsilon)
    for c in range(width // segment):
        at = slice(c * segment, (c + 1) * segment)
        moment_ref[:, at] = moment[c * rows : (c + 1) * rows]
        rate_ref[:, at] = rate[c * rows : (c + 1) * rows]


def store_flat(back_ref, seg_ref, kept_ref, away_ref, lanes):
    flat = dot(back_ref[...], seg_ref[...]).astype(BF)
    half = kept_ref.shape[0]
    kept_ref[:, lanes] = flat[:half]
    away_ref[:, lanes] = flat[half:]


def second_kernel(
    hidden_rows, up_scale, own, back_ref, part_ref, got_ref, weights_ref, moment_ref, rate_ref, x_ref, g_ref, *rest
):
    if own:
        feedback_ref, kept_ref, away_ref, error_ref, local_ref, seg_ref = rest
    else:
        kept_ref, away_ref, local_ref, seg_ref = rest
    rows = 2 * hidden_rows
    segment = seg_ref.shape[1]
    width = x_ref.shape[1]
    step_one = part_ref[...] + got_ref[...].astype(F32)
    local_moment = beta_one * moment_ref[...] + (1.0 - beta_one) * step_one
    local_ref[...] = (weights_ref[...].astype(F32) - local_moment * rate_ref[...]).astype(BF)
    columns = gradient_rows(local_ref[...], x_ref, g_ref, hidden_rows, up_scale)
    for c in range(width // segment):
        seg_ref[c * rows : (c + 1) * rows] = columns(slice(c * segment, (c + 1) * segment)).astype(BF)
    store_flat(back_ref, seg_ref, kept_ref, away_ref, slice(0, segment))
    if own:
        shifted = local_moment + feedback_ref[...].astype(F32)
        magnitude = jnp.sum(jnp.abs(shifted), axis=1, keepdims=True) * (1.0 / width) + 1e-06
        packed = magnitude * jnp.tanh(shifted / magnitude)
        error_ref[...] = (shifted - packed).astype(BF)
        for c in range(width // segment):
            seg_ref[c * rows : (c + 1) * rows] = packed[:, c * segment : (c + 1) * segment].astype(BF)
        store_flat(back_ref, seg_ref, kept_ref, away_ref, slice(segment, 2 * segment))


def tokens_of(step, arrays, *others):
    return [x[step] for x in lax.optimization_barrier((*arrays, *others))[: len(arrays)]]


def call(kernel, out_shape, operands, scratch=()):
    return pl.pallas_call(
        kernel,
        out_shape=out_shape,
        in_specs=[pl.BlockSpec(memory_space=pltpu.VMEM)] * len(operands),
        out_specs=jax.tree.map(lambda _: pl.BlockSpec(memory_space=pltpu.VMEM), out_shape),
        scratch_shapes=list(scratch),
        cost_estimate=pl.CostEstimate(flops=1, bytes_accessed=1, transcendentals=0),
        compiler_params=pltpu.CompilerParams(vmem_limit_bytes=16 * 1024 * 1024),
    )(*operands)


def per_device(master, moment, variance, flat_slot, feedback, activations, output_grads):
    n_dp, n_mp = lax.axis_size("dp"), lax.axis_size("mp")
    me = lax.axis_index("dp")
    span, segment = master.shape[1:]
    segments = flat_slot.shape[0]
    hidden_rows, width = feedback.shape[2:]
    rows = 2 * hidden_rows
    up_scale = width ** (-0.5)
    far = bits_of(n_dp, 2)
    mp_bits = bits_of(n_mp)
    shape = jax.ShapeDtypeStruct

    near_w = master[0].astype(BF)
    spans = jnp.concatenate([after(moment[0], near_w), variance[0]], axis=1)
    near_a = spans.astype(BF)
    low = (spans[:, :segment] - lax.reduce_precision(spans[:, :segment], 8, 7)).astype(BF)
    steps = []
    for mask in far:
        near_w = jnp.concatenate([near_w, swap(near_w, "dp", mask)], axis=0)
        steps.append(near_w)
    blocks_a = [near_a]
    for mask in reversed(mp_bits):
        blocks_a = blocks_a + [swap(b, "mp", mask) for b in blocks_a]
    all_a = after(jnp.concatenate([near_a, low] + blocks_a[1:], axis=1), steps[0])

    slot = after(flat_slot, steps[-1])
    owner = (slot // span) ^ me
    position = jnp.zeros_like(owner)
    for place, mask in enumerate(far + [1]):
        position = position + jnp.where((owner & mask) != 0, 1 << place, 0)
    position = position * span + slot % span
    position = position.reshape(rows, width // segment).T.reshape(segments)
    line = jnp.arange(segments, dtype=jnp.int32)
    place_map = (position[:, None] == line[None, :]).astype(BF)
    back_map = (line[:, None] == position[None, :]).astype(BF)

    blocks_w = [near_w]
    for mask in reversed(mp_bits):
        blocks_w = blocks_w + [swap(b, "mp", mask) for b in blocks_w]
    pairs_w = [(b, swap(b, "dp", 1)) for b in blocks_w]

    tensor = (rows, width)
    one = tokens_of(0, (activations, output_grads), steps[-2])
    half = segments // 2
    weights, parts, sent = [], [], []
    for w0, w1 in pairs_w:
        kernel = functools.partial(first_kernel, hidden_rows, up_scale, min(width, 1024))
        out = (shape(tensor, BF), shape(tensor, F32), shape(tensor, BF))
        w_t, part, part_sent = call(kernel, out, (place_map, w0, w1, *one))
        weights.append(w_t)
        parts.append(part)
        sent.append(part_sent)
    two = tokens_of(1, (activations, output_grads), sent[-1])

    for step, mask in enumerate(mp_bits):
        if step > 0:
            parts = [p + q.astype(F32) for p, q in zip(parts, got)]
            sent = [p.astype(BF) for p in parts]
        crossed = [swap(p, "mp", mask) for p in sent]
        got = [crossed[k ^ mask] for k in range(n_mp)]

    for mask in far[:-2]:
        all_a = jnp.concatenate([all_a, after(swap(all_a, "dp", mask), steps[-1])], axis=0)
    ends = [0] + [(3 + 2 * k) * segment for k in range(n_mp)]
    blocks_a = [all_a[:, ends[k] : ends[k + 1]] for k in range(n_mp)]
    blocks_a[0] = after(blocks_a[0], sent[0])
    arrived = [after(swap(b, "dp", far[-2]), sent[0] if k else sent[-1]) for k, b in enumerate(blocks_a)]
    blocks_a = [jnp.concatenate(pair, axis=0) for pair in zip(blocks_a, arrived)]
    arrived = [swap(b, "dp", far[-1]) for b in blocks_a]

    half = segments // 2
    sums, event = [None] * n_mp, sent[-1]
    for k in reversed(range(n_mp)):
        own = k == 0
        block = jnp.concatenate([blocks_a[k], after(arrived[k], event)], axis=0)
        terms = [block[:, at : at + segment] for at in range(0, block.shape[1], segment)]
        terms += [swap(term, "dp", 1) for term in terms]
        moment_t, rate = call(
            functools.partial(moments_kernel, rows), (shape(tensor, F32), shape(tensor, F32)), (place_map, *terms)
        )
        operands = [back_map, parts[k], got[k], weights[k], moment_t, rate, *two]
        out = [shape((half, (2 if own else 1) * segment), BF)] * 2
        if own:
            operands.append(feedback[0].reshape(tensor))
            out.append(shape(tensor, BF))
        result = call(
            functools.partial(second_kernel, hidden_rows, up_scale, own),
            tuple(out),
            operands,
            [pltpu.VMEM(tensor, BF), pltpu.VMEM((segments, segment), BF)],
        )
        event = result[0]
        sums[k] = result[0].astype(F32) + swap(result[1], "dp", 1).astype(F32)
    error = result[2]

    for mask in far[::-1]:
        count = sums[0].shape[0] // 2
        sums = [p[:count] + swap(p[count:].astype(BF), "dp", mask).astype(F32) for p in sums]
    own_grad, own_packed = sums[0][:, :segment], sums[0][:, segment:]
    grads = [own_grad] + sums[1:]
    for mask in mp_bits:
        crossed = [swap(p.astype(BF), "mp", mask).astype(F32) for p in grads[mask:]]
        grads = [p + q for p, q in zip(grads, crossed)]
    own_grad = grads[0]
    mean_grad = own_grad / n_dp
    mean_moment = own_packed / n_dp
    moment_new = beta_one * mean_moment + (1.0 - beta_one) * mean_grad
    denominator = jnp.sqrt(variance[0]) + epsilon
    master_new = master[0] - step_rate * (mean_moment + moment_new) / denominator
    return (master_new[None], moment_new[None], error.reshape(feedback.shape))


def solution(mesh):
    in_specs = (
        P("mp", "dp", None),
        P("mp", "dp", None),
        P("mp", "dp", None),
        P(),
        P("dp", None, "mp", None),
        P(None, ("dp", "mp"), None),
        P(None, ("dp", "mp"), None),
    )
    out_specs = (P("mp", "dp", None), P("mp", "dp", None), P("dp", None, "mp", None))
    return jax.shard_map(
        per_device, mesh=mesh, in_specs=in_specs, out_specs=out_specs, check_vma=False
    )
```

```python
import functools

import jax
import jax.numpy as jnp
from jax import lax
from jax.experimental import pallas as pl
from jax.experimental.pallas import tpu as pltpu
from jax.sharding import PartitionSpec as P

beta_one = 0.9
step_rate = 0.05
epsilon = 1e-08
down_scale = 28672.0 ** (-0.5)
BF = jnp.bfloat16
F32 = jnp.float32
NT = (((1,), (1,)), ((), ()))
NN = (((1,), (0,)), ((), ()))


def dot(a, b, dims=NN):
    return lax.dot_general(a, b, dims, preferred_element_type=F32)


def swap(x, axis, mask):
    n = lax.axis_size(axis)
    return lax.ppermute(x, axis, [(i, i ^ mask) for i in range(n)])


def after(x, *others):
    return lax.optimization_barrier((x, *others))[0]


def bits_of(n, lowest=1):
    masks = []
    mask = n // 2
    while mask >= lowest:
        masks.append(mask)
        mask //= 2
    return masks


def gradient_rows(weights, x_ref, g_ref, hidden_rows, up_scale):
    before = up_scale * dot(weights, x_ref[...], NT)[:hidden_rows]
    back = down_scale * dot(weights, g_ref[...], NT)[hidden_rows:]
    sigmoid = jax.nn.sigmoid(before)
    hidden = before * sigmoid
    slope = back * (sigmoid * (1.0 + before * (1.0 - sigmoid)))
    zeros = jnp.zeros_like(slope)
    left_up = jnp.concatenate([slope, zeros], axis=0).astype(BF)
    left_down = jnp.concatenate([zeros, hidden], axis=0).astype(BF)

    def columns(at):
        return up_scale * dot(left_up, x_ref[:, at]) + down_scale * dot(left_down, g_ref[:, at])

    return columns


def first_kernel(hidden_rows, up_scale, chunk, place_ref, w0_ref, w1_ref, x_ref, g_ref, weights_ref, part_ref, sent_ref):
    rows = 2 * hidden_rows
    half, segment = w0_ref.shape
    width = x_ref.shape[1]
    ordered = dot(place_ref[:, :half], w0_ref[...]) + dot(place_ref[:, half:], w1_ref[...])
    for c in range(width // segment):
        weights_ref[:, c * segment : (c + 1) * segment] = ordered[c * rows : (c + 1) * rows].astype(BF)
    columns = gradient_rows(weights_ref[...], x_ref, g_ref, hidden_rows, up_scale)
    for c in range(width // chunk):
        at = slice(c * chunk, (c + 1) * chunk)
        part = columns(at)
        part_ref[:, at] = part
        sent_ref[:, at] = part.astype(BF)


def moments_kernel(rows, place_ref, *refs):
    terms, (moment_ref, rate_ref) = refs[:-2], refs[-2:]
    count = len(terms) // 2
    half, segment = terms[0].shape
    width = moment_ref.shape[1]
    near, far = place_ref[:, :half], place_ref[:, half:]
    ordered = [dot(near, a[...]) + dot(far, b[...]) for a, b in zip(terms[:count], terms[count:])]
    moment = sum(ordered[2:], ordered[0])
    rate = step_rate / (jnp.sqrt(ordered[1]) + epsilon)
    for c in range(width // segment):
        at = slice(c * segment, (c + 1) * segment)
        moment_ref[:, at] = moment[c * rows : (c + 1) * rows]
        rate_ref[:, at] = rate[c * rows : (c + 1) * rows]


def store_flat(back_ref, seg_ref, kept_ref, away_ref, lanes):
    flat = dot(back_ref[...], seg_ref[...]).astype(BF)
    half = kept_ref.shape[0]
    kept_ref[:, lanes] = flat[:half]
    away_ref[:, lanes] = flat[half:]


def second_kernel(
    hidden_rows, up_scale, own, back_ref, part_ref, got_ref, weights_ref, moment_ref, rate_ref, x_ref, g_ref, *rest
):
    if own:
        feedback_ref, kept_ref, away_ref, error_ref, local_ref, seg_ref = rest
    else:
        kept_ref, away_ref, local_ref, seg_ref = rest
    rows = 2 * hidden_rows
    segment = seg_ref.shape[1]
    width = x_ref.shape[1]
    step_one = part_ref[...] + got_ref[...].astype(F32)
    local_moment = beta_one * moment_ref[...] + (1.0 - beta_one) * step_one
    local_ref[...] = (weights_ref[...].astype(F32) - local_moment * rate_ref[...]).astype(BF)
    columns = gradient_rows(local_ref[...], x_ref, g_ref, hidden_rows, up_scale)
    for c in range(width // segment):
        seg_ref[c * rows : (c + 1) * rows] = columns(slice(c * segment, (c + 1) * segment)).astype(BF)
    store_flat(back_ref, seg_ref, kept_ref, away_ref, slice(0, segment))
    if own:
        shifted = local_moment + feedback_ref[...].astype(F32)
        magnitude = jnp.sum(jnp.abs(shifted), axis=1, keepdims=True) * (1.0 / width) + 1e-06
        packed = magnitude * jnp.tanh(shifted / magnitude)
        error_ref[...] = (shifted - packed).astype(BF)
        for c in range(width // segment):
            seg_ref[c * rows : (c + 1) * rows] = packed[:, c * segment : (c + 1) * segment].astype(BF)
        store_flat(back_ref, seg_ref, kept_ref, away_ref, slice(segment, 2 * segment))


def tokens_of(step, arrays, *others):
    return [x[step] for x in lax.optimization_barrier((*arrays, *others))[: len(arrays)]]


def call(kernel, out_shape, operands, scratch=()):
    return pl.pallas_call(
        kernel,
        out_shape=out_shape,
        in_specs=[pl.BlockSpec(memory_space=pltpu.VMEM)] * len(operands),
        out_specs=jax.tree.map(lambda _: pl.BlockSpec(memory_space=pltpu.VMEM), out_shape),
        scratch_shapes=list(scratch),
        cost_estimate=pl.CostEstimate(flops=1, bytes_accessed=1, transcendentals=0),
        compiler_params=pltpu.CompilerParams(vmem_limit_bytes=16 * 1024 * 1024),
    )(*operands)


def per_device(master, moment, variance, flat_slot, feedback, activations, output_grads):
    n_dp, n_mp = lax.axis_size("dp"), lax.axis_size("mp")
    me = lax.axis_index("dp")
    span, segment = master.shape[1:]
    segments = flat_slot.shape[0]
    hidden_rows, width = feedback.shape[2:]
    rows = 2 * hidden_rows
    up_scale = width ** (-0.5)
    far = bits_of(n_dp, 2)
    mp_bits = bits_of(n_mp)
    shape = jax.ShapeDtypeStruct

    near_w = master[0].astype(BF)
    spans = jnp.concatenate([after(moment[0], near_w), variance[0]], axis=1)
    near_a = spans.astype(BF)
    low = (spans[:, :segment] - lax.reduce_precision(spans[:, :segment], 8, 7)).astype(BF)
    steps = []
    for mask in far:
        near_w = jnp.concatenate([near_w, swap(near_w, "dp", mask)], axis=0)
        steps.append(near_w)
    blocks_a = [near_a]
    for mask in reversed(mp_bits):
        blocks_a = blocks_a + [swap(b, "mp", mask) for b in blocks_a]
    all_a = after(jnp.concatenate([near_a, low] + blocks_a[1:], axis=1), steps[0])

    slot = after(flat_slot, steps[-1])
    owner = (slot // span) ^ me
    position = jnp.zeros_like(owner)
    for place, mask in enumerate(far + [1]):
        position = position + jnp.where((owner & mask) != 0, 1 << place, 0)
    position = position * span + slot % span
    position = position.reshape(rows, width // segment).T.reshape(segments)
    line = jnp.arange(segments, dtype=jnp.int32)
    place_map = (position[:, None] == line[None, :]).astype(BF)
    back_map = (line[:, None] == position[None, :]).astype(BF)

    blocks_w = [near_w]
    for mask in reversed(mp_bits):
        blocks_w = blocks_w + [swap(b, "mp", mask) for b in blocks_w]
    pairs_w = [(b, swap(b, "dp", 1)) for b in blocks_w]

    tensor = (rows, width)
    one = tokens_of(0, (activations, output_grads), steps[-2])
    half = segments // 2
    weights, parts, sent = [], [], []
    for w0, w1 in pairs_w:
        kernel = functools.partial(first_kernel, hidden_rows, up_scale, min(width, 1024))
        out = (shape(tensor, BF), shape(tensor, F32), shape(tensor, BF))
        w_t, part, part_sent = call(kernel, out, (place_map, w0, w1, *one))
        weights.append(w_t)
        parts.append(part)
        sent.append(part_sent)
    two = tokens_of(1, (activations, output_grads), sent[-1])

    for step, mask in enumerate(mp_bits):
        if step > 0:
            parts = [p + q.astype(F32) for p, q in zip(parts, got)]
            sent = [p.astype(BF) for p in parts]
        crossed = [swap(p, "mp", mask) for p in sent]
        got = [crossed[k ^ mask] for k in range(n_mp)]

    for mask in far[:-2]:
        all_a = jnp.concatenate([all_a, after(swap(all_a, "dp", mask), steps[-1])], axis=0)
    ends = [0] + [(3 + 2 * k) * segment for k in range(n_mp)]
    blocks_a = [all_a[:, ends[k] : ends[k + 1]] for k in range(n_mp)]
    blocks_a[0] = after(blocks_a[0], sent[0])
    arrived = [after(swap(b, "dp", far[-2]), sent[0] if k else sent[-1]) for k, b in enumerate(blocks_a)]
    blocks_a = [jnp.concatenate(pair, axis=0) for pair in zip(blocks_a, arrived)]
    arrived = [swap(b, "dp", far[-1]) for b in blocks_a]

    half = segments // 2
    sums, event = [None] * n_mp, sent[-1]
    for k in reversed(range(n_mp)):
        own = k == 0
        block = jnp.concatenate([blocks_a[k], after(arrived[k], event)], axis=0)
        terms = [block[:, at : at + segment] for at in range(0, block.shape[1], segment)]
        terms += [swap(term, "dp", 1) for term in terms]
        moment_t, rate = call(
            functools.partial(moments_kernel, rows), (shape(tensor, F32), shape(tensor, F32)), (place_map, *terms)
        )
        operands = [back_map, parts[k], got[k], weights[k], moment_t, rate, *two]
        out = [shape((half, (2 if own else 1) * segment), BF)] * 2
        if own:
            operands.append(feedback[0].reshape(tensor))
            out.append(shape(tensor, BF))
        result = call(
            functools.partial(second_kernel, hidden_rows, up_scale, own),
            tuple(out),
            operands,
            [pltpu.VMEM(tensor, BF), pltpu.VMEM((segments, segment), BF)],
        )
        event = result[0]
        sums[k] = result[0].astype(F32) + swap(result[1], "dp", 1).astype(F32)
    error = result[2]

    def halve(total, mask):
        count = total.shape[0] // 2
        return total[:count] + swap(total[count:].astype(BF), "dp", mask).astype(F32)

    for mask in far[:0:-1]:
        sums = [halve(p, mask) for p in sums]
    grads = [sums[0][:, :segment]] + sums[1:]
    for mask in mp_bits:
        crossed = [swap(p.astype(BF), "mp", mask).astype(F32) for p in grads[mask:]]
        grads = [p + q for p, q in zip(grads, crossed)]
    both = halve(jnp.concatenate([grads[0], sums[0][:, segment:]], axis=1), far[0])
    own_grad, own_packed = both[:, :segment], both[:, segment:]
    mean_grad = own_grad / n_dp
    mean_moment = own_packed / n_dp
    moment_new = beta_one * mean_moment + (1.0 - beta_one) * mean_grad
    denominator = jnp.sqrt(variance[0]) + epsilon
    master_new = master[0] - step_rate * (mean_moment + moment_new) / denominator
    return (master_new[None], moment_new[None], error.reshape(feedback.shape))


def solution(mesh):
    in_specs = (
        P("mp", "dp", None),
        P("mp", "dp", None),
        P("mp", "dp", None),
        P(),
        P("dp", None, "mp", None),
        P(None, ("dp", "mp"), None),
        P(None, ("dp", "mp"), None),
    )
    out_specs = (P("mp", "dp", None), P("mp", "dp", None), P("dp", None, "mp", None))
    return jax.shard_map(
        per_device, mesh=mesh, in_specs=in_specs, out_specs=out_specs, check_vma=False
    )
```

```python
import functools

import jax
import jax.numpy as jnp
from jax import lax
from jax.experimental import pallas as pl
from jax.experimental.pallas import tpu as pltpu
from jax.sharding import PartitionSpec as P

beta_one = 0.9
step_rate = 0.05
epsilon = 1e-08
down_scale = 28672.0 ** (-0.5)
BF = jnp.bfloat16
F32 = jnp.float32
NT = (((1,), (1,)), ((), ()))
NN = (((1,), (0,)), ((), ()))


def dot(a, b, dims=NN):
    return lax.dot_general(a, b, dims, preferred_element_type=F32)


def swap(x, axis, mask):
    n = lax.axis_size(axis)
    return lax.ppermute(x, axis, [(i, i ^ mask) for i in range(n)])


def after(x, *others):
    return lax.optimization_barrier((x, *others))[0]


def bits_of(n, lowest=1):
    masks = []
    mask = n // 2
    while mask >= lowest:
        masks.append(mask)
        mask //= 2
    return masks


def gradient_rows(weights, x_ref, g_ref, hidden_rows, up_scale):
    before = up_scale * dot(weights, x_ref[...], NT)[:hidden_rows]
    back = down_scale * dot(weights, g_ref[...], NT)[hidden_rows:]
    sigmoid = jax.nn.sigmoid(before)
    hidden = before * sigmoid
    slope = back * (sigmoid * (1.0 + before * (1.0 - sigmoid)))
    zeros = jnp.zeros_like(slope)
    left_up = jnp.concatenate([slope, zeros], axis=0).astype(BF)
    left_down = jnp.concatenate([zeros, hidden], axis=0).astype(BF)

    def columns(at):
        return up_scale * dot(left_up, x_ref[:, at]) + down_scale * dot(left_down, g_ref[:, at])

    return columns


def first_kernel(hidden_rows, up_scale, chunk, place_ref, w0_ref, w1_ref, x_ref, g_ref, weights_ref, part_ref, sent_ref):
    rows = 2 * hidden_rows
    half, segment = w0_ref.shape
    width = x_ref.shape[1]
    ordered = dot(place_ref[:, :half], w0_ref[...]) + dot(place_ref[:, half:], w1_ref[...])
    for c in range(width // segment):
        weights_ref[:, c * segment : (c + 1) * segment] = ordered[c * rows : (c + 1) * rows].astype(BF)
    columns = gradient_rows(weights_ref[...], x_ref, g_ref, hidden_rows, up_scale)
    for c in range(width // chunk):
        at = slice(c * chunk, (c + 1) * chunk)
        part = columns(at)
        part_ref[:, at] = part
        sent_ref[:, at] = part.astype(BF)


def store_flat(back_ref, seg_ref, kept_ref, away_ref, lanes):
    flat = dot(back_ref[...], seg_ref[...]).astype(BF)
    half = kept_ref.shape[0]
    kept_ref[:, lanes] = flat[:half]
    away_ref[:, lanes] = flat[half:]


def second_kernel(
    hidden_rows, up_scale, own, place_ref, back_ref, part_ref, got_ref, weights_ref, x_ref, g_ref, near_ref, *rest
):
    if own:
        *far_refs, feedback_ref, kept_ref, away_ref, error_ref, local_ref, seg_ref, shifted_ref = rest
    else:
        *far_refs, kept_ref, away_ref, local_ref, seg_ref = rest
    rows = 2 * hidden_rows
    half = near_ref.shape[0]
    segment = seg_ref.shape[1]
    width = x_ref.shape[1]
    near = dot(place_ref[:, :half], near_ref[...])
    terms = [
        near[:, i * segment : (i + 1) * segment] + dot(place_ref[:, half:], ref[...]) for i, ref in enumerate(far_refs)
    ]
    moment = sum(terms[2:], terms[0])
    rate = step_rate / (jnp.sqrt(terms[1]) + epsilon)
    for c in range(width // segment):
        at, run = slice(c * segment, (c + 1) * segment), slice(c * rows, (c + 1) * rows)
        step_one = part_ref[:, at] + got_ref[:, at].astype(F32)
        local_moment = beta_one * moment[run] + (1.0 - beta_one) * step_one
        local_ref[:, at] = (weights_ref[:, at].astype(F32) - local_moment * rate[run]).astype(BF)
        if own:
            shifted_ref[:, at] = local_moment + feedback_ref[:, at].astype(F32)
    columns = gradient_rows(local_ref[...], x_ref, g_ref, hidden_rows, up_scale)
    for c in range(width // segment):
        seg_ref[c * rows : (c + 1) * rows] = columns(slice(c * segment, (c + 1) * segment)).astype(BF)
    store_flat(back_ref, seg_ref, kept_ref, away_ref, slice(0, segment))
    if own:
        shifted = shifted_ref[...]
        magnitude = jnp.sum(jnp.abs(shifted), axis=1, keepdims=True) * (1.0 / width) + 1e-06
        packed = magnitude * jnp.tanh(shifted / magnitude)
        error_ref[...] = (shifted - packed).astype(BF)
        for c in range(width // segment):
            seg_ref[c * rows : (c + 1) * rows] = packed[:, c * segment : (c + 1) * segment].astype(BF)
        store_flat(back_ref, seg_ref, kept_ref, away_ref, slice(segment, 2 * segment))


def tokens_of(step, arrays, *others):
    return [x[step] for x in lax.optimization_barrier((*arrays, *others))[: len(arrays)]]


def call(kernel, out_shape, operands, scratch=()):
    return pl.pallas_call(
        kernel,
        out_shape=out_shape,
        in_specs=[pl.BlockSpec(memory_space=pltpu.VMEM)] * len(operands),
        out_specs=jax.tree.map(lambda _: pl.BlockSpec(memory_space=pltpu.VMEM), out_shape),
        scratch_shapes=list(scratch),
        cost_estimate=pl.CostEstimate(flops=1, bytes_accessed=1, transcendentals=0),
        compiler_params=pltpu.CompilerParams(vmem_limit_bytes=16 * 1024 * 1024),
    )(*operands)


def per_device(master, moment, variance, flat_slot, feedback, activations, output_grads):
    n_dp, n_mp = lax.axis_size("dp"), lax.axis_size("mp")
    me = lax.axis_index("dp")
    span, segment = master.shape[1:]
    segments = flat_slot.shape[0]
    hidden_rows, width = feedback.shape[2:]
    rows = 2 * hidden_rows
    up_scale = width ** (-0.5)
    far = bits_of(n_dp, 2)
    mp_bits = bits_of(n_mp)
    shape = jax.ShapeDtypeStruct

    near_w = master[0].astype(BF)
    spans = jnp.concatenate([after(moment[0], near_w), variance[0]], axis=1)
    near_a = spans.astype(BF)
    low = (spans[:, :segment] - lax.reduce_precision(spans[:, :segment], 8, 7)).astype(BF)
    steps = []
    for mask in far:
        near_w = jnp.concatenate([near_w, swap(near_w, "dp", mask)], axis=0)
        steps.append(near_w)
    blocks_a = [near_a]
    for mask in reversed(mp_bits):
        blocks_a = blocks_a + [swap(b, "mp", mask) for b in blocks_a]
    all_a = after(jnp.concatenate([near_a, low] + blocks_a[1:], axis=1), steps[0])

    slot = after(flat_slot, steps[-1])
    owner = (slot // span) ^ me
    position = jnp.zeros_like(owner)
    for place, mask in enumerate(far + [1]):
        position = position + jnp.where((owner & mask) != 0, 1 << place, 0)
    position = position * span + slot % span
    position = position.reshape(rows, width // segment).T.reshape(segments)
    line = jnp.arange(segments, dtype=jnp.int32)
    place_map = (position[:, None] == line[None, :]).astype(BF)
    back_map = (line[:, None] == position[None, :]).astype(BF)

    blocks_w = [near_w]
    for mask in reversed(mp_bits):
        blocks_w = blocks_w + [swap(b, "mp", mask) for b in blocks_w]
    pairs_w = [(b, swap(b, "dp", 1)) for b in blocks_w]

    tensor = (rows, width)
    one = tokens_of(0, (activations, output_grads), steps[-2])
    half = segments // 2
    weights, parts, sent = [], [], []
    for w0, w1 in pairs_w:
        kernel = functools.partial(first_kernel, hidden_rows, up_scale, min(width, 1024))
        out = (shape(tensor, BF), shape(tensor, F32), shape(tensor, BF))
        w_t, part, part_sent = call(kernel, out, (place_map, w0, w1, *one))
        weights.append(w_t)
        parts.append(part)
        sent.append(part_sent)
    two = tokens_of(1, (activations, output_grads), sent[-1])

    for step, mask in enumerate(mp_bits):
        if step > 0:
            parts = [p + q.astype(F32) for p, q in zip(parts, got)]
            sent = [p.astype(BF) for p in parts]
        crossed = [swap(p, "mp", mask) for p in sent]
        got = [crossed[k ^ mask] for k in range(n_mp)]

    for mask in far[:-2]:
        all_a = jnp.concatenate([all_a, after(swap(all_a, "dp", mask), steps[-1])], axis=0)
    ends = [0] + [(3 + 2 * k) * segment for k in range(n_mp)]
    blocks_a = [all_a[:, ends[k] : ends[k + 1]] for k in range(n_mp)]
    blocks_a[0] = after(blocks_a[0], sent[0])
    arrived = [after(swap(b, "dp", far[-2]), sent[0] if k else sent[-1]) for k, b in enumerate(blocks_a)]
    blocks_a = [jnp.concatenate(pair, axis=0) for pair in zip(blocks_a, arrived)]
    arrived = [swap(b, "dp", far[-1]) for b in blocks_a]

    half = segments // 2
    sums, event = [None] * n_mp, sent[-1]
    for k in reversed(range(n_mp)):
        own = k == 0
        block = jnp.concatenate([blocks_a[k], after(arrived[k], event)], axis=0)
        far_terms = [swap(block[:, at : at + segment], "dp", 1) for at in range(0, block.shape[1], segment)]
        operands = [place_map, back_map, parts[k], got[k], weights[k], *two, block, *far_terms]
        out = [shape((half, (2 if own else 1) * segment), BF)] * 2
        scratch = [pltpu.VMEM(tensor, BF), pltpu.VMEM((segments, segment), BF)]
        if own:
            operands.append(feedback[0].reshape(tensor))
            out.append(shape(tensor, BF))
            scratch.append(pltpu.VMEM(tensor, F32))
        result = call(
            functools.partial(second_kernel, hidden_rows, up_scale, own),
            tuple(out),
            operands,
            scratch,
        )
        event = result[0]
        sums[k] = result[0].astype(F32) + swap(result[1], "dp", 1).astype(F32)
    error = result[2]

    for mask in far[::-1]:
        count = sums[0].shape[0] // 2
        sums = [p[:count] + swap(p[count:].astype(BF), "dp", mask).astype(F32) for p in sums]
    own_grad, own_packed = sums[0][:, :segment], sums[0][:, segment:]
    grads = [own_grad] + sums[1:]
    for mask in mp_bits:
        crossed = [swap(p.astype(BF), "mp", mask).astype(F32) for p in grads[mask:]]
        grads = [p + q for p, q in zip(grads, crossed)]
    own_grad = grads[0]
    mean_grad = own_grad / n_dp
    mean_moment = own_packed / n_dp
    moment_new = beta_one * mean_moment + (1.0 - beta_one) * mean_grad
    denominator = jnp.sqrt(variance[0]) + epsilon
    master_new = master[0] - step_rate * (mean_moment + moment_new) / denominator
    return (master_new[None], moment_new[None], error.reshape(feedback.shape))


def solution(mesh):
    in_specs = (
        P("mp", "dp", None),
        P("mp", "dp", None),
        P("mp", "dp", None),
        P(),
        P("dp", None, "mp", None),
        P(None, ("dp", "mp"), None),
        P(None, ("dp", "mp"), None),
    )
    out_specs = (P("mp", "dp", None), P("mp", "dp", None), P("dp", None, "mp", None))
    return jax.shard_map(
        per_device, mesh=mesh, in_specs=in_specs, out_specs=out_specs, check_vma=False
    )
```

```python
import functools

import jax
import jax.numpy as jnp
from jax import lax
from jax.experimental import pallas as pl
from jax.experimental.pallas import tpu as pltpu
from jax.sharding import PartitionSpec as P

beta_one = 0.9
step_rate = 0.05
epsilon = 1e-08
down_scale = 28672.0 ** (-0.5)
BF = jnp.bfloat16
F32 = jnp.float32
NT = (((1,), (1,)), ((), ()))
NN = (((1,), (0,)), ((), ()))


def dot(a, b, dims=NN):
    return lax.dot_general(a, b, dims, preferred_element_type=F32)


def swap(x, axis, mask):
    n = lax.axis_size(axis)
    return lax.ppermute(x, axis, [(i, i ^ mask) for i in range(n)])


def after(x, *others):
    return lax.optimization_barrier((x, *others))[0]


def halve(total, mask, *others):
    count = total.shape[0] // 2
    return total[:count] + after(swap(total[count:].astype(BF), "dp", mask), *others).astype(F32)


def bits_of(n, lowest=1):
    masks = []
    mask = n // 2
    while mask >= lowest:
        masks.append(mask)
        mask //= 2
    return masks


def gradient_rows(weights, x_ref, g_ref, hidden_rows, up_scale):
    before = up_scale * dot(weights, x_ref[...], NT)[:hidden_rows]
    back = down_scale * dot(weights, g_ref[...], NT)[hidden_rows:]
    sigmoid = jax.nn.sigmoid(before)
    hidden = before * sigmoid
    slope = back * (sigmoid * (1.0 + before * (1.0 - sigmoid)))
    zeros = jnp.zeros_like(slope)
    left_up = jnp.concatenate([slope, zeros], axis=0).astype(BF)
    left_down = jnp.concatenate([zeros, hidden], axis=0).astype(BF)

    def columns(at):
        return up_scale * dot(left_up, x_ref[:, at]) + down_scale * dot(left_down, g_ref[:, at])

    return columns


def first_kernel(hidden_rows, up_scale, chunk, place_ref, w0_ref, w1_ref, x_ref, g_ref, weights_ref, part_ref, sent_ref):
    rows = 2 * hidden_rows
    half, segment = w0_ref.shape
    width = x_ref.shape[1]
    ordered = dot(place_ref[:, :half], w0_ref[...]) + dot(place_ref[:, half:], w1_ref[...])
    for c in range(width // segment):
        weights_ref[:, c * segment : (c + 1) * segment] = ordered[c * rows : (c + 1) * rows].astype(BF)
    columns = gradient_rows(weights_ref[...], x_ref, g_ref, hidden_rows, up_scale)
    for c in range(width // chunk):
        at = slice(c * chunk, (c + 1) * chunk)
        part = columns(at)
        part_ref[:, at] = part
        sent_ref[:, at] = part.astype(BF)


def store_flat(back_ref, seg_ref, kept_ref, away_ref, lanes):
    flat = dot(back_ref[...], seg_ref[...]).astype(BF)
    half = kept_ref.shape[0]
    kept_ref[:, lanes] = flat[:half]
    away_ref[:, lanes] = flat[half:]


def second_kernel(
    hidden_rows, up_scale, own, place_ref, back_ref, part_ref, got_ref, weights_ref, x_ref, g_ref, near_ref, *rest
):
    if own:
        *far_refs, feedback_ref, kept_ref, away_ref, error_ref, local_ref, seg_ref, shifted_ref = rest
    else:
        *far_refs, kept_ref, away_ref, local_ref, seg_ref = rest
    rows = 2 * hidden_rows
    half = near_ref.shape[0]
    segment = seg_ref.shape[1]
    width = x_ref.shape[1]
    near = dot(place_ref[:, :half], near_ref[...])
    terms = [
        near[:, i * segment : (i + 1) * segment] + dot(place_ref[:, half:], ref[...]) for i, ref in enumerate(far_refs)
    ]
    moment = sum(terms[2:], terms[0])
    rate = step_rate / (jnp.sqrt(terms[1]) + epsilon)
    for c in range(width // segment):
        at, run = slice(c * segment, (c + 1) * segment), slice(c * rows, (c + 1) * rows)
        step_one = part_ref[:, at] + got_ref[:, at].astype(F32)
        local_moment = beta_one * moment[run] + (1.0 - beta_one) * step_one
        local_ref[:, at] = (weights_ref[:, at].astype(F32) - local_moment * rate[run]).astype(BF)
        if own:
            shifted_ref[:, at] = local_moment + feedback_ref[:, at].astype(F32)
    columns = gradient_rows(local_ref[...], x_ref, g_ref, hidden_rows, up_scale)
    for c in range(width // segment):
        seg_ref[c * rows : (c + 1) * rows] = columns(slice(c * segment, (c + 1) * segment)).astype(BF)
    store_flat(back_ref, seg_ref, kept_ref, away_ref, slice(0, segment))
    if own:
        shifted = shifted_ref[...]
        magnitude = jnp.sum(jnp.abs(shifted), axis=1, keepdims=True) * (1.0 / width) + 1e-06
        packed = magnitude * jnp.tanh(shifted / magnitude)
        error_ref[...] = (shifted - packed).astype(BF)
        for c in range(width // segment):
            seg_ref[c * rows : (c + 1) * rows] = packed[:, c * segment : (c + 1) * segment].astype(BF)
        store_flat(back_ref, seg_ref, kept_ref, away_ref, slice(segment, 2 * segment))


def tokens_of(step, arrays, *others):
    return [x[step] for x in lax.optimization_barrier((*arrays, *others))[: len(arrays)]]


def call(kernel, out_shape, operands, scratch=()):
    return pl.pallas_call(
        kernel,
        out_shape=out_shape,
        in_specs=[pl.BlockSpec(memory_space=pltpu.VMEM)] * len(operands),
        out_specs=jax.tree.map(lambda _: pl.BlockSpec(memory_space=pltpu.VMEM), out_shape),
        scratch_shapes=list(scratch),
        cost_estimate=pl.CostEstimate(flops=1, bytes_accessed=1, transcendentals=0),
        compiler_params=pltpu.CompilerParams(vmem_limit_bytes=16 * 1024 * 1024),
    )(*operands)


def per_device(master, moment, variance, flat_slot, feedback, activations, output_grads):
    n_dp, n_mp = lax.axis_size("dp"), lax.axis_size("mp")
    me = lax.axis_index("dp")
    span, segment = master.shape[1:]
    segments = flat_slot.shape[0]
    hidden_rows, width = feedback.shape[2:]
    rows = 2 * hidden_rows
    up_scale = width ** (-0.5)
    far = bits_of(n_dp, 2)
    mp_bits = bits_of(n_mp)
    shape = jax.ShapeDtypeStruct

    near_w = master[0].astype(BF)
    spans = jnp.concatenate([after(moment[0], near_w), variance[0]], axis=1)
    near_a = spans.astype(BF)
    low = (spans[:, :segment] - lax.reduce_precision(spans[:, :segment], 8, 7)).astype(BF)
    steps = []
    for mask in far:
        near_w = jnp.concatenate([near_w, swap(near_w, "dp", mask)], axis=0)
        steps.append(near_w)
    blocks_a = [near_a]
    for mask in reversed(mp_bits):
        blocks_a = blocks_a + [swap(b, "mp", mask) for b in blocks_a]
    all_a = after(jnp.concatenate([near_a, low] + blocks_a[1:], axis=1), steps[0])

    slot = after(flat_slot, steps[-1])
    owner = (slot // span) ^ me
    position = jnp.zeros_like(owner)
    for place, mask in enumerate(far + [1]):
        position = position + jnp.where((owner & mask) != 0, 1 << place, 0)
    position = position * span + slot % span
    position = position.reshape(rows, width // segment).T.reshape(segments)
    line = jnp.arange(segments, dtype=jnp.int32)
    place_map = (position[:, None] == line[None, :]).astype(BF)
    back_map = (line[:, None] == position[None, :]).astype(BF)

    blocks_w = [near_w]
    for mask in reversed(mp_bits):
        blocks_w = blocks_w + [swap(b, "mp", mask) for b in blocks_w]
    pairs_w = [(b, swap(b, "dp", 1)) for b in blocks_w]

    tensor = (rows, width)
    one = tokens_of(0, (activations, output_grads), steps[-2])
    half = segments // 2
    weights, parts, sent = [], [], []
    for w0, w1 in pairs_w:
        kernel = functools.partial(first_kernel, hidden_rows, up_scale, min(width, 1024))
        out = (shape(tensor, BF), shape(tensor, F32), shape(tensor, BF))
        w_t, part, part_sent = call(kernel, out, (place_map, w0, w1, *one))
        weights.append(w_t)
        parts.append(part)
        sent.append(part_sent)
    two = tokens_of(1, (activations, output_grads), sent[-1])

    for step, mask in enumerate(mp_bits):
        if step > 0:
            parts = [p + q.astype(F32) for p, q in zip(parts, got)]
            sent = [p.astype(BF) for p in parts]
        crossed = [swap(p, "mp", mask) for p in sent]
        got = [crossed[k ^ mask] for k in range(n_mp)]

    for mask in far[:-2]:
        all_a = jnp.concatenate([all_a, after(swap(all_a, "dp", mask), steps[-1])], axis=0)
    ends = [0] + [(3 + 2 * k) * segment for k in range(n_mp)]
    blocks_a = [all_a[:, ends[k] : ends[k + 1]] for k in range(n_mp)]
    blocks_a[0] = after(blocks_a[0], sent[0])
    arrived = [after(swap(b, "dp", far[-2]), sent[0] if k else sent[-1]) for k, b in enumerate(blocks_a)]
    blocks_a = [jnp.concatenate(pair, axis=0) for pair in zip(blocks_a, arrived)]
    arrived = [swap(blocks_a[0], "dp", far[-1])]
    for block in blocks_a[1:]:
        terms = [swap(block[:, at : at + segment], "dp", far[-1]) for at in (0, segment)]
        arrived.append(jnp.concatenate(lax.optimization_barrier((*terms, sent[-1], blocks_a[0]))[:2], axis=1))

    half = segments // 2
    sums, event = [None] * n_mp, sent[-1]
    for k in reversed(range(n_mp)):
        own = k == 0
        block = jnp.concatenate([blocks_a[k], after(arrived[k], event)], axis=0)
        far_terms = [swap(block[:, at : at + segment], "dp", 1) for at in range(0, block.shape[1], segment)]
        operands = [place_map, back_map, parts[k], got[k], weights[k], *two, block, *far_terms]
        out = [shape((half, (2 if own else 1) * segment), BF)] * 2
        scratch = [pltpu.VMEM(tensor, BF), pltpu.VMEM((segments, segment), BF)]
        if own:
            operands.append(feedback[0].reshape(tensor))
            out.append(shape(tensor, BF))
            scratch.append(pltpu.VMEM(tensor, F32))
        result = call(
            functools.partial(second_kernel, hidden_rows, up_scale, own),
            tuple(out),
            operands,
            scratch,
        )
        event = result[0]
        if own:
            sums[1:] = [halve(p, far[-1], event) for p in sums[1:]]
            away, error = after(result[1], *sums[1:]), result[2]
        else:
            away = result[1]
        sums[k] = result[0].astype(F32) + swap(away, "dp", 1).astype(F32)
    sums[0] = halve(sums[0], far[-1])

    grads = [sums[0][:, :segment]] + sums[1:]
    for mask in mp_bits:
        crossed = [swap(p.astype(BF), "mp", mask).astype(F32) for p in grads[mask:]]
        grads = [p + q for p, q in zip(grads, crossed)]
    both = jnp.concatenate([grads[0], sums[0][:, segment:]], axis=1)
    for mask in far[-2::-1]:
        both = halve(both, mask)
    own_grad, own_packed = both[:, :segment], both[:, segment:]
    mean_grad = own_grad / n_dp
    mean_moment = own_packed / n_dp
    moment_new = beta_one * mean_moment + (1.0 - beta_one) * mean_grad
    denominator = jnp.sqrt(variance[0]) + epsilon
    master_new = master[0] - step_rate * (mean_moment + moment_new) / denominator
    return (master_new[None], moment_new[None], error.reshape(feedback.shape))


def solution(mesh):
    in_specs = (
        P("mp", "dp", None),
        P("mp", "dp", None),
        P("mp", "dp", None),
        P(),
        P("dp", None, "mp", None),
        P(None, ("dp", "mp"), None),
        P(None, ("dp", "mp"), None),
    )
    out_specs = (P("mp", "dp", None), P("mp", "dp", None), P("dp", None, "mp", None))
    return jax.shard_map(
        per_device, mesh=mesh, in_specs=in_specs, out_specs=out_specs, check_vma=False
    )
```

```python
import functools

import jax
import jax.numpy as jnp
from jax import lax
from jax.experimental import pallas as pl
from jax.experimental.pallas import tpu as pltpu
from jax.sharding import PartitionSpec as P

beta_one = 0.9
step_rate = 0.05
epsilon = 1e-08
down_scale = 28672.0 ** (-0.5)
BF = jnp.bfloat16
F32 = jnp.float32
NT = (((1,), (1,)), ((), ()))
NN = (((1,), (0,)), ((), ()))


def dot(a, b, dims=NN):
    return lax.dot_general(a, b, dims, preferred_element_type=F32)


def swap(x, axis, mask):
    n = lax.axis_size(axis)
    return lax.ppermute(x, axis, [(i, i ^ mask) for i in range(n)])


def after(x, *others):
    return lax.optimization_barrier((x, *others))[0]


def halve(total, mask):
    count = total.shape[0] // 2
    return total[:count] + swap(total[count:].astype(BF), "dp", mask).astype(F32)


def bits_of(n, lowest=1):
    masks = []
    mask = n // 2
    while mask >= lowest:
        masks.append(mask)
        mask //= 2
    return masks


def gradient_rows(weights, x_ref, g_ref, hidden_rows, up_scale):
    before = up_scale * dot(weights, x_ref[...], NT)[:hidden_rows]
    back = down_scale * dot(weights, g_ref[...], NT)[hidden_rows:]
    sigmoid = jax.nn.sigmoid(before)
    hidden = before * sigmoid
    slope = back * (sigmoid * (1.0 + before * (1.0 - sigmoid)))
    zeros = jnp.zeros_like(slope)
    left_up = jnp.concatenate([slope, zeros], axis=0).astype(BF)
    left_down = jnp.concatenate([zeros, hidden], axis=0).astype(BF)

    def columns(at):
        return up_scale * dot(left_up, x_ref[:, at]) + down_scale * dot(left_down, g_ref[:, at])

    return columns


def first_kernel(hidden_rows, up_scale, chunk, place_ref, w0_ref, w1_ref, x_ref, g_ref, weights_ref, part_ref, sent_ref):
    rows = 2 * hidden_rows
    half, segment = w0_ref.shape
    width = x_ref.shape[1]
    ordered = dot(place_ref[:, :half], w0_ref[...]) + dot(place_ref[:, half:], w1_ref[...])
    for c in range(width // segment):
        weights_ref[:, c * segment : (c + 1) * segment] = ordered[c * rows : (c + 1) * rows].astype(BF)
    columns = gradient_rows(weights_ref[...], x_ref, g_ref, hidden_rows, up_scale)
    for c in range(width // chunk):
        at = slice(c * chunk, (c + 1) * chunk)
        part = columns(at)
        part_ref[:, at] = part
        sent_ref[:, at] = part.astype(BF)


def store_flat(back_ref, seg_ref, kept_ref, away_ref, lanes):
    flat = dot(back_ref[...], seg_ref[...]).astype(BF)
    half = kept_ref.shape[0]
    kept_ref[:, lanes] = flat[:half]
    away_ref[:, lanes] = flat[half:]


def second_kernel(
    hidden_rows, up_scale, own, place_ref, back_ref, part_ref, got_ref, weights_ref, x_ref, g_ref, near_ref, *rest
):
    if own:
        *far_refs, feedback_ref, kept_ref, away_ref, error_ref, local_ref, seg_ref, shifted_ref = rest
    else:
        *far_refs, kept_ref, away_ref, local_ref, seg_ref = rest
    rows = 2 * hidden_rows
    half = near_ref.shape[0]
    segment = seg_ref.shape[1]
    width = x_ref.shape[1]
    near = dot(place_ref[:, :half], near_ref[...])
    terms = [
        near[:, i * segment : (i + 1) * segment] + dot(place_ref[:, half:], ref[...]) for i, ref in enumerate(far_refs)
    ]
    moment = sum(terms[2:], terms[0])
    rate = step_rate / (jnp.sqrt(terms[1]) + epsilon)
    for c in range(width // segment):
        at, run = slice(c * segment, (c + 1) * segment), slice(c * rows, (c + 1) * rows)
        step_one = part_ref[:, at] + got_ref[:, at].astype(F32)
        local_moment = beta_one * moment[run] + (1.0 - beta_one) * step_one
        local_ref[:, at] = (weights_ref[:, at].astype(F32) - local_moment * rate[run]).astype(BF)
        if own:
            shifted_ref[:, at] = local_moment + feedback_ref[:, at].astype(F32)
    columns = gradient_rows(local_ref[...], x_ref, g_ref, hidden_rows, up_scale)
    for c in range(width // segment):
        seg_ref[c * rows : (c + 1) * rows] = columns(slice(c * segment, (c + 1) * segment)).astype(BF)
    store_flat(back_ref, seg_ref, kept_ref, away_ref, slice(0, segment))
    if own:
        shifted = shifted_ref[...]
        magnitude = jnp.sum(jnp.abs(shifted), axis=1, keepdims=True) * (1.0 / width) + 1e-06
        packed = magnitude * jnp.tanh(shifted / magnitude)
        error_ref[...] = (shifted - packed).astype(BF)
        for c in range(width // segment):
            seg_ref[c * rows : (c + 1) * rows] = packed[:, c * segment : (c + 1) * segment].astype(BF)
        store_flat(back_ref, seg_ref, kept_ref, away_ref, slice(segment, 2 * segment))


def tokens_of(step, arrays, *others):
    return [x[step] for x in lax.optimization_barrier((*arrays, *others))[: len(arrays)]]


def call(kernel, out_shape, operands, scratch=()):
    return pl.pallas_call(
        kernel,
        out_shape=out_shape,
        in_specs=[pl.BlockSpec(memory_space=pltpu.VMEM)] * len(operands),
        out_specs=jax.tree.map(lambda _: pl.BlockSpec(memory_space=pltpu.VMEM), out_shape),
        scratch_shapes=list(scratch),
        cost_estimate=pl.CostEstimate(flops=1, bytes_accessed=1, transcendentals=0),
        compiler_params=pltpu.CompilerParams(vmem_limit_bytes=16 * 1024 * 1024),
    )(*operands)


def per_device(master, moment, variance, flat_slot, feedback, activations, output_grads):
    n_dp, n_mp = lax.axis_size("dp"), lax.axis_size("mp")
    me = lax.axis_index("dp")
    span, segment = master.shape[1:]
    segments = flat_slot.shape[0]
    hidden_rows, width = feedback.shape[2:]
    rows = 2 * hidden_rows
    up_scale = width ** (-0.5)
    far = bits_of(n_dp, 2)
    mp_bits = bits_of(n_mp)
    shape = jax.ShapeDtypeStruct

    near_w = master[0].astype(BF)
    spans = jnp.concatenate([after(moment[0], near_w), variance[0]], axis=1)
    near_a = spans.astype(BF)
    low = (spans[:, :segment] - lax.reduce_precision(spans[:, :segment], 8, 7)).astype(BF)
    steps = []
    for mask in far:
        near_w = jnp.concatenate([near_w, swap(near_w, "dp", mask)], axis=0)
        steps.append(near_w)
    blocks_a = [near_a]
    for mask in reversed(mp_bits):
        blocks_a = blocks_a + [swap(b, "mp", mask) for b in blocks_a]
    all_a = after(jnp.concatenate([near_a, low] + blocks_a[1:], axis=1), steps[0])

    slot = after(flat_slot, steps[-1])
    owner = (slot // span) ^ me
    position = jnp.zeros_like(owner)
    for place, mask in enumerate(far + [1]):
        position = position + jnp.where((owner & mask) != 0, 1 << place, 0)
    position = position * span + slot % span
    position = position.reshape(rows, width // segment).T.reshape(segments)
    line = jnp.arange(segments, dtype=jnp.int32)
    place_map = (position[:, None] == line[None, :]).astype(BF)
    back_map = (line[:, None] == position[None, :]).astype(BF)

    blocks_w = [near_w]
    for mask in reversed(mp_bits):
        blocks_w = blocks_w + [swap(b, "mp", mask) for b in blocks_w]
    pairs_w = [(b, swap(b, "dp", 1)) for b in blocks_w]

    tensor = (rows, width)
    one = tokens_of(0, (activations, output_grads), steps[-2])
    half = segments // 2
    weights, parts, sent = [], [], []
    for w0, w1 in pairs_w:
        kernel = functools.partial(first_kernel, hidden_rows, up_scale, min(width, 1024))
        out = (shape(tensor, BF), shape(tensor, F32), shape(tensor, BF))
        w_t, part, part_sent = call(kernel, out, (place_map, w0, w1, *one))
        weights.append(w_t)
        parts.append(part)
        sent.append(part_sent)
    two = tokens_of(1, (activations, output_grads), sent[-1])

    for step, mask in enumerate(mp_bits):
        if step > 0:
            parts = [p + q.astype(F32) for p, q in zip(parts, got)]
            sent = [p.astype(BF) for p in parts]
        crossed = [swap(p, "mp", mask) for p in sent]
        got = [crossed[k ^ mask] for k in range(n_mp)]

    for mask in far[:-2]:
        all_a = jnp.concatenate([all_a, after(swap(all_a, "dp", mask), steps[-1])], axis=0)
    ends = [0] + [(3 + 2 * k) * segment for k in range(n_mp)]
    blocks_a = [all_a[:, ends[k] : ends[k + 1]] for k in range(n_mp)]
    blocks_a[0] = after(blocks_a[0], sent[0])
    arrived = [after(swap(b, "dp", far[-2]), sent[0] if k else sent[-1]) for k, b in enumerate(blocks_a)]
    blocks_a = [jnp.concatenate(pair, axis=0) for pair in zip(blocks_a, arrived)]
    arrived = [swap(blocks_a[0], "dp", far[-1])]
    for block in blocks_a[1:]:
        terms = [swap(block[:, at : at + segment], "dp", far[-1]) for at in (0, segment)]
        arrived.append(jnp.concatenate(lax.optimization_barrier((*terms, sent[-1], blocks_a[0]))[:2], axis=1))

    half = segments // 2
    sums, event = [None] * n_mp, sent[-1]
    for k in reversed(range(n_mp)):
        own = k == 0
        block = jnp.concatenate([blocks_a[k], after(arrived[k], event)], axis=0)
        far_terms = [swap(block[:, at : at + segment], "dp", 1) for at in range(0, block.shape[1], segment)]
        operands = [place_map, back_map, parts[k], got[k], weights[k], *two, block, *far_terms]
        out = [shape((half, (2 if own else 1) * segment), BF)] * 2
        scratch = [pltpu.VMEM(tensor, BF), pltpu.VMEM((segments, segment), BF)]
        if own:
            operands.append(feedback[0].reshape(tensor))
            out.append(shape(tensor, BF))
            scratch.append(pltpu.VMEM(tensor, F32))
        result = call(
            functools.partial(second_kernel, hidden_rows, up_scale, own),
            tuple(out),
            operands,
            scratch,
        )
        event = result[0]
        sums[k] = result[0].astype(F32) + swap(result[1], "dp", 1).astype(F32)
    error = result[2]

    sums = [halve(p, far[-1]) for p in sums]
    grads = [sums[0][:, :segment]] + sums[1:]
    for mask in mp_bits:
        crossed = [swap(p.astype(BF), "mp", mask).astype(F32) for p in grads[mask:]]
        grads = [p + q for p, q in zip(grads, crossed)]
    both = jnp.concatenate([grads[0], sums[0][:, segment:]], axis=1)
    for mask in far[-2::-1]:
        both = halve(both, mask)
    own_grad, own_packed = both[:, :segment], both[:, segment:]
    mean_grad = own_grad / n_dp
    mean_moment = own_packed / n_dp
    moment_new = beta_one * mean_moment + (1.0 - beta_one) * mean_grad
    denominator = jnp.sqrt(variance[0]) + epsilon
    master_new = master[0] - step_rate * (mean_moment + moment_new) / denominator
    return (master_new[None], moment_new[None], error.reshape(feedback.shape))


def solution(mesh):
    in_specs = (
        P("mp", "dp", None),
        P("mp", "dp", None),
        P("mp", "dp", None),
        P(),
        P("dp", None, "mp", None),
        P(None, ("dp", "mp"), None),
        P(None, ("dp", "mp"), None),
    )
    out_specs = (P("mp", "dp", None), P("mp", "dp", None), P("dp", None, "mp", None))
    return jax.shard_map(
        per_device, mesh=mesh, in_specs=in_specs, out_specs=out_specs, check_vma=False
    )
```

```python
import functools

import jax
import jax.numpy as jnp
from jax import lax
from jax.experimental import pallas as pl
from jax.experimental.pallas import tpu as pltpu
from jax.sharding import PartitionSpec as P

beta_one = 0.9
step_rate = 0.05
epsilon = 1e-08
down_scale = 28672.0 ** (-0.5)
BF = jnp.bfloat16
F32 = jnp.float32
NT = (((1,), (1,)), ((), ()))
NN = (((1,), (0,)), ((), ()))


def dot(a, b, dims=NN):
    return lax.dot_general(a, b, dims, preferred_element_type=F32)


def swap(x, axis, mask):
    n = lax.axis_size(axis)
    return lax.ppermute(x, axis, [(i, i ^ mask) for i in range(n)])


def after(x, *others):
    return lax.optimization_barrier((x, *others))[0]


def bits_of(n, lowest=1):
    masks = []
    mask = n // 2
    while mask >= lowest:
        masks.append(mask)
        mask //= 2
    return masks


def gradient_rows(weights, x_ref, g_ref, hidden_rows, up_scale):
    before = up_scale * dot(weights, x_ref[...], NT)[:hidden_rows]
    back = down_scale * dot(weights, g_ref[...], NT)[hidden_rows:]
    sigmoid = jax.nn.sigmoid(before)
    hidden = before * sigmoid
    slope = back * (sigmoid * (1.0 + before * (1.0 - sigmoid)))
    zeros = jnp.zeros_like(slope)
    left_up = jnp.concatenate([slope, zeros], axis=0).astype(BF)
    left_down = jnp.concatenate([zeros, hidden], axis=0).astype(BF)

    def columns(at):
        return up_scale * dot(left_up, x_ref[:, at]) + down_scale * dot(left_down, g_ref[:, at])

    return columns


def first_kernel(hidden_rows, up_scale, chunk, place_ref, w0_ref, w1_ref, x_ref, g_ref, weights_ref, part_ref, sent_ref):
    rows = 2 * hidden_rows
    half, segment = w0_ref.shape
    width = x_ref.shape[1]
    ordered = dot(place_ref[:, :half], w0_ref[...]) + dot(place_ref[:, half:], w1_ref[...])
    for c in range(width // segment):
        weights_ref[:, c * segment : (c + 1) * segment] = ordered[c * rows : (c + 1) * rows].astype(BF)
    columns = gradient_rows(weights_ref[...], x_ref, g_ref, hidden_rows, up_scale)
    for c in range(width // chunk):
        at = slice(c * chunk, (c + 1) * chunk)
        part = columns(at)
        part_ref[:, at] = part
        sent_ref[:, at] = part.astype(BF)


def store_flat(back_ref, seg_ref, kept_ref, away_ref, lanes):
    flat = dot(back_ref[...], seg_ref[...]).astype(BF)
    half = kept_ref.shape[0]
    kept_ref[:, lanes] = flat[:half]
    away_ref[:, lanes] = flat[half:]


def second_kernel(
    hidden_rows, up_scale, own, place_ref, back_ref, part_ref, got_ref, weights_ref, x_ref, g_ref, near_ref, *rest
):
    if own:
        *far_refs, feedback_ref, kept_ref, away_ref, error_ref, local_ref, seg_ref, shifted_ref = rest
    else:
        *far_refs, kept_ref, away_ref, local_ref, seg_ref = rest
    rows = 2 * hidden_rows
    half = near_ref.shape[0]
    segment = seg_ref.shape[1]
    width = x_ref.shape[1]
    near = dot(place_ref[:, :half], near_ref[...])
    terms = [
        near[:, i * segment : (i + 1) * segment] + dot(place_ref[:, half:], ref[...]) for i, ref in enumerate(far_refs)
    ]
    moment = sum(terms[2:], terms[0])
    rate = step_rate / (jnp.sqrt(terms[1]) + epsilon)
    for c in range(width // segment):
        at, run = slice(c * segment, (c + 1) * segment), slice(c * rows, (c + 1) * rows)
        step_one = part_ref[:, at] + got_ref[:, at].astype(F32)
        local_moment = beta_one * moment[run] + (1.0 - beta_one) * step_one
        local_ref[:, at] = (weights_ref[:, at].astype(F32) - local_moment * rate[run]).astype(BF)
        if own:
            shifted_ref[:, at] = local_moment + feedback_ref[:, at].astype(F32)
    columns = gradient_rows(local_ref[...], x_ref, g_ref, hidden_rows, up_scale)
    for c in range(width // segment):
        seg_ref[c * rows : (c + 1) * rows] = columns(slice(c * segment, (c + 1) * segment)).astype(BF)
    store_flat(back_ref, seg_ref, kept_ref, away_ref, slice(0, segment))
    if own:
        shifted = shifted_ref[...]
        magnitude = jnp.sum(jnp.abs(shifted), axis=1, keepdims=True) * (1.0 / width) + 1e-06
        packed = magnitude * jnp.tanh(shifted / magnitude)
        error_ref[...] = (shifted - packed).astype(BF)
        for c in range(width // segment):
            seg_ref[c * rows : (c + 1) * rows] = packed[:, c * segment : (c + 1) * segment].astype(BF)
        store_flat(back_ref, seg_ref, kept_ref, away_ref, slice(segment, 2 * segment))


def tokens_of(step, arrays, *others):
    return [x[step] for x in lax.optimization_barrier((*arrays, *others))[: len(arrays)]]


def call(kernel, out_shape, operands, scratch=()):
    return pl.pallas_call(
        kernel,
        out_shape=out_shape,
        in_specs=[pl.BlockSpec(memory_space=pltpu.VMEM)] * len(operands),
        out_specs=jax.tree.map(lambda _: pl.BlockSpec(memory_space=pltpu.VMEM), out_shape),
        scratch_shapes=list(scratch),
        cost_estimate=pl.CostEstimate(flops=1, bytes_accessed=1, transcendentals=0),
        compiler_params=pltpu.CompilerParams(vmem_limit_bytes=16 * 1024 * 1024),
    )(*operands)


def per_device(master, moment, variance, flat_slot, feedback, activations, output_grads):
    n_dp, n_mp = lax.axis_size("dp"), lax.axis_size("mp")
    me = lax.axis_index("dp")
    span, segment = master.shape[1:]
    segments = flat_slot.shape[0]
    hidden_rows, width = feedback.shape[2:]
    rows = 2 * hidden_rows
    up_scale = width ** (-0.5)
    far = bits_of(n_dp, 2)
    mp_bits = bits_of(n_mp)
    shape = jax.ShapeDtypeStruct

    near_w = master[0].astype(BF)
    spans = jnp.pad(after(moment[0], near_w), ((0, 0), (0, segment))) + jnp.pad(variance[0], ((0, 0), (segment, 0)))
    near_a = spans.astype(BF)
    steps = []
    for mask in far:
        near_w = jnp.concatenate([near_w, swap(near_w, "dp", mask)], axis=0)
        steps.append(near_w)
    blocks_a = [near_a]
    for mask in reversed(mp_bits):
        blocks_a = blocks_a + [swap(b, "mp", mask) for b in blocks_a]
    exact = after(moment[0], steps[0])
    low = (exact - lax.reduce_precision(exact, 8, 7)).astype(BF)
    all_a = after(jnp.concatenate([near_a, low] + blocks_a[1:], axis=1), steps[0])

    slot = after(flat_slot, steps[-1])
    owner = (slot // span) ^ me
    position = jnp.zeros_like(owner)
    for place, mask in enumerate(far + [1]):
        position = position + jnp.where((owner & mask) != 0, 1 << place, 0)
    position = position * span + slot % span
    position = position.reshape(rows, width // segment).T.reshape(segments)
    line = jnp.arange(segments, dtype=jnp.int32)
    place_map = (position[:, None] == line[None, :]).astype(BF)
    back_map = (line[:, None] == position[None, :]).astype(BF)

    blocks_w = [near_w]
    for mask in reversed(mp_bits):
        blocks_w = blocks_w + [swap(b, "mp", mask) for b in blocks_w]
    pairs_w = [(b, swap(b, "dp", 1)) for b in blocks_w]

    tensor = (rows, width)
    one = tokens_of(0, (activations, output_grads), steps[-2])
    half = segments // 2
    weights, parts, sent = [], [], []
    for w0, w1 in pairs_w:
        kernel = functools.partial(first_kernel, hidden_rows, up_scale, min(width, 1024))
        out = (shape(tensor, BF), shape(tensor, F32), shape(tensor, BF))
        w_t, part, part_sent = call(kernel, out, (place_map, w0, w1, *one))
        weights.append(w_t)
        parts.append(part)
        sent.append(part_sent)
    two = tokens_of(1, (activations, output_grads), sent[-1])

    for step, mask in enumerate(mp_bits):
        if step > 0:
            parts = [p + q.astype(F32) for p, q in zip(parts, got)]
            sent = [p.astype(BF) for p in parts]
        crossed = [swap(p, "mp", mask) for p in sent]
        got = [crossed[k ^ mask] for k in range(n_mp)]

    for mask in far[:-2]:
        all_a = jnp.concatenate([all_a, after(swap(all_a, "dp", mask), steps[-1])], axis=0)
    ends = [0] + [(3 + 2 * k) * segment for k in range(n_mp)]
    blocks_a = [all_a[:, ends[k] : ends[k + 1]] for k in range(n_mp)]
    blocks_a[0] = after(blocks_a[0], sent[0])
    arrived = [after(swap(b, "dp", far[-2]), sent[0] if k else sent[-1]) for k, b in enumerate(blocks_a)]
    blocks_a = [jnp.concatenate(pair, axis=0) for pair in zip(blocks_a, arrived)]
    arrived = [swap(b, "dp", far[-1]) for b in blocks_a]

    half = segments // 2
    sums, event = [None] * n_mp, sent[-1]
    for k in reversed(range(n_mp)):
        own = k == 0
        block = jnp.concatenate([blocks_a[k], after(arrived[k], event)], axis=0)
        far_terms = [swap(block[:, at : at + segment], "dp", 1) for at in range(0, block.shape[1], segment)]
        operands = [place_map, back_map, parts[k], got[k], weights[k], *two, block, *far_terms]
        out = [shape((half, (2 if own else 1) * segment), BF)] * 2
        scratch = [pltpu.VMEM(tensor, BF), pltpu.VMEM((segments, segment), BF)]
        if own:
            operands.append(feedback[0].reshape(tensor))
            out.append(shape(tensor, BF))
            scratch.append(pltpu.VMEM(tensor, F32))
        result = call(
            functools.partial(second_kernel, hidden_rows, up_scale, own),
            tuple(out),
            operands,
            scratch,
        )
        event = result[0]
        sums[k] = result[0].astype(F32) + swap(result[1], "dp", 1).astype(F32)
    error = result[2]

    for mask in far[::-1]:
        count = sums[0].shape[0] // 2
        sums = [p[:count] + swap(p[count:].astype(BF), "dp", mask).astype(F32) for p in sums]
    own_grad, own_packed = sums[0][:, :segment], sums[0][:, segment:]
    grads = [own_grad] + sums[1:]
    for mask in mp_bits:
        crossed = [swap(p.astype(BF), "mp", mask).astype(F32) for p in grads[mask:]]
        grads = [p + q for p, q in zip(grads, crossed)]
    own_grad = grads[0]
    mean_grad = own_grad / n_dp
    mean_moment = own_packed / n_dp
    moment_new = beta_one * mean_moment + (1.0 - beta_one) * mean_grad
    denominator = jnp.sqrt(variance[0]) + epsilon
    master_new = master[0] - step_rate * (mean_moment + moment_new) / denominator
    return (master_new[None], moment_new[None], error.reshape(feedback.shape))


def solution(mesh):
    in_specs = (
        P("mp", "dp", None),
        P("mp", "dp", None),
        P("mp", "dp", None),
        P(),
        P("dp", None, "mp", None),
        P(None, ("dp", "mp"), None),
        P(None, ("dp", "mp"), None),
    )
    out_specs = (P("mp", "dp", None), P("mp", "dp", None), P("dp", None, "mp", None))
    return jax.shard_map(
        per_device, mesh=mesh, in_specs=in_specs, out_specs=out_specs, check_vma=False
    )
```

```python
import functools

import jax
import jax.numpy as jnp
from jax import lax
from jax.experimental import pallas as pl
from jax.experimental.pallas import tpu as pltpu
from jax.sharding import PartitionSpec as P

beta_one = 0.9
step_rate = 0.05
epsilon = 1e-08
down_scale = 28672.0 ** (-0.5)
BF = jnp.bfloat16
F32 = jnp.float32
NT = (((1,), (1,)), ((), ()))
NN = (((1,), (0,)), ((), ()))


def dot(a, b, dims=NN):
    return lax.dot_general(a, b, dims, preferred_element_type=F32)


def swap(x, axis, mask):
    n = lax.axis_size(axis)
    return lax.ppermute(x, axis, [(i, i ^ mask) for i in range(n)])


def after(x, *others):
    return lax.optimization_barrier((x, *others))[0]


def halve(total, mask):
    count = total.shape[0] // 2
    return total[:count] + swap(total[count:].astype(BF), "dp", mask).astype(F32)


def bits_of(n, lowest=1):
    masks = []
    mask = n // 2
    while mask >= lowest:
        masks.append(mask)
        mask //= 2
    return masks


def gradient_rows(weights, x_ref, g_ref, hidden_rows, up_scale):
    before = up_scale * dot(weights, x_ref[...], NT)[:hidden_rows]
    back = down_scale * dot(weights, g_ref[...], NT)[hidden_rows:]
    sigmoid = jax.nn.sigmoid(before)
    hidden = before * sigmoid
    slope = back * (sigmoid * (1.0 + before * (1.0 - sigmoid)))
    zeros = jnp.zeros_like(slope)
    left_up = jnp.concatenate([slope, zeros], axis=0).astype(BF)
    left_down = jnp.concatenate([zeros, hidden], axis=0).astype(BF)

    def columns(at):
        return up_scale * dot(left_up, x_ref[:, at]) + down_scale * dot(left_down, g_ref[:, at])

    return columns


def first_kernel(hidden_rows, up_scale, chunk, place_ref, w0_ref, w1_ref, x_ref, g_ref, weights_ref, part_ref, sent_ref):
    rows = 2 * hidden_rows
    half, segment = w0_ref.shape
    width = x_ref.shape[1]
    ordered = dot(place_ref[:, :half], w0_ref[...]) + dot(place_ref[:, half:], w1_ref[...])
    for c in range(width // segment):
        weights_ref[:, c * segment : (c + 1) * segment] = ordered[c * rows : (c + 1) * rows].astype(BF)
    columns = gradient_rows(weights_ref[...], x_ref, g_ref, hidden_rows, up_scale)
    for c in range(width // chunk):
        at = slice(c * chunk, (c + 1) * chunk)
        part = columns(at)
        part_ref[:, at] = part
        sent_ref[:, at] = part.astype(BF)


def store_flat(back_ref, seg_ref, kept_ref, away_ref, lanes):
    flat = dot(back_ref[...], seg_ref[...]).astype(BF)
    half = kept_ref.shape[0]
    kept_ref[:, lanes] = flat[:half]
    away_ref[:, lanes] = flat[half:]


def second_kernel(
    hidden_rows, up_scale, own, place_ref, back_ref, part_ref, got_ref, weights_ref, x_ref, g_ref, near_ref, *rest
):
    if own:
        *far_refs, feedback_ref, kept_ref, away_ref, error_ref, local_ref, seg_ref, shifted_ref = rest
    else:
        *far_refs, kept_ref, away_ref, local_ref, seg_ref = rest
    rows = 2 * hidden_rows
    half = near_ref.shape[0]
    segment = seg_ref.shape[1]
    width = x_ref.shape[1]
    near = dot(place_ref[:, :half], near_ref[...])
    terms = [
        near[:, i * segment : (i + 1) * segment] + dot(place_ref[:, half:], ref[...]) for i, ref in enumerate(far_refs)
    ]
    moment = sum(terms[2:], terms[0])
    rate = step_rate / (jnp.sqrt(terms[1]) + epsilon)
    for c in range(width // segment):
        at, run = slice(c * segment, (c + 1) * segment), slice(c * rows, (c + 1) * rows)
        step_one = part_ref[:, at] + got_ref[:, at].astype(F32)
        local_moment = beta_one * moment[run] + (1.0 - beta_one) * step_one
        local_ref[:, at] = (weights_ref[:, at].astype(F32) - local_moment * rate[run]).astype(BF)
        if own:
            shifted_ref[:, at] = local_moment + feedback_ref[:, at].astype(F32)
    columns = gradient_rows(local_ref[...], x_ref, g_ref, hidden_rows, up_scale)
    for c in range(width // segment):
        seg_ref[c * rows : (c + 1) * rows] = columns(slice(c * segment, (c + 1) * segment)).astype(BF)
    store_flat(back_ref, seg_ref, kept_ref, away_ref, slice(0, segment))
    if own:
        shifted = shifted_ref[...]
        magnitude = jnp.sum(jnp.abs(shifted), axis=1, keepdims=True) * (1.0 / width) + 1e-06
        packed = magnitude * jnp.tanh(shifted / magnitude)
        error_ref[...] = (shifted - packed).astype(BF)
        for c in range(width // segment):
            seg_ref[c * rows : (c + 1) * rows] = packed[:, c * segment : (c + 1) * segment].astype(BF)
        store_flat(back_ref, seg_ref, kept_ref, away_ref, slice(segment, 2 * segment))


def tokens_of(step, arrays, *others):
    return [x[step] for x in lax.optimization_barrier((*arrays, *others))[: len(arrays)]]


def call(kernel, out_shape, operands, scratch=()):
    return pl.pallas_call(
        kernel,
        out_shape=out_shape,
        in_specs=[pl.BlockSpec(memory_space=pltpu.VMEM)] * len(operands),
        out_specs=jax.tree.map(lambda _: pl.BlockSpec(memory_space=pltpu.VMEM), out_shape),
        scratch_shapes=list(scratch),
        cost_estimate=pl.CostEstimate(flops=1, bytes_accessed=1, transcendentals=0),
        compiler_params=pltpu.CompilerParams(vmem_limit_bytes=16 * 1024 * 1024),
    )(*operands)


def per_device(master, moment, variance, flat_slot, feedback, activations, output_grads):
    n_dp, n_mp = lax.axis_size("dp"), lax.axis_size("mp")
    me = lax.axis_index("dp")
    span, segment = master.shape[1:]
    segments = flat_slot.shape[0]
    hidden_rows, width = feedback.shape[2:]
    rows = 2 * hidden_rows
    up_scale = width ** (-0.5)
    far = bits_of(n_dp, 2)
    mp_bits = bits_of(n_mp)
    shape = jax.ShapeDtypeStruct

    near_w = master[0].astype(BF)
    spans = jnp.concatenate([after(moment[0], near_w), variance[0]], axis=1)
    near_a = spans.astype(BF)
    low = (spans[:, :segment] - lax.reduce_precision(spans[:, :segment], 8, 7)).astype(BF)
    steps = []
    for mask in far:
        near_w = jnp.concatenate([near_w, swap(near_w, "dp", mask)], axis=0)
        steps.append(near_w)
    blocks_a = [near_a]
    for mask in reversed(mp_bits):
        blocks_a = blocks_a + [swap(b, "mp", mask) for b in blocks_a]
    all_a = after(jnp.concatenate([near_a, low] + blocks_a[1:], axis=1), steps[0])

    slot = after(flat_slot, steps[-1])
    owner = (slot // span) ^ me
    position = jnp.zeros_like(owner)
    for place, mask in enumerate(far + [1]):
        position = position + jnp.where((owner & mask) != 0, 1 << place, 0)
    position = position * span + slot % span
    position = position.reshape(rows, width // segment).T.reshape(segments)
    line = jnp.arange(segments, dtype=jnp.int32)
    place_map = (position[:, None] == line[None, :]).astype(BF)
    back_map = (line[:, None] == position[None, :]).astype(BF)

    blocks_w = [near_w]
    for mask in reversed(mp_bits):
        blocks_w = blocks_w + [swap(b, "mp", mask) for b in blocks_w]
    pairs_w = [(b, swap(b, "dp", 1)) for b in blocks_w]

    tensor = (rows, width)
    one = tokens_of(0, (activations, output_grads), steps[-2])
    half = segments // 2
    weights, parts, sent = [], [], []
    for w0, w1 in pairs_w:
        kernel = functools.partial(first_kernel, hidden_rows, up_scale, min(width, 1024))
        out = (shape(tensor, BF), shape(tensor, F32), shape(tensor, BF))
        w_t, part, part_sent = call(kernel, out, (place_map, w0, w1, *one))
        weights.append(w_t)
        parts.append(part)
        sent.append(part_sent)
    two = tokens_of(1, (activations, output_grads), sent[-1])

    for step, mask in enumerate(mp_bits):
        if step > 0:
            parts = [p + q.astype(F32) for p, q in zip(parts, got)]
            sent = [p.astype(BF) for p in parts]
        crossed = [swap(p, "mp", mask) for p in sent]
        got = [crossed[k ^ mask] for k in range(n_mp)]

    for mask in far[:-2]:
        all_a = jnp.concatenate([all_a, after(swap(all_a, "dp", mask), steps[-1])], axis=0)
    ends = [0] + [(3 + 2 * k) * segment for k in range(n_mp)]
    blocks_a = [all_a[:, ends[k] : ends[k + 1]] for k in range(n_mp)]
    blocks_a[0] = after(blocks_a[0], sent[0])
    arrived = [after(swap(b, "dp", far[-2]), sent[0] if k else sent[-1]) for k, b in enumerate(blocks_a)]
    blocks_a = [jnp.concatenate(pair, axis=0) for pair in zip(blocks_a, arrived)]
    arrived = [swap(blocks_a[0], "dp", far[-1])]
    for block in blocks_a[1:]:
        terms = [swap(block[:, at : at + segment], "dp", far[-1]) for at in (0, segment)]
        arrived.append(jnp.concatenate(lax.optimization_barrier((*terms, sent[-1], blocks_a[0]))[:2], axis=1))

    half = segments // 2
    sums, event = [None] * n_mp, sent[-1]
    for k in reversed(range(n_mp)):
        own = k == 0
        block = jnp.concatenate([blocks_a[k], after(arrived[k], event)], axis=0)
        far_terms = [swap(block[:, at : at + segment], "dp", 1) for at in range(0, block.shape[1], segment)]
        operands = [place_map, back_map, parts[k], got[k], weights[k], *two, block, *far_terms]
        out = [shape((half, (2 if own else 1) * segment), BF)] * 2
        scratch = [pltpu.VMEM(tensor, BF), pltpu.VMEM((segments, segment), BF)]
        if own:
            operands.append(feedback[0].reshape(tensor))
            out.append(shape(tensor, BF))
            scratch.append(pltpu.VMEM(tensor, F32))
        result = call(
            functools.partial(second_kernel, hidden_rows, up_scale, own),
            tuple(out),
            operands,
            scratch,
        )
        event = result[0]
        sums[k] = result[0].astype(F32) + swap(result[1], "dp", 1).astype(F32)
    error = result[2]

    for mask in far[:0:-1]:
        sums = [halve(p, mask) for p in sums]
    grads = [sums[0][:, :segment]] + sums[1:]
    for mask in mp_bits:
        crossed = [swap(p.astype(BF), "mp", mask).astype(F32) for p in grads[mask:]]
        grads = [p + q for p, q in zip(grads, crossed)]
    both = halve(jnp.concatenate([grads[0], sums[0][:, segment:]], axis=1), far[0])
    own_grad, own_packed = both[:, :segment], both[:, segment:]
    mean_grad = own_grad / n_dp
    mean_moment = own_packed / n_dp
    moment_new = beta_one * mean_moment + (1.0 - beta_one) * mean_grad
    denominator = jnp.sqrt(variance[0]) + epsilon
    master_new = master[0] - step_rate * (mean_moment + moment_new) / denominator
    return (master_new[None], moment_new[None], error.reshape(feedback.shape))


def solution(mesh):
    in_specs = (
        P("mp", "dp", None),
        P("mp", "dp", None),
        P("mp", "dp", None),
        P(),
        P("dp", None, "mp", None),
        P(None, ("dp", "mp"), None),
        P(None, ("dp", "mp"), None),
    )
    out_specs = (P("mp", "dp", None), P("mp", "dp", None), P("dp", None, "mp", None))
    return jax.shard_map(
        per_device, mesh=mesh, in_specs=in_specs, out_specs=out_specs, check_vma=False
    )
```

```python
import functools

import jax
import jax.numpy as jnp
from jax import lax
from jax.experimental import pallas as pl
from jax.experimental.pallas import tpu as pltpu
from jax.sharding import PartitionSpec as P

beta_one = 0.9
step_rate = 0.05
epsilon = 1e-08
down_scale = 28672.0 ** (-0.5)
BF = jnp.bfloat16
F32 = jnp.float32
NT = (((1,), (1,)), ((), ()))
NN = (((1,), (0,)), ((), ()))


def dot(a, b, dims=NN):
    return lax.dot_general(a, b, dims, preferred_element_type=F32)


def swap(x, axis, mask):
    n = lax.axis_size(axis)
    return lax.ppermute(x, axis, [(i, i ^ mask) for i in range(n)])


def after(x, *others):
    return lax.optimization_barrier((x, *others))[0]


def halve(total, mask):
    count = total.shape[0] // 2
    return total[:count] + swap(total[count:].astype(BF), "dp", mask).astype(F32)


def bits_of(n, lowest=1):
    masks = []
    mask = n // 2
    while mask >= lowest:
        masks.append(mask)
        mask //= 2
    return masks


def gradient_rows(weights, x_ref, g_ref, hidden_rows, up_scale):
    before = up_scale * dot(weights, x_ref[...], NT)[:hidden_rows]
    back = down_scale * dot(weights, g_ref[...], NT)[hidden_rows:]
    sigmoid = jax.nn.sigmoid(before)
    hidden = before * sigmoid
    slope = back * (sigmoid * (1.0 + before * (1.0 - sigmoid)))
    zeros = jnp.zeros_like(slope)
    left_up = jnp.concatenate([slope, zeros], axis=0).astype(BF)
    left_down = jnp.concatenate([zeros, hidden], axis=0).astype(BF)

    def columns(at):
        return up_scale * dot(left_up, x_ref[:, at]) + down_scale * dot(left_down, g_ref[:, at])

    return columns


def first_kernel(hidden_rows, up_scale, chunk, place_ref, w0_ref, w1_ref, x_ref, g_ref, weights_ref, part_ref, sent_ref):
    rows = 2 * hidden_rows
    half, segment = w0_ref.shape
    width = x_ref.shape[1]
    ordered = dot(place_ref[:, :half], w0_ref[...]) + dot(place_ref[:, half:], w1_ref[...])
    for c in range(width // segment):
        weights_ref[:, c * segment : (c + 1) * segment] = ordered[c * rows : (c + 1) * rows].astype(BF)
    columns = gradient_rows(weights_ref[...], x_ref, g_ref, hidden_rows, up_scale)
    for c in range(width // chunk):
        at = slice(c * chunk, (c + 1) * chunk)
        part = columns(at)
        part_ref[:, at] = part
        sent_ref[:, at] = part.astype(BF)


def store_flat(back_ref, seg_ref, kept_ref, away_ref, lanes):
    flat = dot(back_ref[...], seg_ref[...]).astype(BF)
    half = kept_ref.shape[0]
    kept_ref[:, lanes] = flat[:half]
    away_ref[:, lanes] = flat[half:]


def second_kernel(
    hidden_rows, up_scale, own, place_ref, back_ref, part_ref, got_ref, weights_ref, x_ref, g_ref, near_ref, *rest
):
    if own:
        *far_refs, feedback_ref, kept_ref, away_ref, error_ref, local_ref, seg_ref, shifted_ref = rest
    else:
        *far_refs, kept_ref, away_ref, local_ref, seg_ref = rest
    rows = 2 * hidden_rows
    half = near_ref.shape[0]
    segment = seg_ref.shape[1]
    width = x_ref.shape[1]
    near = dot(place_ref[:, :half], near_ref[...])
    terms = [
        near[:, i * segment : (i + 1) * segment] + dot(place_ref[:, half:], ref[...]) for i, ref in enumerate(far_refs)
    ]
    moment = sum(terms[2:], terms[0])
    rate = step_rate / (jnp.sqrt(terms[1]) + epsilon)
    for c in range(width // segment):
        at, run = slice(c * segment, (c + 1) * segment), slice(c * rows, (c + 1) * rows)
        step_one = part_ref[:, at] + got_ref[:, at].astype(F32)
        local_moment = beta_one * moment[run] + (1.0 - beta_one) * step_one
        local_ref[:, at] = (weights_ref[:, at].astype(F32) - local_moment * rate[run]).astype(BF)
        if own:
            shifted_ref[:, at] = local_moment + feedback_ref[:, at].astype(F32)
    columns = gradient_rows(local_ref[...], x_ref, g_ref, hidden_rows, up_scale)
    for c in range(width // segment):
        seg_ref[c * rows : (c + 1) * rows] = columns(slice(c * segment, (c + 1) * segment)).astype(BF)
    store_flat(back_ref, seg_ref, kept_ref, away_ref, slice(0, segment))
    if own:
        shifted = shifted_ref[...]
        magnitude = jnp.sum(jnp.abs(shifted), axis=1, keepdims=True) * (1.0 / width) + 1e-06
        packed = magnitude * jnp.tanh(shifted / magnitude)
        error_ref[...] = (shifted - packed).astype(BF)
        for c in range(width // segment):
            seg_ref[c * rows : (c + 1) * rows] = packed[:, c * segment : (c + 1) * segment].astype(BF)
        store_flat(back_ref, seg_ref, kept_ref, away_ref, slice(segment, 2 * segment))


def tokens_of(step, arrays, *others):
    return [x[step] for x in lax.optimization_barrier((*arrays, *others))[: len(arrays)]]


def call(kernel, out_shape, operands, scratch=()):
    return pl.pallas_call(
        kernel,
        out_shape=out_shape,
        in_specs=[pl.BlockSpec(memory_space=pltpu.VMEM)] * len(operands),
        out_specs=jax.tree.map(lambda _: pl.BlockSpec(memory_space=pltpu.VMEM), out_shape),
        scratch_shapes=list(scratch),
        cost_estimate=pl.CostEstimate(flops=1, bytes_accessed=1, transcendentals=0),
        compiler_params=pltpu.CompilerParams(vmem_limit_bytes=16 * 1024 * 1024),
    )(*operands)


def per_device(master, moment, variance, flat_slot, feedback, activations, output_grads):
    n_dp, n_mp = lax.axis_size("dp"), lax.axis_size("mp")
    me = lax.axis_index("dp")
    span, segment = master.shape[1:]
    segments = flat_slot.shape[0]
    hidden_rows, width = feedback.shape[2:]
    rows = 2 * hidden_rows
    up_scale = width ** (-0.5)
    far = bits_of(n_dp, 2)
    mp_bits = bits_of(n_mp)
    shape = jax.ShapeDtypeStruct

    near_w = master[0].astype(BF)
    spans = jnp.pad(after(moment[0], near_w), ((0, 0), (0, segment))) + jnp.pad(variance[0], ((0, 0), (segment, 0)))
    near_a = spans.astype(BF)
    steps = []
    for mask in far:
        near_w = jnp.concatenate([near_w, swap(near_w, "dp", mask)], axis=0)
        steps.append(near_w)
    blocks_a = [near_a]
    for mask in reversed(mp_bits):
        blocks_a = blocks_a + [swap(b, "mp", mask) for b in blocks_a]
    exact = after(moment[0], steps[0])
    low = (exact - lax.reduce_precision(exact, 8, 7)).astype(BF)
    all_a = after(jnp.concatenate([near_a, low] + blocks_a[1:], axis=1), steps[0])

    slot = after(flat_slot, steps[-1])
    owner = (slot // span) ^ me
    position = jnp.zeros_like(owner)
    for place, mask in enumerate(far + [1]):
        position = position + jnp.where((owner & mask) != 0, 1 << place, 0)
    position = position * span + slot % span
    position = position.reshape(rows, width // segment).T.reshape(segments)
    line = jnp.arange(segments, dtype=jnp.int32)
    place_map = (position[:, None] == line[None, :]).astype(BF)
    back_map = (line[:, None] == position[None, :]).astype(BF)

    blocks_w = [near_w]
    for mask in reversed(mp_bits):
        blocks_w = blocks_w + [swap(b, "mp", mask) for b in blocks_w]
    pairs_w = [(b, swap(b, "dp", 1)) for b in blocks_w]

    tensor = (rows, width)
    one = tokens_of(0, (activations, output_grads), steps[-2])
    half = segments // 2
    weights, parts, sent = [], [], []
    for w0, w1 in pairs_w:
        kernel = functools.partial(first_kernel, hidden_rows, up_scale, min(width, 1024))
        out = (shape(tensor, BF), shape(tensor, F32), shape(tensor, BF))
        w_t, part, part_sent = call(kernel, out, (place_map, w0, w1, *one))
        weights.append(w_t)
        parts.append(part)
        sent.append(part_sent)
    two = tokens_of(1, (activations, output_grads), sent[-1])

    for step, mask in enumerate(mp_bits):
        if step > 0:
            parts = [p + q.astype(F32) for p, q in zip(parts, got)]
            sent = [p.astype(BF) for p in parts]
        crossed = [swap(p, "mp", mask) for p in sent]
        got = [crossed[k ^ mask] for k in range(n_mp)]

    for mask in far[:-2]:
        all_a = jnp.concatenate([all_a, after(swap(all_a, "dp", mask), steps[-1])], axis=0)
    ends = [0] + [(3 + 2 * k) * segment for k in range(n_mp)]
    blocks_a = [all_a[:, ends[k] : ends[k + 1]] for k in range(n_mp)]
    blocks_a[0] = after(blocks_a[0], sent[0])
    arrived = [after(swap(b, "dp", far[-2]), sent[0] if k else sent[-1]) for k, b in enumerate(blocks_a)]
    blocks_a = [jnp.concatenate(pair, axis=0) for pair in zip(blocks_a, arrived)]
    arrived = [swap(blocks_a[0], "dp", far[-1])]
    for block in blocks_a[1:]:
        terms = [swap(block[:, at : at + segment], "dp", far[-1]) for at in (0, segment)]
        arrived.append(jnp.concatenate(lax.optimization_barrier((*terms, sent[-1], blocks_a[0]))[:2], axis=1))

    half = segments // 2
    sums, event = [None] * n_mp, sent[-1]
    for k in reversed(range(n_mp)):
        own = k == 0
        block = jnp.concatenate([blocks_a[k], after(arrived[k], event)], axis=0)
        far_terms = [swap(block[:, at : at + segment], "dp", 1) for at in range(0, block.shape[1], segment)]
        operands = [place_map, back_map, parts[k], got[k], weights[k], *two, block, *far_terms]
        out = [shape((half, (2 if own else 1) * segment), BF)] * 2
        scratch = [pltpu.VMEM(tensor, BF), pltpu.VMEM((segments, segment), BF)]
        if own:
            operands.append(feedback[0].reshape(tensor))
            out.append(shape(tensor, BF))
            scratch.append(pltpu.VMEM(tensor, F32))
        result = call(
            functools.partial(second_kernel, hidden_rows, up_scale, own),
            tuple(out),
            operands,
            scratch,
        )
        event = result[0]
        sums[k] = result[0].astype(F32) + swap(result[1], "dp", 1).astype(F32)
    error = result[2]

    for mask in far[:0:-1]:
        sums = [halve(p, mask) for p in sums]
    grads = [sums[0][:, :segment]] + sums[1:]
    for mask in mp_bits:
        crossed = [swap(p.astype(BF), "mp", mask).astype(F32) for p in grads[mask:]]
        grads = [p + q for p, q in zip(grads, crossed)]
    both = halve(jnp.concatenate([grads[0], sums[0][:, segment:]], axis=1), far[0])
    own_grad, own_packed = both[:, :segment], both[:, segment:]
    mean_grad = own_grad / n_dp
    mean_moment = own_packed / n_dp
    moment_new = beta_one * mean_moment + (1.0 - beta_one) * mean_grad
    denominator = jnp.sqrt(variance[0]) + epsilon
    master_new = master[0] - step_rate * (mean_moment + moment_new) / denominator
    return (master_new[None], moment_new[None], error.reshape(feedback.shape))


def solution(mesh):
    in_specs = (
        P("mp", "dp", None),
        P("mp", "dp", None),
        P("mp", "dp", None),
        P(),
        P("dp", None, "mp", None),
        P(None, ("dp", "mp"), None),
        P(None, ("dp", "mp"), None),
    )
    out_specs = (P("mp", "dp", None), P("mp", "dp", None), P("dp", None, "mp", None))
    return jax.shard_map(
        per_device, mesh=mesh, in_specs=in_specs, out_specs=out_specs, check_vma=False
    )
```
